256 devices in a mesh: ctx: 32 (over z, y_lo, core), tp: 8 (over x, y_hi).
Axes of the slice: x: 4, y: 4 (y_hi: 2, y_lo: 2; y = y_hi * 2 + y_lo), z: 8, core: 2. Of those that a mesh axis runs over, the one named last changes fastest.
Arguments:
- tokens: bfloat16 [16384, 5376], P('ctx'), may hold values from -6 to 6
- query_weight: bfloat16 [5376, 2048], P('ctx', 'tp'), may hold values from -0.078125 to 0.078125
- key_matrix: bfloat16 [5376, 1024], P('ctx', 'tp'), may hold values from -0.078125 to 0.078125
- value_matrix: bfloat16 [5376, 1024], P('ctx', 'tp'), may hold values from -0.078125 to 0.078125
- query_gain: float32 [128], replicated, may hold values from 0.5 to 2.5
- key_norm_gain: float32 [128], replicated, may hold values from 0.5 to 2.5
- cotangent: bfloat16 [16384, 2048], P('ctx', 'tp'), may hold values from -24 to 24
Outputs:
- attended: bfloat16 [16384, 2048], P('ctx', 'tp')
- token_gradient: bfloat16 [16384, 5376], P('ctx', 'tp')
- query_gradient: bfloat16 [5376, 2048], P('ctx', 'tp')
- key_weight_gradient: bfloat16 [5376, 1024], P('ctx', 'tp')
- value_weight_gradient: bfloat16 [5376, 1024], P('ctx', 'tp')
The draws below stay inside these ranges and needn't reach their ends.
All inputs are finite; a program needn't handle non-finite values.
Results may differ from the reference program's by a relative error of at most 0.035.
Values may be sent and summed in bfloat16 or wider, within the bound.
No kernel may reach another device: no remote copies, remote signals or barrier semaphores. Data moves between devices by JAX's collectives and lax.ppermute only.
A program may use at most 128 MiB of HBM per device.

```python
import math
import jax
import jax.numpy as jnp
from jax import lax

MODEL_WIDTH = 5376
QUERY_HEADS = 16
KEY_VALUE_HEADS = 8
HEAD_WIDTH = 128
WINDOW_LENGTH = 1024
QUERY_SCALAR = 168
TOK_DEV = 512
TOKEN_COUNT = 16384
N_CTX = 32
N_TP = 8


def spiked(values, own_key, source, target, parts, factor):
    owner, partner = [(jnp.arange(values.shape[axis_at]) // (values.shape[axis_at] // parts)).reshape([-1 if axis == axis_at else 1 for axis in range(values.ndim)]) for axis_at in (source, target)]
    chosen = jax.random.permutation(own_key, parts)[partner]
    strong = (owner == chosen) | (owner == (partner + parts // 2) % parts)
    return jnp.where(strong, factor * values, values)


def levels(stream_key, extent, shards, low, largest):
    factor_of = 1.0
    for position, blocks in shards:
        heights = jax.random.uniform(jax.random.fold_in(jax.random.fold_in(stream_key, 6), position), (blocks,), jnp.float32, low / len(shards), largest / len(shards))
        factor_of = factor_of * jnp.repeat(jnp.exp(heights), extent[position] // blocks).reshape((-1,) + (1,) * (len(extent) - 1 - position))
    return factor_of


def gaussian(own_key, shape, deviation, bound, pieces=(), kind=jnp.bfloat16):
    drawn = jax.random.normal(own_key, shape, jnp.float32) * deviation
    if len(pieces) > 0:
        drawn = levels(own_key, shape, pieces, -0.22, 0.18) * drawn
    return jnp.clip(drawn, min=-bound, max=bound).astype(kind)


def heavy_noise(key, extent, deviation, limit, split, heavy, kind=jnp.bfloat16):
    array = deviation * jax.random.normal(key, extent, jnp.float32)
    if split:
        array = array * levels(key, extent, split, -0.22, 0.18)
    return jnp.clip(spiked(array, jax.random.fold_in(key, 3), *heavy), -limit, limit).astype(kind)


def setup_inputs(seed: int = 0) -> dict:
    streams_of = jax.random.split(jax.random.key(seed), 8)
    return {
        "tokens": heavy_noise(streams_of[0], (TOKEN_COUNT, MODEL_WIDTH), 1.0, 6.0, ((0, 32),), (0, 1, 32, 2.75)),
        "query_weight": gaussian(streams_of[1], (MODEL_WIDTH, QUERY_HEADS * HEAD_WIDTH), MODEL_WIDTH ** -0.5, 0.078125, ((0, 32), (1, 8))),
        "key_matrix": gaussian(streams_of[2], (MODEL_WIDTH, KEY_VALUE_HEADS * HEAD_WIDTH), MODEL_WIDTH ** -0.5, 0.078125, ((0, 32), (1, 8))),
        "value_matrix": gaussian(streams_of[3], (MODEL_WIDTH, KEY_VALUE_HEADS * HEAD_WIDTH), MODEL_WIDTH ** -0.5, 0.078125, ((0, 32), (1, 8))),
        "query_gain": jnp.clip(jnp.exp(jax.random.uniform(streams_of[4], (HEAD_WIDTH,), jnp.float32, math.log(0.5), math.log(2.5))), 0.5, 2.5),
        "key_norm_gain": jnp.clip(jnp.exp(jax.random.uniform(streams_of[5], (HEAD_WIDTH,), jnp.float32, math.log(0.5), math.log(2.5))), 0.5, 2.5),
        "cotangent": gaussian(streams_of[6], (TOKEN_COUNT, QUERY_HEADS * HEAD_WIDTH), 4.0, 24.0, ((0, 32), (1, 8))),
    }


rope_base = 10000.0
norm_eps = 1e-06

def normalize_and_rotate(unnormed_rows, gain_vector, token_positions, head_count, head_size):
    row_total = unnormed_rows.shape[0]
    shaped = unnormed_rows.reshape(row_total, head_count, head_size)
    mean_square = lax.optimization_barrier(jnp.mean(shaped * shaped, axis=-1, keepdims=True))
    normed = shaped * lax.rsqrt(mean_square + norm_eps) * gain_vector
    half_size = head_size // 2
    inverse = jnp.power(jnp.float32(rope_base), -jnp.arange(0, head_size, 2).astype(jnp.float32) / head_size)
    angles = token_positions[:, None] * inverse[None, :]
    cosine = jnp.cos(angles)[:, None, :]
    sine_part = jnp.sin(angles)[:, None, :]
    leading = normed[..., :half_size]
    trailing = normed[..., half_size:]
    turned = jnp.concatenate([leading * cosine - trailing * sine_part, trailing * cosine + leading * sine_part], axis=-1)
    return turned.reshape(row_total, head_count * head_size)

def band_attention(query_rows, key_row_block, value_row_block, output_rows, first_query, first_key, score_scale):
    query_wide = query_rows.astype(jnp.float32)
    key_wide = key_row_block.astype(jnp.float32)
    value_wide = value_row_block.astype(jnp.float32)
    out_wide = output_rows.astype(jnp.float32)
    scores = jnp.einsum('tkgd,ckd->kgtc', query_wide, key_wide) * score_scale
    query_place = first_query + jnp.arange(query_rows.shape[0])
    key_place = first_key + jnp.arange(key_row_block.shape[0])
    visible = (key_place[None, :] >= 0) & (key_place[None, :] <= query_place[:, None]) & (key_place[None, :] > query_place[:, None] - WINDOW_LENGTH)
    exponent_terms = jnp.where(visible, jnp.exp(scores), 0.0)
    totals = lax.optimization_barrier(jnp.sum(exponent_terms, axis=-1, keepdims=True))
    probs = exponent_terms / totals
    weights = probs.astype(jnp.bfloat16)
    weight_wide = lax.optimization_barrier(weights).astype(jnp.float32)
    mixed = jnp.einsum('kgtc,ckd->tkgd', weight_wide, value_wide)
    attended = mixed.astype(jnp.bfloat16)
    delta = lax.optimization_barrier(jnp.sum(out_wide * lax.optimization_barrier(attended).astype(jnp.float32), axis=-1))
    delta = jnp.transpose(delta, (1, 2, 0))[..., None]
    prob_grads = jnp.einsum('tkgd,ckd->kgtc', out_wide, value_wide)
    score_grads = (probs * (prob_grads - delta)).astype(jnp.bfloat16)
    score_wide = lax.optimization_barrier(score_grads).astype(jnp.float32)
    query_grads = jnp.einsum('kgtc,ckd->tkgd', score_wide, key_wide) * score_scale
    key_grads = jnp.einsum('kgtc,tkgd->ckd', score_wide, query_wide) * score_scale
    value_grads = jnp.einsum('kgtc,tkgd->ckd', weight_wide, out_wide)
    return (attended, query_grads, key_grads, value_grads)

def reference(tokens, query_weight, key_matrix, value_matrix, query_gain, key_norm_gain, cotangent):
    group_width = QUERY_HEADS // KEY_VALUE_HEADS
    score_scale = QUERY_SCALAR ** (-0.5)
    token_positions = jnp.arange(TOKEN_COUNT).astype(jnp.float32)
    query_raw = jnp.dot(tokens, query_weight, preferred_element_type=jnp.float32)
    key_raw = jnp.dot(tokens, key_matrix, preferred_element_type=jnp.float32)
    value_unprojected = jnp.dot(tokens, value_matrix, preferred_element_type=jnp.float32)

    def rotate_queries(unnormed_rows):
        return normalize_and_rotate(unnormed_rows, query_gain, token_positions, QUERY_HEADS, HEAD_WIDTH)

    def rotate_keys(unnormed_rows):
        return normalize_and_rotate(unnormed_rows, key_norm_gain, token_positions, KEY_VALUE_HEADS, HEAD_WIDTH)
    query_after_rotation, query_pull = jax.vjp(rotate_queries, query_raw)
    key_after_rotation, key_pullback = jax.vjp(rotate_keys, key_raw)
    query_rows = query_after_rotation.astype(jnp.bfloat16).reshape(TOKEN_COUNT, KEY_VALUE_HEADS, group_width, HEAD_WIDTH)
    key_row_block = key_after_rotation.astype(jnp.bfloat16).reshape(TOKEN_COUNT, KEY_VALUE_HEADS, HEAD_WIDTH)
    value_row_block = value_unprojected.astype(jnp.bfloat16).reshape(TOKEN_COUNT, KEY_VALUE_HEADS, HEAD_WIDTH)
    output_rows = cotangent.reshape(TOKEN_COUNT, KEY_VALUE_HEADS, group_width, HEAD_WIDTH)
    key_rows_padded = jnp.concatenate([jnp.zeros((WINDOW_LENGTH, KEY_VALUE_HEADS, HEAD_WIDTH), jnp.bfloat16), key_row_block], axis=0)
    value_rows_padded = jnp.concatenate([jnp.zeros((WINDOW_LENGTH, KEY_VALUE_HEADS, HEAD_WIDTH), jnp.bfloat16), value_row_block], axis=0)
    span = WINDOW_LENGTH + TOK_DEV

    def block_step(carried, block_index):
        key_gradient_sums, value_gradient_sums = carried
        start_row = (block_index * TOK_DEV).astype(jnp.int32)
        query_block = lax.dynamic_slice_in_dim(query_rows, start_row, TOK_DEV, 0)
        out_block = lax.dynamic_slice_in_dim(output_rows, start_row, TOK_DEV, 0)
        key_block = lax.dynamic_slice_in_dim(key_rows_padded, start_row, span, 0)
        value_block = lax.dynamic_slice_in_dim(value_rows_padded, start_row, span, 0)
        attended, query_grads, key_grads, value_grads = band_attention(query_block, key_block, value_block, out_block, start_row, start_row - WINDOW_LENGTH, score_scale)
        key_gradient_sums = lax.dynamic_update_slice_in_dim(key_gradient_sums, lax.dynamic_slice_in_dim(key_gradient_sums, start_row, span, 0) + key_grads, start_row, 0)
        value_gradient_sums = lax.dynamic_update_slice_in_dim(value_gradient_sums, lax.dynamic_slice_in_dim(value_gradient_sums, start_row, span, 0) + value_grads, start_row, 0)
        return ((key_gradient_sums, value_gradient_sums), (attended, query_grads))
    initial_zero_sums = jnp.zeros((TOKEN_COUNT + WINDOW_LENGTH, KEY_VALUE_HEADS, HEAD_WIDTH), jnp.float32)
    (key_gradient_sums, value_gradient_sums), (attended_blocks, query_blocks) = lax.scan(block_step, (initial_zero_sums, initial_zero_sums), jnp.arange(N_CTX, dtype=jnp.int32))
    attended = attended_blocks.reshape(TOKEN_COUNT, QUERY_HEADS * HEAD_WIDTH)
    query_back, = query_pull(query_blocks.reshape(TOKEN_COUNT, QUERY_HEADS * HEAD_WIDTH))
    key_backprop, = key_pullback(key_gradient_sums[WINDOW_LENGTH:].reshape(TOKEN_COUNT, KEY_VALUE_HEADS * HEAD_WIDTH))
    query_back = query_back.astype(jnp.bfloat16)
    key_backprop = key_backprop.astype(jnp.bfloat16)
    value_backprop = value_gradient_sums[WINDOW_LENGTH:].reshape(TOKEN_COUNT, KEY_VALUE_HEADS * HEAD_WIDTH).astype(jnp.bfloat16)
    query_cols = QUERY_HEADS * HEAD_WIDTH // N_TP
    key_column_list = KEY_VALUE_HEADS * HEAD_WIDTH // N_TP
    token_sum = jnp.zeros((TOKEN_COUNT, MODEL_WIDTH), jnp.float32)
    for group_index in range(N_TP):
        query_part = slice(group_index * query_cols, (group_index + 1) * query_cols)
        key_part = slice(group_index * key_column_list, (group_index + 1) * key_column_list)
        term_value = jnp.dot(query_back[:, query_part], query_weight[:, query_part].T, preferred_element_type=jnp.float32)
        term_value = term_value + jnp.dot(key_backprop[:, key_part], key_matrix[:, key_part].T, preferred_element_type=jnp.float32)
        term_value = term_value + jnp.dot(value_backprop[:, key_part], value_matrix[:, key_part].T, preferred_element_type=jnp.float32)
        token_sum = token_sum + lax.optimization_barrier(term_value.astype(jnp.bfloat16)).astype(jnp.float32)
    token_gradient = token_sum.astype(jnp.bfloat16)
    back_rows = jnp.concatenate([query_back, key_backprop, value_backprop], axis=1)

    def block_adder(block_index, running):
        start_row = (block_index * TOK_DEV).astype(jnp.int32)
        token_block = lax.dynamic_slice_in_dim(tokens, start_row, TOK_DEV, 0)
        back_block = lax.dynamic_slice_in_dim(back_rows, start_row, TOK_DEV, 0)
        term_value = lax.dot_general(token_block, back_block, (((0,), (0,)), ((), ())), preferred_element_type=jnp.float32)
        return running + lax.optimization_barrier(term_value.astype(jnp.bfloat16)).astype(jnp.float32)
    summed_weight = lax.fori_loop(0, N_CTX, block_adder, jnp.zeros((MODEL_WIDTH, (QUERY_HEADS + 2 * KEY_VALUE_HEADS) * HEAD_WIDTH), jnp.float32))
    query_gradient = summed_weight[:, :QUERY_HEADS * HEAD_WIDTH].astype(jnp.bfloat16)
    key_weight_gradient = summed_weight[:, QUERY_HEADS * HEAD_WIDTH:(QUERY_HEADS + KEY_VALUE_HEADS) * HEAD_WIDTH].astype(jnp.bfloat16)
    value_weight_gradient = summed_weight[:, (QUERY_HEADS + KEY_VALUE_HEADS) * HEAD_WIDTH:].astype(jnp.bfloat16)
    return (attended, token_gradient, query_gradient, key_weight_gradient, value_weight_gradient)
```

```python
import jax
import jax.numpy as jnp
from jax import lax
from jax.experimental import pallas as pl
from jax.experimental.pallas import tpu as pltpu
from jax.sharding import PartitionSpec as P

HEAD_WIDTH = 128
WINDOW_LENGTH = 1024
QUERY_SCALAR = 168


rope_base = 10000.0
norm_eps = 1e-06


def passed_along(shard, axis, by):
    size = lax.axis_size(axis)
    pairs = [(i, i + by) for i in range(size) if 0 <= i + by < size]
    return lax.ppermute(shard, axis, pairs)


def normalize_and_rotate(unnormed_rows, gain_vector, token_positions, head_count, head_size):
    row_total = unnormed_rows.shape[0]
    shaped = unnormed_rows.reshape(row_total, head_count, head_size)
    mean_square = jnp.mean(shaped * shaped, axis=-1, keepdims=True)
    normed = shaped * lax.rsqrt(mean_square + norm_eps) * gain_vector
    half_size = head_size // 2
    inverse = jnp.power(
        jnp.float32(rope_base), -jnp.arange(0, head_size, 2).astype(jnp.float32) / head_size
    )
    angles = token_positions[:, None] * inverse[None, :]
    cosine = jnp.cos(angles)[:, None, :]
    sine_part = jnp.sin(angles)[:, None, :]
    leading = normed[..., :half_size]
    trailing = normed[..., half_size:]
    turned = jnp.concatenate(
        [leading * cosine - trailing * sine_part, trailing * cosine + leading * sine_part], axis=-1
    )
    return turned.reshape(row_total, head_count * head_size)


def band_attention(
    query_rows, key_row_block, value_row_block, output_rows, first_query, first_key, score_scale
):
    scores = (
        jnp.einsum("tkgd,ckd->kgtc", query_rows, key_row_block, preferred_element_type=jnp.float32)
        * score_scale
    )
    query_place = first_query + jnp.arange(query_rows.shape[0], dtype=jnp.int32)
    key_place = first_key + jnp.arange(key_row_block.shape[0], dtype=jnp.int32)
    visible = (
        (key_place[None, :] >= 0)
        & (key_place[None, :] <= query_place[:, None])
        & (key_place[None, :] > query_place[:, None] - WINDOW_LENGTH)
    )
    exponent_terms = jnp.where(visible, jnp.exp(scores), 0.0)
    totals = jnp.sum(exponent_terms, axis=-1, keepdims=True)
    probs = exponent_terms / totals
    weights = probs.astype(jnp.bfloat16)
    mixed = jnp.einsum(
        "kgtc,ckd->tkgd", weights, value_row_block, preferred_element_type=jnp.float32
    )
    attended = mixed.astype(jnp.bfloat16)
    delta = jnp.sum(
        output_rows.astype(jnp.float32) * lax.optimization_barrier(attended).astype(jnp.float32),
        axis=-1,
    )
    delta = jnp.transpose(delta, (1, 2, 0))[..., None]
    prob_grads = jnp.einsum(
        "tkgd,ckd->kgtc", output_rows, value_row_block, preferred_element_type=jnp.float32
    )
    score_grads = (probs * (prob_grads - delta)).astype(jnp.bfloat16)
    query_grads = (
        jnp.einsum("kgtc,ckd->tkgd", score_grads, key_row_block, preferred_element_type=jnp.float32)
        * score_scale
    )
    key_grads = (
        jnp.einsum("kgtc,tkgd->ckd", score_grads, query_rows, preferred_element_type=jnp.float32)
        * score_scale
    )
    value_grads = jnp.einsum(
        "kgtc,tkgd->ckd", weights, output_rows, preferred_element_type=jnp.float32
    )
    return (attended, query_grads, key_grads, value_grads)


Z_SIZE = 8
X_SIZE = 4


def along_z(step):
    return [(i, ((i // 4 + step) % Z_SIZE) * 4 + i % 4) for i in range(4 * Z_SIZE)]


def along_x(step):
    return [(i, ((i // 2 + step) % X_SIZE) * 2 + i % 2) for i in range(2 * X_SIZE)]


SIBLING = [(i, i ^ 1) for i in range(32)]
NEAR_Y = [(i, i ^ 2) for i in range(32)]
FAR_Y = [(i, i ^ 1) for i in range(8)]


def up_z(piece):
    return lax.ppermute(piece, "ctx", along_z(1))


def down_z(piece):
    return lax.ppermute(piece, "ctx", along_z(-1))


def swap_y(piece):
    return lax.ppermute(piece, "ctx", NEAR_Y)


def swap_core(piece):
    return lax.ppermute(piece, "ctx", SIBLING)


def up_x(piece):
    return lax.ppermute(piece, "tp", along_x(1))


def down_x(piece):
    return lax.ppermute(piece, "tp", along_x(-1))


def swap_far(piece):
    return lax.ppermute(piece, "tp", FAR_Y)


def summed(*terms):
    total = terms[0].astype(jnp.float32)
    for term in terms[1:]:
        total = total + term.astype(jnp.float32)
    return total.astype(jnp.bfloat16)


def reorder_blocks(blocks, order):
    def copy_block(order_ref, in_ref, out_ref):
        out_ref[...] = in_ref[...]

    count, rows, width = blocks.shape
    return pl.pallas_call(
        copy_block,
        out_shape=jax.ShapeDtypeStruct(blocks.shape, blocks.dtype),
        grid_spec=pltpu.PrefetchScalarGridSpec(
            num_scalar_prefetch=1,
            grid=(count,),
            in_specs=[pl.BlockSpec((1, rows, width), lambda i, order_ref: (order_ref[i], 0, 0))],
            out_specs=pl.BlockSpec((1, rows, width), lambda i, order_ref: (i, 0, 0)),
        ),
        cost_estimate=pl.CostEstimate(
            flops=0, bytes_accessed=4 * count * rows * width, transcendentals=0
        ),
    )(order, blocks)


def gather_pairs_first(shard):
    pair = jnp.stack([shard, swap_y(shard)])
    ups, downs = [], []
    up, down = pair, pair
    for _ in range(3):
        up, down = up_z(up), down_z(down)
        ups.append(up)
        downs.append(down)
    far = jnp.stack([up_z(up[0]), down_z(down[1])])
    return jnp.stack([pair, downs[0], downs[1], downs[2], far, ups[2], ups[1], ups[0]])


def gather_ring_first(shard):
    half = shard.shape[1] // 2
    ups, downs = [], []
    up, down = shard, shard
    for _ in range(3):
        up, down = up_z(up), down_z(down)
        ups.append(up)
        downs.append(down)
    far = jnp.concatenate([up_z(up[:, :half]), down_z(down[:, half:])], axis=1)
    near = [shard, downs[0], downs[1], downs[2], far, ups[2], ups[1], ups[0]]
    mine = jnp.stack([shard, downs[0], ups[0]])
    theirs = swap_y(mine)
    mine2 = jnp.stack([downs[1], ups[1]])
    theirs2 = swap_y(mine2)
    mine3 = jnp.stack([downs[2], ups[2], far])
    theirs3 = swap_y(mine3)
    other = [
        theirs[0],
        theirs[1],
        theirs2[0],
        theirs3[0],
        theirs3[2],
        theirs3[1],
        theirs2[1],
        theirs[2],
    ]
    return jnp.stack([jnp.stack([a, b]) for a, b in zip(near, other)])


def scatter_ring(parts, first, second):
    up = first(parts[4])
    down = second(parts[4])
    up = up_z(up)
    down = down_z(down)
    upper = jnp.concatenate([summed(first(parts[3]), up), second(parts[3])], axis=first.axis)
    lower = jnp.concatenate([first(parts[5]), summed(second(parts[5]), down)], axis=first.axis)
    upper, lower = up_z(upper), down_z(lower)
    upper, lower = summed(parts[2], upper), summed(parts[6], lower)
    upper, lower = up_z(upper), down_z(lower)
    upper, lower = summed(parts[1], upper), summed(parts[7], lower)
    upper, lower = up_z(upper), down_z(lower)
    return parts[0], upper, lower


class Half:
    def __init__(self, axis, which):
        self.axis = axis
        self.which = which

    def __call__(self, array):
        return jnp.split(array, 2, axis=self.axis)[self.which]


def shards(tokens, query_weight, key_matrix, value_matrix, query_gain, key_norm_gain, cotangent):
    row_count = tokens.shape[0]
    heads_query = query_weight.shape[1] // HEAD_WIDTH
    heads_key = key_matrix.shape[1] // HEAD_WIDTH
    group_width = heads_query // heads_key
    reach_back = WINDOW_LENGTH // row_count
    score_scale = QUERY_SCALAR ** (-0.5)
    ctx = lax.axis_index("ctx")
    tp = lax.axis_index("tp")
    z, y, core = ctx // 4, (ctx // 2) % 2, ctx % 2
    x, far_y = tp // 2, tp % 2
    first_row = ctx * row_count
    token_positions = (first_row + jnp.arange(row_count, dtype=jnp.int32)).astype(jnp.float32)
    shard_rows = query_weight.shape[0]
    depth = tokens.shape[1]

    places = jnp.arange(32, dtype=jnp.int32)
    order = (
        ((places // 2) % 8 + z) % 8 * 4 + (places % 2 + y) % 2 * 2 + (places // 16 + core) % 2
    ).astype(jnp.int32)
    tokens_by_rows = reorder_blocks(tokens.T.reshape(32, shard_rows, row_count), order).reshape(
        depth, row_count
    )

    kv_mine = gather_pairs_first(jnp.concatenate([key_matrix, value_matrix], axis=1))
    query_mine = gather_ring_first(query_weight)
    kv_whole = jnp.stack([kv_mine, swap_core(kv_mine)]).reshape(depth, 2 * HEAD_WIDTH)
    query_whole = jnp.stack([query_mine, swap_core(query_mine)]).reshape(depth, 2 * HEAD_WIDTH)

    def project(weights):
        return lax.dot_general(
            tokens_by_rows, weights, (((0,), (0,)), ((), ())), preferred_element_type=jnp.float32
        )

    kv_raw = project(kv_whole)
    key_raw, value_unprojected = kv_raw[:, :HEAD_WIDTH], kv_raw[:, HEAD_WIDTH:]
    query_raw = project(query_whole)

    def rotate_queries(unnormed_rows):
        return normalize_and_rotate(
            unnormed_rows, query_gain, token_positions, heads_query, HEAD_WIDTH
        )

    def rotate_keys(unnormed_rows):
        return normalize_and_rotate(
            unnormed_rows, key_norm_gain, token_positions, heads_key, HEAD_WIDTH
        )

    query_after_rotation, query_pull = jax.vjp(rotate_queries, query_raw)
    key_after_rotation, key_pullback = jax.vjp(rotate_keys, key_raw)
    query_rows = query_after_rotation.astype(jnp.bfloat16).reshape(
        row_count, heads_key, group_width, HEAD_WIDTH
    )
    stacked = jnp.stack(
        [
            key_after_rotation.astype(jnp.bfloat16).reshape(row_count, heads_key, HEAD_WIDTH),
            value_unprojected.astype(jnp.bfloat16).reshape(row_count, heads_key, HEAD_WIDTH),
        ]
    )
    arrivals = [passed_along(stacked, "ctx", by) for by in range(reach_back, 0, -1)]
    band_rows = jnp.concatenate(arrivals + [stacked], axis=1)
    output_rows = cotangent.reshape(row_count, heads_key, group_width, HEAD_WIDTH)
    attended, query_grads, key_grads, value_grads = band_attention(
        query_rows,
        band_rows[0],
        band_rows[1],
        output_rows,
        first_row,
        first_row - WINDOW_LENGTH,
        score_scale,
    )
    band_grads = jnp.stack([key_grads, value_grads])

    def band_tile(distance):
        lowest = (reach_back - distance) * row_count
        return band_grads[:, lowest : lowest + row_count]

    returned = band_tile(0)
    for by in range(reach_back, 0, -1):
        returned = returned + passed_along(
            band_tile(by).astype(jnp.bfloat16), "ctx", -by
        ).astype(jnp.float32)
    (query_back,) = query_pull(query_grads.reshape(row_count, heads_query * HEAD_WIDTH))
    (key_backprop,) = key_pullback(returned[0].reshape(row_count, heads_key * HEAD_WIDTH))
    query_back = query_back.astype(jnp.bfloat16)
    kv_back = jnp.concatenate(
        [key_backprop.astype(jnp.bfloat16), returned[1].reshape(row_count, HEAD_WIDTH).astype(jnp.bfloat16)],
        axis=1,
    )

    def weight_terms(back):
        terms = jnp.dot(tokens_by_rows, back, preferred_element_type=jnp.float32)
        terms = terms.astype(jnp.bfloat16).reshape(2, 8, 2, shard_rows, 2 * HEAD_WIDTH)
        return summed(terms[0], swap_core(terms[1]))

    query_terms = weight_terms(query_back)
    query_own, query_up, query_down = scatter_ring(
        [query_terms[i] for i in range(8)], Half(0, 0), Half(0, 1)
    )
    query_pair = summed(query_own, query_up, query_down)
    query_gradient = summed(query_pair[0], swap_y(query_pair[1]))

    kv_terms = weight_terms(kv_back)
    late = jnp.stack([kv_terms[i, 1] for i in (4, 3, 5)])
    rest = jnp.stack([kv_terms[i, 1] for i in (2, 6, 1, 7, 0)])
    late, rest = swap_y(late), swap_y(rest)
    arrived = {4: late[0], 3: late[1], 5: late[2], 2: rest[0], 6: rest[1], 1: rest[2], 7: rest[3], 0: rest[4]}
    kv_gradient = summed(
        *scatter_ring(
            [summed(kv_terms[i, 0], arrived[i]) for i in range(8)], Half(1, 0), Half(1, 1)
        )
    )

    token_terms = lax.dot_general(
        query_whole, query_back, (((1,), (1,)), ((), ())), preferred_element_type=jnp.float32
    ) + lax.dot_general(
        kv_whole, kv_back, (((1,), (1,)), ((), ())), preferred_element_type=jnp.float32
    )
    token_terms = token_terms.astype(jnp.bfloat16).reshape(2, 8, 2 * shard_rows, row_count)

    def token_part(x_offset, far_offset):
        owner = (x + x_offset) % 4 * 2 + (far_y + far_offset) % 2
        return lax.dynamic_slice_in_dim(token_terms, (owner - z) % 8, 1, 1)

    def token_pair(x_offset):
        return jnp.stack([token_part(x_offset, 0), token_part(x_offset, 1)])

    up = up_x(token_part(2, 0))
    down = down_x(token_part(2, 1))
    upper = jnp.stack([summed(token_part(1, 0), up), token_part(1, 1)])
    lower = jnp.stack([token_part(3, 0), summed(token_part(3, 1), down)])
    upper, lower = up_x(upper), down_x(lower)
    token_own = summed(token_pair(0), upper, lower)
    token_sum = summed(token_own[0], swap_far(token_own[1])).reshape(2, 2, shard_rows, row_count)
    token_sum = jnp.where(core == 1, token_sum[::-1], token_sum)
    token_sum = jnp.where(y == 1, token_sum[:, ::-1], token_sum)
    token_gradient = jnp.transpose(token_sum, (3, 1, 0, 2)).reshape(row_count, 4 * shard_rows)
    key_columns = key_matrix.shape[1]
    return (
        attended.reshape(row_count, heads_query * HEAD_WIDTH),
        token_gradient,
        query_gradient,
        kv_gradient[:, :key_columns],
        kv_gradient[:, key_columns:],
    )


def solution(mesh):
    in_specs = (
        P("ctx", None),
        P("ctx", "tp"),
        P("ctx", "tp"),
        P("ctx", "tp"),
        P(),
        P(),
        P("ctx", "tp"),
    )
    out_specs = (P("ctx", "tp"), P("ctx", "tp"), P("ctx", "tp"), P("ctx", "tp"), P("ctx", "tp"))
    return jax.shard_map(shards, mesh=mesh, in_specs=in_specs, out_specs=out_specs, check_vma=False)
```

```python
import functools

import jax
import jax.numpy as jnp
from jax import lax
from jax.experimental import pallas as pl
from jax.experimental.pallas import tpu as pltpu
from jax.sharding import PartitionSpec as P

HEAD_WIDTH = 128
WINDOW_LENGTH = 1024
QUERY_SCALAR = 168
SCORE_SCALE = QUERY_SCALAR ** (-0.5)

rope_base = 10000.0
norm_eps = 1e-06

Z_SIZE = 8
X_SIZE = 4
ROWS = 512
TILE = 256
SPAN = WINDOW_LENGTH + TILE
BAND = WINDOW_LENGTH + ROWS
DEPTH = 5376
BLOCK = 336
PART = 672
BF = jnp.bfloat16
F32 = jnp.float32
VMEM_BYTES = 50 * 1024 * 1024


def along_z(step):
    return [(i, ((i // 4 + step) % Z_SIZE) * 4 + i % 4) for i in range(4 * Z_SIZE)]


def along_x(step):
    return [(i, ((i // 2 + step) % X_SIZE) * 2 + i % 2) for i in range(2 * X_SIZE)]


SIBLING = [(i, i ^ 1) for i in range(32)]
NEAR_Y = [(i, i ^ 2) for i in range(32)]
FAR_Y = [(i, i ^ 1) for i in range(8)]


def up_z(piece):
    return lax.ppermute(piece, "ctx", along_z(1))


def down_z(piece):
    return lax.ppermute(piece, "ctx", along_z(-1))


def swap_y(piece):
    return lax.ppermute(piece, "ctx", NEAR_Y)


def swap_core(piece):
    return lax.ppermute(piece, "ctx", SIBLING)


def up_x(piece):
    return lax.ppermute(piece, "tp", along_x(1))


def down_x(piece):
    return lax.ppermute(piece, "tp", along_x(-1))


def swap_far(piece):
    return lax.ppermute(piece, "tp", FAR_Y)


def passed_along(shard, by):
    pairs = [(i, i + by) for i in range(32) if 0 <= i + by < 32]
    return lax.ppermute(shard, "ctx", pairs)


def summed(*terms):
    total = terms[0].astype(F32)
    for term in terms[1:]:
        total = total + term.astype(F32)
    return total.astype(BF)


def dot(left, right, left_axis=1, right_axis=0):
    return lax.dot_general(
        left, right, (((left_axis,), (right_axis,)), ((), ())), preferred_element_type=F32
    )


def params():
    return pltpu.CompilerParams(vmem_limit_bytes=VMEM_BYTES)


def cost(flops, moved):
    return pl.CostEstimate(flops=flops, bytes_accessed=moved, transcendentals=0)


VMEM = pl.BlockSpec(memory_space=pltpu.VMEM)
SMEM = pl.BlockSpec(memory_space=pltpu.SMEM)


def rotate(raw, gain, cosine, sine):
    scale = lax.rsqrt(jnp.mean(raw * raw, axis=-1, keepdims=True) + norm_eps)
    normed = raw * scale * gain
    return normed * cosine + pltpu.roll(normed, HEAD_WIDTH // 2, 1) * sine


def rotate_back(raw, grads, gain, cosine, sine):
    scale = lax.rsqrt(jnp.mean(raw * raw, axis=-1, keepdims=True) + norm_eps)
    turned = (grads * cosine - pltpu.roll(grads, HEAD_WIDTH // 2, 1) * sine) * gain
    inner = jnp.mean(raw * turned, axis=-1, keepdims=True)
    return turned * scale - raw * (scale * scale * scale * inner)


DEPTH_STEPS = 3
DEPTH_STEP = DEPTH // DEPTH_STEPS


def project_body(offsets, normed_heads, pos, tokens, gain, cosine, sine, *refs):
    pieces = refs[: 2 * len(offsets)]
    raw, rows, weights = refs[2 * len(offsets) :]
    step = pl.program_id(0)

    @pl.when(step == 0)
    def place():
        z, y, core = pos[0], pos[1], pos[2]
        for number, piece in enumerate(pieces):
            z_offset, y_offsets = offsets[number % len(offsets)]
            column = core if number < len(offsets) else 1 - core
            column = pl.multiple_of(column * HEAD_WIDTH, HEAD_WIDTH)
            for slot, y_offset in enumerate(y_offsets):
                block = lax.rem(z + z_offset, 8) * 2 + lax.rem(y + y_offset, 2)
                start = pl.multiple_of(block * BLOCK, 16)
                weights[pl.ds(start, BLOCK), pl.ds(column, HEAD_WIDTH)] = piece[slot]
        raw[...] = jnp.zeros_like(raw)

    start = pl.multiple_of(step * DEPTH_STEP, DEPTH_STEP)
    raw[...] += dot(tokens[...], weights[pl.ds(start, DEPTH_STEP), :])

    @pl.when(step == DEPTH_STEPS - 1)
    def finish():
        for head in range(2):
            columns = slice(head * HEAD_WIDTH, (head + 1) * HEAD_WIDTH)
            part = raw[:, columns]
            if head < normed_heads:
                part = rotate(part, gain[...], cosine[...], sine[...])
            rows[head] = part.astype(BF)


def project(pos, tokens, gain, cosine, sine, mine, theirs, normed_heads):
    offsets = tuple((z_offset, y_offsets) for _, z_offset, y_offsets in mine)
    pieces = [entry[0] for entry in mine] + [entry[0] for entry in theirs]
    whole = lambda shape: pl.BlockSpec(shape, lambda k: (0,) * len(shape))
    return pl.pallas_call(
        functools.partial(project_body, offsets, normed_heads),
        grid=(DEPTH_STEPS,),
        in_specs=[
            SMEM,
            pl.BlockSpec((ROWS, DEPTH_STEP), lambda k: (0, k)),
            whole((1, HEAD_WIDTH)),
            whole((ROWS, HEAD_WIDTH)),
            whole((ROWS, HEAD_WIDTH)),
        ]
        + [whole(piece.shape) for piece in pieces],
        out_specs=[
            whole((ROWS, 2 * HEAD_WIDTH)),
            whole((2, ROWS, HEAD_WIDTH)),
            whole((DEPTH, 2 * HEAD_WIDTH)),
        ],
        out_shape=[
            jax.ShapeDtypeStruct((ROWS, 2 * HEAD_WIDTH), F32),
            jax.ShapeDtypeStruct((2, ROWS, HEAD_WIDTH), BF),
            jax.ShapeDtypeStruct((DEPTH, 2 * HEAD_WIDTH), BF),
        ],
        compiler_params=params(),
        cost_estimate=cost(2 * ROWS * DEPTH * 256, 12_000_000),
    )(pos, tokens, gain, cosine, sine, *pieces)


def attend_body(
    pos, queries, near0, near1, near2, cotangent, attended, grads0, grads1, grads2, score_grads,
    keys, values, values_turned, terms, weights, key_sums, value_sums,
):
    for part, ref in enumerate((near2, near1, near0)):
        keys[part * ROWS : (part + 1) * ROWS] = ref[0]
        values[part * ROWS : (part + 1) * ROWS] = ref[1]
        values_turned[:, part * ROWS : (part + 1) * ROWS] = ref[1].astype(F32).T.astype(BF)
    key_sums[...] = jnp.zeros_like(key_sums)
    value_sums[...] = jnp.zeros_like(value_sums)
    valid2 = (pos[3] >= 2).astype(F32)
    valid1 = (pos[3] >= 1).astype(F32)
    valid = (valid2, valid2, valid1, valid1, None, None)
    key_place = lax.broadcasted_iota(jnp.int32, (TILE, TILE), 0)
    query_place = lax.broadcasted_iota(jnp.int32, (TILE, TILE), 1)
    for head in range(2):
        columns = slice(head * HEAD_WIDTH, (head + 1) * HEAD_WIDTH)
        for tile in range(2):
            here = slice(tile * TILE, (tile + 1) * TILE)
            span = slice(tile * TILE, tile * TILE + SPAN)
            query = queries[head, here]
            out = cotangent[here, columns]
            total = jnp.zeros((1, TILE), F32)
            for block in range(5):
                low = block * TILE
                scores = dot(keys[tile * TILE + low : tile * TILE + low + TILE], query, 1, 1)
                term = jnp.exp(scores * SCORE_SCALE)
                if block == 0:
                    term = jnp.where(key_place > query_place, term, 0.0)
                if block == 4:
                    term = jnp.where(key_place <= query_place, term, 0.0)
                if valid[tile + block] is not None:
                    term = term * valid[tile + block]
                terms[low : low + TILE] = term
                total = total + jnp.sum(term, axis=0, keepdims=True)
            inverse = 1.0 / total
            for block in range(5):
                low = block * TILE
                weights[low : low + TILE] = (terms[low : low + TILE] * inverse).astype(BF)
            mixed = dot(values_turned[:, span], weights[...])
            rounded = mixed.astype(BF).astype(F32)
            attended[here, columns] = mixed.T.astype(BF)
            delta = jnp.sum(out.astype(F32).T * rounded, axis=0, keepdims=True)
            for block in range(5):
                low = block * TILE
                prob_grads = dot(values[tile * TILE + low : tile * TILE + low + TILE], out, 1, 1)
                probs = terms[low : low + TILE] * inverse
                score_grads[head, tile, low : low + TILE] = (probs * (prob_grads - delta)).astype(BF)
            key_sums[span] += dot(score_grads[head, tile], query)
            value_sums[span] += dot(weights[...], out)
    for part, ref in enumerate((grads2, grads1, grads0)):
        rows = slice(part * ROWS, (part + 1) * ROWS)
        ref[0] = (key_sums[rows] * SCORE_SCALE).astype(ref.dtype)
        ref[1] = value_sums[rows].astype(ref.dtype)


def attend(pos, queries, near0, near1, near2, cotangent):
    pair = (2, ROWS, HEAD_WIDTH)
    return pl.pallas_call(
        attend_body,
        in_specs=[SMEM] + [VMEM] * 5,
        out_specs=[VMEM] * 5,
        out_shape=[
            jax.ShapeDtypeStruct((ROWS, 2 * HEAD_WIDTH), BF),
            jax.ShapeDtypeStruct(pair, F32),
            jax.ShapeDtypeStruct(pair, BF),
            jax.ShapeDtypeStruct(pair, BF),
            jax.ShapeDtypeStruct((2, 2, SPAN, TILE), BF),
        ],
        scratch_shapes=[
            pltpu.VMEM((BAND, HEAD_WIDTH), BF),
            pltpu.VMEM((BAND, HEAD_WIDTH), BF),
            pltpu.VMEM((HEAD_WIDTH, BAND), BF),
            pltpu.VMEM((SPAN, TILE), F32),
            pltpu.VMEM((SPAN, TILE), BF),
            pltpu.VMEM((BAND, HEAD_WIDTH), F32),
            pltpu.VMEM((BAND, HEAD_WIDTH), F32),
        ],
        compiler_params=params(),
        cost_estimate=cost(8_000_000_000, 8_000_000),
    )(pos, queries, near0, near1, near2, cotangent)


def query_back_body(
    score_grads, near0, near1, near2, raw, gain, cosine, sine, back, back_turned, keys_turned
):
    for part, ref in enumerate((near2, near1, near0)):
        keys_turned[:, part * ROWS : (part + 1) * ROWS] = ref[0].astype(F32).T.astype(BF)
    for head in range(2):
        columns = slice(head * HEAD_WIDTH, (head + 1) * HEAD_WIDTH)
        for tile in range(2):
            here = slice(tile * TILE, (tile + 1) * TILE)
            grads = dot(keys_turned[:, tile * TILE : tile * TILE + SPAN], score_grads[head, tile])
            grads = (grads * SCORE_SCALE).T
            part = rotate_back(raw[here, columns], grads, gain[...], cosine[here], sine[here])
            back[here, columns] = part.astype(BF)
            back_turned[columns, here] = part.T.astype(BF)


def query_back(score_grads, near0, near1, near2, raw, gain, cosine, sine):
    return pl.pallas_call(
        query_back_body,
        in_specs=[VMEM] * 8,
        out_specs=[VMEM] * 2,
        out_shape=[
            jax.ShapeDtypeStruct((ROWS, 2 * HEAD_WIDTH), BF),
            jax.ShapeDtypeStruct((2 * HEAD_WIDTH, ROWS), BF),
        ],
        scratch_shapes=[pltpu.VMEM((HEAD_WIDTH, BAND), BF)],
        compiler_params=params(),
        cost_estimate=cost(1_000_000_000, 4_000_000),
    )(score_grads, near0, near1, near2, raw, gain, cosine, sine)


def pair_back_body(own, from1, from2, raw, gain, cosine, sine, back, back_turned):
    grads = own[...] + from1[...].astype(F32) + from2[...].astype(F32)
    key_part = rotate_back(raw[:, :HEAD_WIDTH], grads[0], gain[...], cosine[...], sine[...])
    for number, part in enumerate((key_part, grads[1])):
        columns = slice(number * HEAD_WIDTH, (number + 1) * HEAD_WIDTH)
        back[:, columns] = part.astype(BF)
        back_turned[columns, :] = part.T.astype(BF)


def pair_back(own, from1, from2, raw, gain, cosine, sine):
    return pl.pallas_call(
        pair_back_body,
        in_specs=[VMEM] * 7,
        out_specs=[VMEM] * 2,
        out_shape=[
            jax.ShapeDtypeStruct((ROWS, 2 * HEAD_WIDTH), BF),
            jax.ShapeDtypeStruct((2 * HEAD_WIDTH, ROWS), BF),
        ],
        compiler_params=params(),
        cost_estimate=cost(10_000_000, 3_000_000),
    )(own, from1, from2, raw, gain, cosine, sine)


def weight_terms_body(pos, tokens, back, mine, theirs):
    step = pl.program_id(0)
    z, y, core = pos[0], pos[1], pos[2]
    halves = (back[:, :HEAD_WIDTH].astype(F32), back[:, HEAD_WIDTH:].astype(F32))
    weight = core.astype(F32)
    first = halves[0] * (1.0 - weight) + halves[1] * weight
    second = halves[1] * (1.0 - weight) + halves[0] * weight
    ordered = jnp.concatenate([first, second], axis=1).astype(BF)
    terms = dot(tokens[...], ordered, 0, 0).astype(BF)
    for block in range(8):
        z_offset = lax.rem(step * 4 + block // 2 - z + 8, 8)
        y_offset = lax.rem(block % 2 + y, 2)
        rows = slice(block * BLOCK, (block + 1) * BLOCK)
        mine[z_offset, y_offset] = terms[rows, :HEAD_WIDTH]
        theirs[z_offset, y_offset] = terms[rows, HEAD_WIDTH:]


def weight_terms(pos, tokens, back):
    shape = (8, 2, BLOCK, HEAD_WIDTH)
    return pl.pallas_call(
        weight_terms_body,
        grid=(2,),
        in_specs=[
            SMEM,
            pl.BlockSpec((ROWS, DEPTH // 2), lambda k: (0, k)),
            pl.BlockSpec((ROWS, 2 * HEAD_WIDTH), lambda k: (0, 0)),
        ],
        out_specs=[pl.BlockSpec(shape, lambda k: (0, 0, 0, 0))] * 2,
        out_shape=[jax.ShapeDtypeStruct(shape, BF)] * 2,
        compiler_params=params(),
        cost_estimate=cost(2 * ROWS * DEPTH * 256, 9_000_000),
    )(pos, tokens, back)


def token_terms_body(parts, pos, query_weights, pair_weights, query_turned, pair_turned, *outs):
    turned = jnp.concatenate([query_turned[...], pair_turned[...]], axis=0)
    for number, (x_offset, far_offset) in enumerate(parts):
        part = lax.rem(pos[4] + x_offset, X_SIZE) * 2 + lax.rem(pos[5] + far_offset, 2)
        rows = pl.ds(pl.multiple_of(part * PART, 16), PART)
        weights = jnp.concatenate([query_weights[rows, :], pair_weights[rows, :]], axis=1)
        outs[number][...] = dot(weights, turned).astype(BF)


def token_terms(pos, query_weights, pair_weights, query_turned, pair_turned, parts):
    return pl.pallas_call(
        functools.partial(token_terms_body, parts),
        in_specs=[SMEM] + [VMEM] * 4,
        out_specs=[VMEM] * len(parts),
        out_shape=[jax.ShapeDtypeStruct((PART, ROWS), BF)] * len(parts),
        compiler_params=params(),
        cost_estimate=cost(2 * PART * ROWS * 512 * len(parts), 5_500_000 + 700_000 * len(parts)),
    )(pos, query_weights, pair_weights, query_turned, pair_turned)


def chip_shard(shard_halves, core):
    kept = jnp.where(core == 0, shard_halves[0], shard_halves[1])
    sent = jnp.where(core == 0, shard_halves[1], shard_halves[0])
    came = swap_core(sent)
    return jnp.concatenate(
        [jnp.where(core == 0, kept, came), jnp.where(core == 0, came, kept)], axis=-2
    )


def gather(pair):
    both = (0, 1)
    entries = [(pair, 0, both)]
    up, down = pair, pair
    for hop in range(1, 4):
        up, down = up_z(up), down_z(down)
        entries += [(up, 8 - hop, both), (down, hop, both)]
    entries += [(up_z(up[:1]), 4, (0,)), (down_z(down[1:]), 4, (1,))]
    return entries


def swapped(entries):
    return [(swap_core(array), z_offset, y_offsets) for array, z_offset, y_offsets in entries]


def scatter_ring(own, came):
    part = lambda hop: summed(own[hop], came[hop])
    far = part(4)
    up, down = up_z(far[:1]), down_z(far[1:])
    upper, lower = part(3), part(5)
    upper = jnp.concatenate([summed(upper[:1], up), upper[1:]])
    lower = jnp.concatenate([lower[:1], summed(lower[1:], down)])
    upper, lower = up_z(upper), down_z(lower)
    upper, lower = summed(own[2], came[2], upper), summed(own[6], came[6], lower)
    upper, lower = up_z(upper), down_z(lower)
    upper, lower = summed(own[1], came[1], upper), summed(own[7], came[7], lower)
    upper, lower = up_z(upper), down_z(lower)
    sent = summed(own[0, 1], came[0, 1], upper[1], lower[1])
    came_y = swap_y(sent)
    return summed(own[0, 0], came[0, 0], upper[0], lower[0], came_y)


def own_rows(chip_part, core):
    rows = chip_part.reshape(2, BLOCK // 2, HEAD_WIDTH)
    kept = jnp.where(core == 0, rows[0], rows[1])
    came = swap_core(jnp.where(core == 0, rows[1], rows[0]))
    return jnp.where(core == 0, kept, came), jnp.where(core == 0, came, kept)


def shards(tokens, query_weight, key_matrix, value_matrix, query_gain, key_norm_gain, cotangent):
    ctx = lax.axis_index("ctx")
    tp = lax.axis_index("tp")
    z, y, core = ctx // 4, (ctx // 2) % 2, ctx % 2
    pos = jnp.stack([z, y, core, ctx, tp // 2, tp % 2]).astype(jnp.int32)
    token_positions = (ctx * ROWS + jnp.arange(ROWS, dtype=jnp.int32)).astype(F32)
    inverse = jnp.power(
        F32(rope_base), -jnp.arange(0, HEAD_WIDTH, 2).astype(F32) / HEAD_WIDTH
    )
    angles = token_positions[:, None] * inverse[None, :]
    cosine, sine = jnp.cos(angles), jnp.sin(angles)
    cosine = jnp.concatenate([cosine, cosine], axis=1)
    sine = jnp.concatenate([-sine, sine], axis=1)
    query_gain = query_gain.reshape(1, HEAD_WIDTH)
    key_gain = key_norm_gain.reshape(1, HEAD_WIDTH)

    chip = chip_shard(
        jnp.stack(
            [
                jnp.stack([key_matrix, query_weight[:, :HEAD_WIDTH]]),
                jnp.stack([value_matrix, query_weight[:, HEAD_WIDTH:]]),
            ]
        ),
        core,
    )
    other = swap_y(chip)
    pair_mine = gather(jnp.stack([chip[0], other[0]]))
    query_mine = gather(jnp.stack([chip[1], other[1]]))
    pair_raw, near0, pair_weights = project(
        pos, tokens, key_gain, cosine, sine, pair_mine, swapped(pair_mine), 1
    )
    near1, near2 = passed_along(near0, 1), passed_along(near0, 2)
    query_raw, queries, query_weights = project(
        pos, tokens, query_gain, cosine, sine, query_mine, swapped(query_mine), 2
    )
    attended, grads0, grads1, grads2, score_grads = attend(
        pos, queries, near0, near1, near2, cotangent
    )
    from2, from1 = passed_along(grads2, -2), passed_along(grads1, -1)
    back, back_turned = query_back(
        score_grads, near0, near1, near2, query_raw, query_gain, cosine, sine
    )
    query_own, query_other = weight_terms(pos, tokens, back)
    query_came = swap_core(query_other)
    back_pair, pair_turned = pair_back(grads0, from1, from2, pair_raw, key_gain, cosine, sine)

    part = functools.partial(
        token_terms, pos, query_weights, pair_weights, back_turned, pair_turned
    )
    far0, far1 = part(((2, 0), (2, 1)))
    half = ROWS // 2
    up1, down1 = up_x(far1[:, :half]), down_x(far1[:, half:])
    up0, down0 = up_x(far0[:, :half]), down_x(far0[:, half:])
    right1, left1, right0, left0, mine1, mine0 = part(
        ((1, 1), (3, 1), (1, 0), (3, 0), (0, 1), (0, 0))
    )
    pair_own, pair_other = weight_terms(pos, tokens, back_pair)
    pair_came = swap_core(pair_other)

    def joined(upward, downward, up, down):
        upward = jnp.concatenate([summed(upward[:, :half], up), upward[:, half:]], axis=1)
        downward = jnp.concatenate([downward[:, :half], summed(downward[:, half:], down)], axis=1)
        return up_x(upward), down_x(downward)

    got_up1, got_down1 = joined(right1, left1, up1, down1)
    got_up0, got_down0 = joined(right0, left0, up0, down0)
    far = swap_far(summed(mine1, got_up1, got_down1))
    token_gradient = summed(mine0, got_up0, got_down0, far).T

    query_chip = scatter_ring(query_own, query_came)
    pair_chip = scatter_ring(pair_own, pair_came)
    query_first, query_second = own_rows(query_chip, core)
    key_gradient, value_gradient = own_rows(pair_chip, core)
    return (
        attended,
        token_gradient,
        jnp.concatenate([query_first, query_second], axis=1),
        key_gradient,
        value_gradient,
    )


def solution(mesh):
    in_specs = (
        P("ctx", None),
        P("ctx", "tp"),
        P("ctx", "tp"),
        P("ctx", "tp"),
        P(),
        P(),
        P("ctx", "tp"),
    )
    out_specs = (P("ctx", "tp"), P("ctx", "tp"), P("ctx", "tp"), P("ctx", "tp"), P("ctx", "tp"))
    return jax.shard_map(shards, mesh=mesh, in_specs=in_specs, out_specs=out_specs, check_vma=False)
```

```python
import functools

import jax
import jax.numpy as jnp
from jax import lax
from jax.experimental import pallas as pl
from jax.experimental.pallas import tpu as pltpu
from jax.sharding import PartitionSpec as P

HEAD_WIDTH = 128
WINDOW_LENGTH = 1024
QUERY_SCALAR = 168
SCORE_SCALE = QUERY_SCALAR ** (-0.5)

rope_base = 10000.0
norm_eps = 1e-06

Z_SIZE = 8
X_SIZE = 4
ROWS = 512
TILE = 256
SPAN = WINDOW_LENGTH + TILE
BAND = WINDOW_LENGTH + ROWS
DEPTH = 5376
BLOCK = 336
PART = 672
BF = jnp.bfloat16
F32 = jnp.float32
VMEM_BYTES = 50 * 1024 * 1024


def along_z(step):
    return [(i, ((i // 4 + step) % Z_SIZE) * 4 + i % 4) for i in range(4 * Z_SIZE)]


def along_x(step):
    return [(i, ((i // 2 + step) % X_SIZE) * 2 + i % 2) for i in range(2 * X_SIZE)]


SIBLING = [(i, i ^ 1) for i in range(32)]
NEAR_Y = [(i, i ^ 2) for i in range(32)]
FAR_Y = [(i, i ^ 1) for i in range(8)]


def up_z(piece):
    return lax.ppermute(piece, "ctx", along_z(1))


def down_z(piece):
    return lax.ppermute(piece, "ctx", along_z(-1))


def swap_y(piece):
    return lax.ppermute(piece, "ctx", NEAR_Y)


def swap_core(piece):
    return lax.ppermute(piece, "ctx", SIBLING)


def up_x(piece):
    return lax.ppermute(piece, "tp", along_x(1))


def down_x(piece):
    return lax.ppermute(piece, "tp", along_x(-1))


def swap_far(piece):
    return lax.ppermute(piece, "tp", FAR_Y)


def passed_along(shard, by):
    pairs = [(i, i + by) for i in range(32) if 0 <= i + by < 32]
    return lax.ppermute(shard, "ctx", pairs)


def summed(*terms):
    total = terms[0].astype(F32)
    for term in terms[1:]:
        total = total + term.astype(F32)
    return total.astype(BF)


def dot(left, right, left_axis=1, right_axis=0):
    return lax.dot_general(
        left, right, (((left_axis,), (right_axis,)), ((), ())), preferred_element_type=F32
    )


def params():
    return pltpu.CompilerParams(vmem_limit_bytes=VMEM_BYTES)


def cost(flops, moved):
    return pl.CostEstimate(flops=flops, bytes_accessed=moved, transcendentals=0)


VMEM = pl.BlockSpec(memory_space=pltpu.VMEM)
ANY = pl.BlockSpec(memory_space=pl.ANY)
SMEM = pl.BlockSpec(memory_space=pltpu.SMEM)


def rotate(raw, gain, cosine, sine):
    scale = lax.rsqrt(jnp.mean(raw * raw, axis=-1, keepdims=True) + norm_eps)
    normed = raw * scale * gain
    return normed * cosine + pltpu.roll(normed, HEAD_WIDTH // 2, 1) * sine


def rotate_back(raw, grads, gain, cosine, sine):
    scale = lax.rsqrt(jnp.mean(raw * raw, axis=-1, keepdims=True) + norm_eps)
    turned = (grads * cosine - pltpu.roll(grads, HEAD_WIDTH // 2, 1) * sine) * gain
    inner = jnp.mean(raw * turned, axis=-1, keepdims=True)
    return turned * scale - raw * (scale * scale * scale * inner)


DEPTH_STEPS = 3
DEPTH_STEP = DEPTH // DEPTH_STEPS
WIDE = 2 * HEAD_WIDTH


def by_core(core, first, second):
    return jnp.where(core == 0, first, second), jnp.where(core == 0, second, first)


def project_body(places, pos, tokens, key_gain, query_gain, cosine, sine, *refs):
    count = len(places)
    pieces = refs[:count]
    pair_raw, query_raw, pair_rows, query_rows, kept, weights, total, sems, out_sem = refs[count:]
    step = pl.program_id(0)
    z, y, core = pos[0], pos[1], pos[2]

    @pl.when(step == 0)
    def place():
        copies = []
        for number, (z_offset, y_offset, column, width) in enumerate(places):
            block = lax.rem(z + z_offset, 8) * 2 + lax.rem(y + y_offset, 2)
            start = pl.multiple_of(block * BLOCK, 16)
            copies.append(
                pltpu.make_async_copy(
                    pieces[number],
                    weights.at[pl.ds(start, BLOCK), pl.ds(column, width)],
                    sems.at[number],
                )
            )
        for copy in copies:
            copy.start()
        for copy in copies:
            copy.wait()
        pltpu.make_async_copy(weights, kept, out_sem).start()
        total[...] = jnp.zeros_like(total)

    start = pl.multiple_of(step * DEPTH_STEP, DEPTH_STEP)
    total[...] += dot(tokens[...], weights[pl.ds(start, DEPTH_STEP), :])

    @pl.when(step == DEPTH_STEPS - 1)
    def finish():
        key, value = by_core(core, total[:, :HEAD_WIDTH], total[:, WIDE : WIDE + HEAD_WIDTH])
        first, second = by_core(core, total[:, HEAD_WIDTH:WIDE], total[:, WIDE + HEAD_WIDTH :])
        pair_raw[...] = key
        query_raw[0] = first
        query_raw[1] = second
        pair_rows[0] = rotate(key, key_gain[...], cosine[...], sine[...]).astype(BF)
        pair_rows[1] = value.astype(BF)
        query_rows[0] = rotate(first, query_gain[...], cosine[...], sine[...]).astype(BF)
        query_rows[1] = rotate(second, query_gain[...], cosine[...], sine[...]).astype(BF)
        pltpu.make_async_copy(weights, kept, out_sem).wait()


def project(pos, tokens, key_gain, query_gain, cosine, sine, entries):
    places = tuple((e[1], e[2], e[3], e[0].shape[1]) for e in entries)
    whole = lambda shape: pl.BlockSpec(shape, lambda k: (0,) * len(shape))
    pair = (2, ROWS, HEAD_WIDTH)
    return pl.pallas_call(
        functools.partial(project_body, places),
        grid=(DEPTH_STEPS,),
        in_specs=[
            SMEM,
            pl.BlockSpec((ROWS, DEPTH_STEP), lambda k: (0, k)),
            whole((1, HEAD_WIDTH)),
            whole((1, HEAD_WIDTH)),
            whole((ROWS, HEAD_WIDTH)),
            whole((ROWS, HEAD_WIDTH)),
        ]
        + [ANY] * len(entries),
        out_specs=[whole((ROWS, HEAD_WIDTH)), whole(pair), whole(pair), whole(pair), ANY],
        out_shape=[
            jax.ShapeDtypeStruct((ROWS, HEAD_WIDTH), F32),
            jax.ShapeDtypeStruct(pair, F32),
            jax.ShapeDtypeStruct(pair, BF),
            jax.ShapeDtypeStruct(pair, BF),
            jax.ShapeDtypeStruct((DEPTH, 2 * WIDE), BF),
        ],
        scratch_shapes=[
            pltpu.VMEM((DEPTH, 2 * WIDE), BF),
            pltpu.VMEM((ROWS, 2 * WIDE), F32),
            pltpu.SemaphoreType.DMA((len(entries),)),
            pltpu.SemaphoreType.DMA,
        ],
        compiler_params=params(),
        cost_estimate=cost(2 * ROWS * DEPTH * 512, 17_000_000),
    )(pos, tokens, key_gain, query_gain, cosine, sine, *[e[0] for e in entries])


def attend_body(
    pos, queries, near0, near1, near2, cotangent, attended, grads0, grads1, grads2, score_grads,
    keys, values, values_turned, terms, weights, key_sums, value_sums,
):
    for part, ref in enumerate((near2, near1, near0)):
        keys[part * ROWS : (part + 1) * ROWS] = ref[0]
        values[part * ROWS : (part + 1) * ROWS] = ref[1]
        values_turned[:, part * ROWS : (part + 1) * ROWS] = ref[1].astype(F32).T.astype(BF)
    key_sums[...] = jnp.zeros_like(key_sums)
    value_sums[...] = jnp.zeros_like(value_sums)
    valid2 = (pos[3] >= 2).astype(F32)
    valid1 = (pos[3] >= 1).astype(F32)
    valid = (valid2, valid2, valid1, valid1, None, None)
    key_place = lax.broadcasted_iota(jnp.int32, (TILE, TILE), 0)
    query_place = lax.broadcasted_iota(jnp.int32, (TILE, TILE), 1)
    for head in range(2):
        columns = slice(head * HEAD_WIDTH, (head + 1) * HEAD_WIDTH)
        for tile in range(2):
            here = slice(tile * TILE, (tile + 1) * TILE)
            span = slice(tile * TILE, tile * TILE + SPAN)
            query = queries[head, here]
            out = cotangent[here, columns]
            total = jnp.zeros((1, TILE), F32)
            for block in range(5):
                low = block * TILE
                scores = dot(keys[tile * TILE + low : tile * TILE + low + TILE], query, 1, 1)
                term = jnp.exp(scores * SCORE_SCALE)
                if block == 0:
                    term = jnp.where(key_place > query_place, term, 0.0)
                if block == 4:
                    term = jnp.where(key_place <= query_place, term, 0.0)
                if valid[tile + block] is not None:
                    term = term * valid[tile + block]
                terms[low : low + TILE] = term
                total = total + jnp.sum(term, axis=0, keepdims=True)
            inverse = 1.0 / total
            for block in range(5):
                low = block * TILE
                weights[low : low + TILE] = (terms[low : low + TILE] * inverse).astype(BF)
            mixed = dot(values_turned[:, span], weights[...])
            rounded = mixed.astype(BF).astype(F32)
            attended[here, columns] = mixed.T.astype(BF)
            delta = jnp.sum(out.astype(F32).T * rounded, axis=0, keepdims=True)
            for block in range(5):
                low = block * TILE
                prob_grads = dot(values[tile * TILE + low : tile * TILE + low + TILE], out, 1, 1)
                probs = terms[low : low + TILE] * inverse
                score_grads[head, tile, low : low + TILE] = (probs * (prob_grads - delta)).astype(BF)
            key_sums[span] += dot(score_grads[head, tile], query)
            value_sums[span] += dot(weights[...], out)
    for part, ref in enumerate((grads2, grads1, grads0)):
        rows = slice(part * ROWS, (part + 1) * ROWS)
        ref[0] = (key_sums[rows] * SCORE_SCALE).astype(ref.dtype)
        ref[1] = value_sums[rows].astype(ref.dtype)


def attend(pos, queries, near0, near1, near2, cotangent):
    pair = (2, ROWS, HEAD_WIDTH)
    return pl.pallas_call(
        attend_body,
        in_specs=[SMEM] + [VMEM] * 5,
        out_specs=[VMEM] * 5,
        out_shape=[
            jax.ShapeDtypeStruct((ROWS, 2 * HEAD_WIDTH), BF),
            jax.ShapeDtypeStruct(pair, F32),
            jax.ShapeDtypeStruct(pair, BF),
            jax.ShapeDtypeStruct(pair, BF),
            jax.ShapeDtypeStruct((2, 2, SPAN, TILE), BF),
        ],
        scratch_shapes=[
            pltpu.VMEM((BAND, HEAD_WIDTH), BF),
            pltpu.VMEM((BAND, HEAD_WIDTH), BF),
            pltpu.VMEM((HEAD_WIDTH, BAND), BF),
            pltpu.VMEM((SPAN, TILE), F32),
            pltpu.VMEM((SPAN, TILE), BF),
            pltpu.VMEM((BAND, HEAD_WIDTH), F32),
            pltpu.VMEM((BAND, HEAD_WIDTH), F32),
        ],
        compiler_params=params(),
        cost_estimate=cost(8_000_000_000, 8_000_000),
    )(pos, queries, near0, near1, near2, cotangent)


def query_back_body(
    score_grads, near0, near1, near2, raw, gain, cosine, sine, back, keys_turned
):
    for part, ref in enumerate((near2, near1, near0)):
        keys_turned[:, part * ROWS : (part + 1) * ROWS] = ref[0].astype(F32).T.astype(BF)
    for head in range(2):
        for tile in range(2):
            here = slice(tile * TILE, (tile + 1) * TILE)
            grads = dot(keys_turned[:, tile * TILE : tile * TILE + SPAN], score_grads[head, tile])
            grads = (grads * SCORE_SCALE).T
            back[head, here] = rotate_back(
                raw[head, here], grads, gain[...], cosine[here], sine[here]
            )


def query_back(score_grads, near0, near1, near2, raw, gain, cosine, sine):
    return pl.pallas_call(
        query_back_body,
        in_specs=[VMEM] * 8,
        out_specs=VMEM,
        out_shape=jax.ShapeDtypeStruct((2, ROWS, HEAD_WIDTH), F32),
        scratch_shapes=[pltpu.VMEM((HEAD_WIDTH, BAND), BF)],
        compiler_params=params(),
        cost_estimate=cost(1_000_000_000, 4_000_000),
    )(score_grads, near0, near1, near2, raw, gain, cosine, sine)


def all_back_body(
    pos, own, from1, from2, raw, gain, cosine, sine, query_part, kept, sent, turned
):
    core = pos[2]
    grads = own[...] + from1[...].astype(F32) + from2[...].astype(F32)
    key_part = rotate_back(raw[...], grads[0], gain[...], cosine[...], sine[...])
    mine, other = by_core(core, key_part, grads[1])
    kept[:, :HEAD_WIDTH] = mine.astype(BF)
    sent[:, :HEAD_WIDTH] = other.astype(BF)
    turned[:HEAD_WIDTH] = mine.T.astype(BF)
    turned[WIDE : WIDE + HEAD_WIDTH] = other.T.astype(BF)
    mine, other = by_core(core, query_part[0], query_part[1])
    kept[:, HEAD_WIDTH:] = mine.astype(BF)
    sent[:, HEAD_WIDTH:] = other.astype(BF)
    turned[HEAD_WIDTH:WIDE] = mine.T.astype(BF)
    turned[WIDE + HEAD_WIDTH :] = other.T.astype(BF)


def all_back(pos, own, from1, from2, raw, gain, cosine, sine, query_part):
    return pl.pallas_call(
        all_back_body,
        in_specs=[SMEM] + [VMEM] * 8,
        out_specs=[VMEM] * 3,
        out_shape=[
            jax.ShapeDtypeStruct((ROWS, WIDE), BF),
            jax.ShapeDtypeStruct((ROWS, WIDE), BF),
            jax.ShapeDtypeStruct((2 * WIDE, ROWS), BF),
        ],
        compiler_params=params(),
        cost_estimate=cost(10_000_000, 3_000_000),
    )(pos, own, from1, from2, raw, gain, cosine, sine, query_part)


GROUPS = ((4,), (3, 5), (2, 6), (1, 7), (0,))


def weight_terms_body(pos, tokens, other_tokens, back, other_back, mine, *refs):
    groups, terms = refs[:-1], refs[-1]
    step = pl.program_id(0)
    z, y = pos[0], pos[1]
    rows = pl.ds(pl.multiple_of(step * (DEPTH // 2), DEPTH // 2), DEPTH // 2)
    terms[rows, :] = (
        dot(tokens[...], back[...], 0, 0) + dot(other_tokens[...], other_back[...], 0, 0)
    ).astype(BF)

    @pl.when(step == 1)
    def spread():
        for number, group in enumerate(GROUPS):
            for slot, z_offset in enumerate(group):
                start = lax.rem(z + z_offset, 8) * PART
                same = pl.ds(pl.multiple_of(start + y * BLOCK, 16), BLOCK)
                other = pl.ds(pl.multiple_of(start + (1 - y) * BLOCK, 16), BLOCK)
                mine[z_offset] = terms[same, :]
                groups[number][slot] = terms[other, :]


def weight_terms(pos, tokens, other_tokens, back, other_back):
    whole = lambda shape: pl.BlockSpec(shape, lambda k: (0,) * len(shape))
    shapes = [(8, BLOCK, WIDE)] + [(len(group), BLOCK, WIDE) for group in GROUPS]
    return pl.pallas_call(
        weight_terms_body,
        grid=(2,),
        in_specs=[
            SMEM,
            pl.BlockSpec((ROWS, DEPTH // 2), lambda k: (0, k)),
            pl.BlockSpec((ROWS, DEPTH // 2), lambda k: (0, k)),
            whole((ROWS, WIDE)),
            whole((ROWS, WIDE)),
        ],
        out_specs=[whole(shape) for shape in shapes],
        out_shape=[jax.ShapeDtypeStruct(shape, BF) for shape in shapes],
        scratch_shapes=[pltpu.VMEM((DEPTH, WIDE), BF)],
        compiler_params=params(),
        cost_estimate=cost(4 * ROWS * DEPTH * 256, 17_000_000),
    )(pos, tokens, other_tokens, back, other_back)


def token_terms_body(count, split, order, *refs):
    turned = refs[count]
    outs = refs[count + 1 :]
    half = ROWS // 2
    for number in range(count):
        part = dot(refs[number][...], turned[...]).astype(BF)
        if split:
            outs[2 * number][...] = part[:, :half]
            outs[2 * number + 1][...] = part[:, half:]
        else:
            outs[number][...] = part


def token_terms(owners, weights, turned, split):
    count = owners.shape[0]
    width = ROWS // 2 if split else ROWS
    number_out = 2 * count if split else count

    def window(number):
        return pl.BlockSpec((PART, 2 * WIDE), lambda k, order: (order[number], 0))

    return pl.pallas_call(
        functools.partial(token_terms_body, count, split),
        grid_spec=pltpu.PrefetchScalarGridSpec(
            num_scalar_prefetch=1,
            grid=(1,),
            in_specs=[window(number) for number in range(count)]
            + [pl.BlockSpec((2 * WIDE, ROWS), lambda k, order: (0, 0))],
            out_specs=[pl.BlockSpec((PART, width), lambda k, order: (0, 0))] * number_out,
        ),
        out_shape=[jax.ShapeDtypeStruct((PART, width), BF)] * number_out,
        compiler_params=params(),
        cost_estimate=cost(2 * PART * ROWS * 512 * count, 1_500_000 * count),
    )(owners, *[weights] * count, turned)


def combine(body, arrays, shapes, after=()):
    count = len(arrays)

    def run(*refs):
        body(refs[:count], refs[count + len(after) :])

    return pl.pallas_call(
        run,
        in_specs=[VMEM] * count + [ANY] * len(after),
        out_specs=[VMEM] * len(shapes),
        out_shape=[jax.ShapeDtypeStruct(shape, BF) for shape in shapes],
        compiler_params=params(),
        cost_estimate=cost(1_000_000, 2_000_000),
    )(*arrays, *after)


def wide(ref):
    return ref[...].astype(F32)


def chip_shard(halves, core):
    kept = jnp.where(core == 0, halves[0], halves[1])
    came = swap_core(jnp.where(core == 0, halves[1], halves[0]))
    return jnp.concatenate(
        [jnp.where(core == 0, kept, came), jnp.where(core == 0, came, kept)], axis=0
    )


def gather(shard):
    entries = []

    def arrived(piece, z_offset, column):
        other = swap_y(piece)
        for array, y_offset in ((piece, 0), (other, 1)):
            entries.append((array, z_offset, y_offset, column))
            entries.append((swap_core(array), z_offset, y_offset, column + WIDE))

    arrived(shard, 0, 0)
    up, down = shard, shard
    for hop in range(1, 4):
        up, down = up_z(up), down_z(down)
        arrived(up, 8 - hop, 0)
        arrived(down, hop, 0)
    arrived(up_z(up[:, :HEAD_WIDTH]), 4, 0)
    arrived(down_z(down[:, HEAD_WIDTH:]), 4, HEAD_WIDTH)
    return entries


def shards(tokens, query_weight, key_matrix, value_matrix, query_gain, key_norm_gain, cotangent):
    ctx = lax.axis_index("ctx")
    tp = lax.axis_index("tp")
    z, y, core = ctx // 4, (ctx // 2) % 2, ctx % 2
    pos = jnp.stack([z, y, core, ctx]).astype(jnp.int32)
    token_positions = (ctx * ROWS + jnp.arange(ROWS, dtype=jnp.int32)).astype(F32)
    inverse = jnp.power(
        F32(rope_base), -jnp.arange(0, HEAD_WIDTH, 2).astype(F32) / HEAD_WIDTH
    )
    angles = token_positions[:, None] * inverse[None, :]
    cosine, sine = jnp.cos(angles), jnp.sin(angles)
    cosine = jnp.concatenate([cosine, cosine], axis=1)
    sine = jnp.concatenate([-sine, sine], axis=1)
    query_gain = query_gain.reshape(1, HEAD_WIDTH)
    key_gain = key_norm_gain.reshape(1, HEAD_WIDTH)

    shard = chip_shard(
        [
            jnp.concatenate([key_matrix, query_weight[:, :HEAD_WIDTH]], axis=1),
            jnp.concatenate([value_matrix, query_weight[:, HEAD_WIDTH:]], axis=1),
        ],
        core,
    )
    entries = gather(shard)
    other_tokens = swap_core(tokens)
    pair_raw, query_raw, near0, queries, weights = project(
        pos, tokens, key_gain, query_gain, cosine, sine, entries
    )
    near1, near2 = passed_along(near0, 1), passed_along(near0, 2)
    attended, grads0, grads1, grads2, score_grads = attend(
        pos, queries, near0, near1, near2, cotangent
    )
    from2, from1 = passed_along(grads2, -2), passed_along(grads1, -1)
    query_part = query_back(
        score_grads, near0, near1, near2, query_raw, query_gain, cosine, sine
    )
    kept, sent, turned = all_back(
        pos, grads0, from1, from2, pair_raw, key_gain, cosine, sine, query_part
    )
    other_back = swap_core(sent)

    def owners(*offsets):
        return jnp.stack(
            [(tp // 2 + i) % X_SIZE * 2 + (tp % 2 + j) % 2 for i, j in offsets]
        ).astype(jnp.int32)

    far1a, far1b, far0a, far0b = token_terms(owners((2, 1), (2, 0)), weights, turned, True)
    up1, down1 = up_x(far1a), down_x(far1b)
    up0, down0 = up_x(far0a), down_x(far0b)
    mine, *groups = weight_terms(pos, tokens, other_tokens, kept, other_back)
    near4, near35, near26, near17, near0y = [swap_y(group) for group in groups]
    right1, left1, right0, left0, mine1, mine0 = token_terms(
        owners((1, 1), (3, 1), (1, 0), (3, 0), (0, 1), (0, 0)), weights, turned, False
    )
    half = ROWS // 2
    token_shape = (PART, ROWS)

    def join(ins, outs):
        upward, downward, up, down = ins
        outs[0][:, :half] = (wide(upward)[:, :half] + wide(up)).astype(BF)
        outs[0][:, half:] = upward[:, half:]
        outs[1][:, :half] = downward[:, :half]
        outs[1][:, half:] = (wide(downward)[:, half:] + wide(down)).astype(BF)

    def first_step(ins, outs):
        own, came = ins
        total = own[4].astype(F32) + came[0].astype(F32)
        outs[0][...] = total[:, :HEAD_WIDTH].astype(BF)
        outs[1][...] = total[:, HEAD_WIDTH:].astype(BF)

    def second_step(ins, outs):
        own, came, up, down = ins
        upper = own[3].astype(F32) + came[0].astype(F32)
        lower = own[5].astype(F32) + came[1].astype(F32)
        outs[0][:, :HEAD_WIDTH] = (upper[:, :HEAD_WIDTH] + wide(up)).astype(BF)
        outs[0][:, HEAD_WIDTH:] = upper[:, HEAD_WIDTH:].astype(BF)
        outs[1][:, :HEAD_WIDTH] = lower[:, :HEAD_WIDTH].astype(BF)
        outs[1][:, HEAD_WIDTH:] = (lower[:, HEAD_WIDTH:] + wide(down)).astype(BF)

    def later_step(hop):
        def body(ins, outs):
            own, came, up, down = ins
            outs[0][...] = (own[hop].astype(F32) + came[0].astype(F32) + wide(up)).astype(BF)
            outs[1][...] = (own[8 - hop].astype(F32) + came[1].astype(F32) + wide(down)).astype(BF)

        return body

    def last_step(ins, outs):
        own, came, up, down = ins
        outs[0][...] = (own[0].astype(F32) + came[0].astype(F32) + wide(up) + wide(down)).astype(BF)

    def total3(ins, outs):
        outs[0][...] = (wide(ins[0]) + wide(ins[1]) + wide(ins[2])).astype(BF)

    narrow, block = (BLOCK, HEAD_WIDTH), (BLOCK, WIDE)
    z1 = combine(first_step, (mine, near4), [narrow] * 2, (right1,))
    up, down = up_z(z1[0]), down_z(z1[1])
    x1 = combine(join, (right1, left1, up1, down1), [token_shape] * 2, (z1[0],))
    got_up1, got_down1 = up_x(x1[0]), down_x(x1[1])
    z2 = combine(second_step, (mine, near35, up, down), [block] * 2, (x1[0],))
    up, down = up_z(z2[0]), down_z(z2[1])
    x2 = combine(join, (right0, left0, up0, down0), [token_shape] * 2, (z2[0],))
    got_up0, got_down0 = up_x(x2[0]), down_x(x2[1])
    z3 = combine(later_step(2), (mine, near26, up, down), [block] * 2, (x2[0],))
    up, down = up_z(z3[0]), down_z(z3[1])
    z4 = combine(later_step(1), (mine, near17, up, down), [block] * 2, (z3[0],))
    up, down = up_z(z4[0]), down_z(z4[1])
    (x3,) = combine(total3, (mine1, got_up1, got_down1), [token_shape], (z4[0],))
    far = swap_far(x3)
    (chip_sum,) = combine(last_step, (mine, near0y, up, down), [block], (x3,))
    token_gradient = summed(mine0, got_up0, got_down0, far).T

    rows = chip_sum.reshape(2, BLOCK // 2, WIDE)
    kept_rows = jnp.where(core == 0, rows[0], rows[1])
    came_rows = swap_core(jnp.where(core == 0, rows[1], rows[0]))
    first = jnp.where(core == 0, kept_rows, came_rows)
    second = jnp.where(core == 0, came_rows, kept_rows)
    return (
        attended,
        token_gradient,
        jnp.concatenate([first[:, HEAD_WIDTH:], second[:, HEAD_WIDTH:]], axis=1),
        first[:, :HEAD_WIDTH],
        second[:, :HEAD_WIDTH],
    )


def solution(mesh):
    in_specs = (
        P("ctx", None),
        P("ctx", "tp"),
        P("ctx", "tp"),
        P("ctx", "tp"),
        P(),
        P(),
        P("ctx", "tp"),
    )
    out_specs = (P("ctx", "tp"), P("ctx", "tp"), P("ctx", "tp"), P("ctx", "tp"), P("ctx", "tp"))
    return jax.shard_map(shards, mesh=mesh, in_specs=in_specs, out_specs=out_specs, check_vma=False)
```

```python
import functools

import jax
import jax.numpy as jnp
from jax import lax
from jax.experimental import pallas as pl
from jax.experimental.pallas import tpu as pltpu
from jax.sharding import PartitionSpec as P

HEAD_WIDTH = 128
WINDOW_LENGTH = 1024
QUERY_SCALAR = 168
SCORE_SCALE = QUERY_SCALAR ** (-0.5)

rope_base = 10000.0
norm_eps = 1e-06

Z_SIZE = 8
X_SIZE = 4
ROWS = 512
TILE = 256
SPAN = WINDOW_LENGTH + TILE
BAND = WINDOW_LENGTH + ROWS
DEPTH = 5376
BLOCK = 336
PART = 672
BF = jnp.bfloat16
F32 = jnp.float32


def along_z(step):
    return [(i, ((i // 4 + step) % Z_SIZE) * 4 + i % 4) for i in range(4 * Z_SIZE)]


def along_x(step):
    return [(i, ((i // 2 + step) % X_SIZE) * 2 + i % 2) for i in range(2 * X_SIZE)]


SIBLING = [(i, i ^ 1) for i in range(32)]
NEAR_Y = [(i, i ^ 2) for i in range(32)]
FAR_Y = [(i, i ^ 1) for i in range(8)]


def up_z(piece):
    return lax.ppermute(piece, "ctx", along_z(1))


def down_z(piece):
    return lax.ppermute(piece, "ctx", along_z(-1))


def swap_y(piece):
    return lax.ppermute(piece, "ctx", NEAR_Y)


def swap_core(piece):
    return lax.ppermute(piece, "ctx", SIBLING)


def up_x(piece):
    return lax.ppermute(piece, "tp", along_x(1))


def down_x(piece):
    return lax.ppermute(piece, "tp", along_x(-1))


def swap_far(piece):
    return lax.ppermute(piece, "tp", FAR_Y)


def passed_along(shard, by):
    pairs = [(i, i + by) for i in range(32) if 0 <= i + by < 32]
    return lax.ppermute(shard, "ctx", pairs)


def summed(*terms):
    total = terms[0].astype(F32)
    for term in terms[1:]:
        total = total + term.astype(F32)
    return total.astype(BF)


def dot(left, right, left_axis=1, right_axis=0):
    return lax.dot_general(
        left, right, (((left_axis,), (right_axis,)), ((), ())), preferred_element_type=F32
    )


def params(mebibytes=50):
    return pltpu.CompilerParams(vmem_limit_bytes=mebibytes * 1024 * 1024)


def cost(flops, moved):
    return pl.CostEstimate(flops=flops, bytes_accessed=moved, transcendentals=0)


VMEM = pl.BlockSpec(memory_space=pltpu.VMEM)
ANY = pl.BlockSpec(memory_space=pl.ANY)
SMEM = pl.BlockSpec(memory_space=pltpu.SMEM)


def rotate(raw, gain, cosine, sine):
    scale = lax.rsqrt(jnp.mean(raw * raw, axis=-1, keepdims=True) + norm_eps)
    normed = raw * scale * gain
    return normed * cosine + pltpu.roll(normed, HEAD_WIDTH // 2, 1) * sine


def rotate_back(raw, grads, gain, cosine, sine):
    scale = lax.rsqrt(jnp.mean(raw * raw, axis=-1, keepdims=True) + norm_eps)
    turned = (grads * cosine - pltpu.roll(grads, HEAD_WIDTH // 2, 1) * sine) * gain
    inner = jnp.mean(raw * turned, axis=-1, keepdims=True)
    return turned * scale - raw * (scale * scale * scale * inner)


DEPTH_STEPS = 3
DEPTH_STEP = DEPTH // DEPTH_STEPS
WIDE = 2 * HEAD_WIDTH


def by_core(core, first, second):
    return jnp.where(core == 0, first, second), jnp.where(core == 0, second, first)


def project_body(places, pos, tokens, other_tokens, *refs):
    count = len(places)
    pieces = refs[:count]
    own, sent, kept, weights, sems, out_sem = refs[count:]
    step = pl.program_id(0)
    z, y = pos[0], pos[1]

    @pl.when(step == 0)
    def place():
        copies = []
        for number, (z_offset, y_offset, column, width) in enumerate(places):
            block = lax.rem(z + z_offset, 8) * 2 + lax.rem(y + y_offset, 2)
            start = pl.multiple_of(block * BLOCK, 16)
            copies.append(
                pltpu.make_async_copy(
                    pieces[number],
                    weights.at[pl.ds(start, BLOCK), pl.ds(column, width)],
                    sems.at[number],
                )
            )
        for copy in copies:
            copy.start()
        for copy in copies:
            copy.wait()
        pltpu.make_async_copy(weights, kept, out_sem).start()
        own[...] = jnp.zeros_like(own)
        sent[...] = jnp.zeros_like(sent)

    start = pl.multiple_of(step * DEPTH_STEP, DEPTH_STEP)
    block = weights[pl.ds(start, DEPTH_STEP), :]
    own[...] += dot(tokens[...], block)
    sent[...] += dot(other_tokens[...], block)

    @pl.when(step == DEPTH_STEPS - 1)
    def finish():
        pltpu.make_async_copy(weights, kept, out_sem).wait()


def project(pos, tokens, other_tokens, entries):
    places = tuple((e[1], e[2], e[3], e[0].shape[1]) for e in entries)
    whole = lambda shape: pl.BlockSpec(shape, lambda k: (0,) * len(shape))
    return pl.pallas_call(
        functools.partial(project_body, places),
        grid=(DEPTH_STEPS,),
        in_specs=[SMEM] + [pl.BlockSpec((ROWS, DEPTH_STEP), lambda k: (0, k))] * 2 + [ANY] * len(entries),
        out_specs=[whole((ROWS, WIDE)), whole((ROWS, WIDE)), ANY],
        out_shape=[
            jax.ShapeDtypeStruct((ROWS, WIDE), F32),
            jax.ShapeDtypeStruct((ROWS, WIDE), F32),
            jax.ShapeDtypeStruct((DEPTH, WIDE), BF),
        ],
        scratch_shapes=[
            pltpu.VMEM((DEPTH, WIDE), BF),
            pltpu.SemaphoreType.DMA((len(entries),)),
            pltpu.SemaphoreType.DMA,
        ],
        compiler_params=params(),
        cost_estimate=cost(2 * ROWS * DEPTH * 512, 17_000_000),
    )(pos, tokens, other_tokens, *[e[0] for e in entries])


def rotate_all_body(
    pos, own, came, key_gain, query_gain, cosine, sine, pair_raw, query_raw, pair_rows, query_rows
):
    core = pos[2]
    key, value = by_core(core, own[:, :HEAD_WIDTH], came[:, :HEAD_WIDTH])
    first, second = by_core(core, own[:, HEAD_WIDTH:], came[:, HEAD_WIDTH:])
    pair_raw[...] = key
    query_raw[0] = first
    query_raw[1] = second
    pair_rows[0] = rotate(key, key_gain[...], cosine[...], sine[...]).astype(BF)
    pair_rows[1] = value.astype(BF)
    query_rows[0] = rotate(first, query_gain[...], cosine[...], sine[...]).astype(BF)
    query_rows[1] = rotate(second, query_gain[...], cosine[...], sine[...]).astype(BF)


def rotate_all(pos, own, came, key_gain, query_gain, cosine, sine):
    pair = (2, ROWS, HEAD_WIDTH)
    return pl.pallas_call(
        rotate_all_body,
        in_specs=[SMEM] + [VMEM] * 6,
        out_specs=[VMEM] * 4,
        out_shape=[
            jax.ShapeDtypeStruct((ROWS, HEAD_WIDTH), F32),
            jax.ShapeDtypeStruct(pair, F32),
            jax.ShapeDtypeStruct(pair, BF),
            jax.ShapeDtypeStruct(pair, BF),
        ],
        compiler_params=params(),
        cost_estimate=cost(10_000_000, 3_000_000),
    )(pos, own, came, key_gain, query_gain, cosine, sine)


def load_band(nears, number, band, sems):
    copies = []
    for part, near in enumerate(nears):
        copy = pltpu.make_async_copy(
            near.at[number], band.at[pl.ds(part * ROWS, ROWS), :], sems.at[number, part]
        )
        copy.start()
        copies.append(copy)
    return copies


def attend_body(
    pos, queries, near0, near1, near2, cotangent, attended, grads0, grads1, grads2, score_grads,
    keys, values, values_turned, terms, weights, key_sums, value_sums, sems,
):
    nears = (near2, near1, near0)
    copies = load_band(nears, 0, keys, sems) + load_band(nears, 1, values, sems)
    for copy in copies:
        copy.wait()
    for part in range(3):
        rows = slice(part * ROWS, (part + 1) * ROWS)
        values_turned[:, rows] = values[rows].astype(F32).T.astype(BF)
    key_sums[...] = jnp.zeros_like(key_sums)
    value_sums[...] = jnp.zeros_like(value_sums)
    valid2 = (pos[3] >= 2).astype(F32)
    valid1 = (pos[3] >= 1).astype(F32)
    valid = (valid2, valid2, valid1, valid1, None, None)
    key_place = lax.broadcasted_iota(jnp.int32, (TILE, TILE), 0)
    query_place = lax.broadcasted_iota(jnp.int32, (TILE, TILE), 1)
    for head in range(2):
        columns = slice(head * HEAD_WIDTH, (head + 1) * HEAD_WIDTH)
        for tile in range(2):
            here = slice(tile * TILE, (tile + 1) * TILE)
            span = slice(tile * TILE, tile * TILE + SPAN)
            query = queries[head, here]
            out = cotangent[here, columns]
            total = jnp.zeros((1, TILE), F32)
            for block in range(5):
                low = block * TILE
                scores = dot(keys[tile * TILE + low : tile * TILE + low + TILE], query, 1, 1)
                term = jnp.exp(scores * SCORE_SCALE)
                if block == 0:
                    term = jnp.where(key_place > query_place, term, 0.0)
                if block == 4:
                    term = jnp.where(key_place <= query_place, term, 0.0)
                if valid[tile + block] is not None:
                    term = term * valid[tile + block]
                terms[low : low + TILE] = term
                total = total + jnp.sum(term, axis=0, keepdims=True)
            inverse = 1.0 / total
            for block in range(5):
                low = block * TILE
                weights[low : low + TILE] = (terms[low : low + TILE] * inverse).astype(BF)
            mixed = dot(values_turned[:, span], weights[...])
            rounded = mixed.astype(BF).astype(F32)
            attended[here, columns] = mixed.T.astype(BF)
            delta = jnp.sum(out.astype(F32).T * rounded, axis=0, keepdims=True)
            for block in range(5):
                low = block * TILE
                prob_grads = dot(values[tile * TILE + low : tile * TILE + low + TILE], out, 1, 1)
                probs = terms[low : low + TILE] * inverse
                score_grads[head, tile, low : low + TILE] = (probs * (prob_grads - delta)).astype(BF)
            key_sums[span] += dot(score_grads[head, tile], query)
            value_sums[span] += dot(weights[...], out)
    for part, ref in enumerate((grads2, grads1, grads0)):
        rows = slice(part * ROWS, (part + 1) * ROWS)
        ref[0] = (key_sums[rows] * SCORE_SCALE).astype(ref.dtype)
        ref[1] = value_sums[rows].astype(ref.dtype)


def attend(pos, queries, near0, near1, near2, cotangent):
    pair = (2, ROWS, HEAD_WIDTH)
    return pl.pallas_call(
        attend_body,
        in_specs=[SMEM, VMEM] + [ANY] * 3 + [VMEM],
        out_specs=[VMEM] * 5,
        out_shape=[
            jax.ShapeDtypeStruct((ROWS, 2 * HEAD_WIDTH), BF),
            jax.ShapeDtypeStruct(pair, F32),
            jax.ShapeDtypeStruct(pair, BF),
            jax.ShapeDtypeStruct(pair, BF),
            jax.ShapeDtypeStruct((2, 2, SPAN, TILE), BF),
        ],
        scratch_shapes=[
            pltpu.VMEM((BAND, HEAD_WIDTH), BF),
            pltpu.VMEM((BAND, HEAD_WIDTH), BF),
            pltpu.VMEM((HEAD_WIDTH, BAND), BF),
            pltpu.VMEM((SPAN, TILE), F32),
            pltpu.VMEM((SPAN, TILE), BF),
            pltpu.VMEM((BAND, HEAD_WIDTH), F32),
            pltpu.VMEM((BAND, HEAD_WIDTH), F32),
            pltpu.SemaphoreType.DMA((2, 3)),
        ],
        compiler_params=params(),
        cost_estimate=cost(8_000_000_000, 8_000_000),
    )(pos, queries, near0, near1, near2, cotangent)


def query_back_body(
    score_grads, near0, near1, near2, raw, gain, cosine, sine, back, keys, keys_turned, sems
):
    for copy in load_band((near2, near1, near0), 0, keys, sems):
        copy.wait()
    for part in range(3):
        rows = slice(part * ROWS, (part + 1) * ROWS)
        keys_turned[:, rows] = keys[rows].astype(F32).T.astype(BF)
    for head in range(2):
        for tile in range(2):
            here = slice(tile * TILE, (tile + 1) * TILE)
            grads = dot(keys_turned[:, tile * TILE : tile * TILE + SPAN], score_grads[head, tile])
            grads = (grads * SCORE_SCALE).T
            back[head, here] = rotate_back(
                raw[head, here], grads, gain[...], cosine[here], sine[here]
            )


def query_back(score_grads, near0, near1, near2, raw, gain, cosine, sine):
    return pl.pallas_call(
        query_back_body,
        in_specs=[VMEM] + [ANY] * 3 + [VMEM] * 4,
        out_specs=VMEM,
        out_shape=jax.ShapeDtypeStruct((2, ROWS, HEAD_WIDTH), F32),
        scratch_shapes=[
            pltpu.VMEM((BAND, HEAD_WIDTH), BF),
            pltpu.VMEM((HEAD_WIDTH, BAND), BF),
            pltpu.SemaphoreType.DMA((1, 3)),
        ],
        compiler_params=params(),
        cost_estimate=cost(1_000_000_000, 4_000_000),
    )(score_grads, near0, near1, near2, raw, gain, cosine, sine)


def all_back_body(
    pos, own, from1, from2, raw, gain, cosine, sine, query_part, kept, sent, turned
):
    core = pos[2]
    grads = own[...] + from1[...].astype(F32) + from2[...].astype(F32)
    key_part = rotate_back(raw[...], grads[0], gain[...], cosine[...], sine[...])
    mine, other = by_core(core, key_part, grads[1])
    kept[:, :HEAD_WIDTH] = mine.astype(BF)
    sent[:, :HEAD_WIDTH] = other.astype(BF)
    turned[:HEAD_WIDTH] = mine.T.astype(BF)
    turned[WIDE : WIDE + HEAD_WIDTH] = other.T.astype(BF)
    mine, other = by_core(core, query_part[0], query_part[1])
    kept[:, HEAD_WIDTH:] = mine.astype(BF)
    sent[:, HEAD_WIDTH:] = other.astype(BF)
    turned[HEAD_WIDTH:WIDE] = mine.T.astype(BF)
    turned[WIDE + HEAD_WIDTH :] = other.T.astype(BF)


def all_back(pos, own, from1, from2, raw, gain, cosine, sine, query_part):
    return pl.pallas_call(
        all_back_body,
        in_specs=[SMEM] + [VMEM] * 8,
        out_specs=[VMEM] * 3,
        out_shape=[
            jax.ShapeDtypeStruct((ROWS, WIDE), BF),
            jax.ShapeDtypeStruct((ROWS, WIDE), BF),
            jax.ShapeDtypeStruct((2 * WIDE, ROWS), BF),
        ],
        compiler_params=params(),
        cost_estimate=cost(10_000_000, 3_000_000),
    )(pos, own, from1, from2, raw, gain, cosine, sine, query_part)


def weight_terms_body(pos, tokens, other_tokens, back, other_back, mine, far_up, far_down, terms):
    step = pl.program_id(0)
    z, y = pos[0], pos[1]
    rows = pl.ds(pl.multiple_of(step * (DEPTH // 2), DEPTH // 2), DEPTH // 2)
    terms[rows, :] = (
        dot(tokens[...], back[...], 0, 0) + dot(other_tokens[...], other_back[...], 0, 0)
    ).astype(BF)

    @pl.when(step == 1)
    def spread():
        for z_offset in range(8):
            start = lax.rem(z + z_offset, 8) * PART
            same = pl.ds(pl.multiple_of(start + y * BLOCK, 16), BLOCK)
            other = pl.ds(pl.multiple_of(start + (1 - y) * BLOCK, 16), BLOCK)
            if z_offset == 4:
                far_up[...] = terms[same, :]
                far_down[...] = terms[other, :]
            else:
                mine[z_offset, 0] = terms[same, :]
                mine[z_offset, 1] = terms[other, :]


def weight_terms(pos, tokens, other_tokens, back, other_back):
    whole = lambda shape: pl.BlockSpec(shape, lambda k: (0,) * len(shape))
    shapes = [(8, 2, BLOCK, WIDE), (BLOCK, WIDE), (BLOCK, WIDE)]
    return pl.pallas_call(
        weight_terms_body,
        grid=(2,),
        in_specs=[
            SMEM,
            pl.BlockSpec((ROWS, DEPTH // 2), lambda k: (0, k)),
            pl.BlockSpec((ROWS, DEPTH // 2), lambda k: (0, k)),
            whole((ROWS, WIDE)),
            whole((ROWS, WIDE)),
        ],
        out_specs=[whole(shape) for shape in shapes],
        out_shape=[jax.ShapeDtypeStruct(shape, BF) for shape in shapes],
        scratch_shapes=[pltpu.VMEM((DEPTH, WIDE), BF)],
        compiler_params=params(),
        cost_estimate=cost(4 * ROWS * DEPTH * 256, 17_000_000),
    )(pos, tokens, other_tokens, back, other_back)


def token_terms_body(count, split, order, *refs):
    turned = refs[2 * count]
    outs = refs[2 * count + 1 :]
    half = ROWS // 2
    for number in range(count):
        part = (
            dot(refs[number][...], turned[:WIDE]) + dot(refs[count + number][...], turned[WIDE:])
        ).astype(BF)
        if split:
            outs[0][number] = part[:, :half]
            outs[1][number] = part[:, half:]
        else:
            outs[number][...] = part


def token_terms(owners, weights, other_weights, turned, split):
    count = owners.shape[0]
    shapes = [(count, PART, ROWS // 2)] * 2 if split else [(PART, ROWS)] * count
    whole = lambda shape: pl.BlockSpec(shape, lambda k, order: (0,) * len(shape))

    def window(number):
        return pl.BlockSpec((PART, WIDE), lambda k, order: (order[number], 0))

    windows = [window(number) for number in range(count)]
    return pl.pallas_call(
        functools.partial(token_terms_body, count, split),
        grid_spec=pltpu.PrefetchScalarGridSpec(
            num_scalar_prefetch=1,
            grid=(1,),
            in_specs=windows + windows + [whole((2 * WIDE, ROWS))],
            out_specs=[whole(shape) for shape in shapes],
        ),
        out_shape=[jax.ShapeDtypeStruct(shape, BF) for shape in shapes],
        compiler_params=params(),
        cost_estimate=cost(2 * PART * ROWS * 512 * count, 1_500_000 * count),
    )(owners, *[weights] * count, *[other_weights] * count, turned)


def combine(body, arrays, shapes, after=()):
    count = len(arrays)

    def run(*refs):
        body(refs[:count], refs[count + len(after) :])

    return pl.pallas_call(
        run,
        in_specs=[VMEM] * count + [ANY] * len(after),
        out_specs=[VMEM] * len(shapes),
        out_shape=[jax.ShapeDtypeStruct(shape, BF) for shape in shapes],
        compiler_params=params(),
        cost_estimate=cost(1_000_000, 2_000_000),
    )(*arrays, *after)


def wide(ref):
    return ref[...].astype(F32)


def chip_shard(halves, core):
    kept = jnp.where(core == 0, halves[0], halves[1])
    came = swap_core(jnp.where(core == 0, halves[1], halves[0]))
    return jnp.concatenate(
        [jnp.where(core == 0, kept, came), jnp.where(core == 0, came, kept)], axis=0
    )


def gather(shard, tokens):
    tokens, shard = lax.optimization_barrier((tokens, shard))
    other_tokens = swap_core(tokens)
    entries = []

    def arrived(piece, z_offset, column):
        entries.append((piece, z_offset, 0, column))
        entries.append((swap_y(piece), z_offset, 1, column))

    arrived(shard, 0, 0)
    up, down = shard, shard
    for hop in range(1, 4):
        up, down = up_z(up), down_z(down)
        if hop == 2:
            up, down, other_tokens = lax.optimization_barrier((up, down, other_tokens))
        arrived(up, 8 - hop, 0)
        arrived(down, hop, 0)
    arrived(up_z(up[:, :HEAD_WIDTH]), 4, 0)
    arrived(down_z(down[:, HEAD_WIDTH:]), 4, HEAD_WIDTH)
    return entries, other_tokens


def shards(tokens, query_weight, key_matrix, value_matrix, query_gain, key_norm_gain, cotangent):
    ctx = lax.axis_index("ctx")
    tp = lax.axis_index("tp")
    z, y, core = ctx // 4, (ctx // 2) % 2, ctx % 2
    pos = jnp.stack([z, y, core, ctx]).astype(jnp.int32)
    token_positions = (ctx * ROWS + jnp.arange(ROWS, dtype=jnp.int32)).astype(F32)
    inverse = jnp.power(
        F32(rope_base), -jnp.arange(0, HEAD_WIDTH, 2).astype(F32) / HEAD_WIDTH
    )
    angles = token_positions[:, None] * inverse[None, :]
    cosine, sine = jnp.cos(angles), jnp.sin(angles)
    cosine = jnp.concatenate([cosine, cosine], axis=1)
    sine = jnp.concatenate([-sine, sine], axis=1)
    query_gain = query_gain.reshape(1, HEAD_WIDTH)
    key_gain = key_norm_gain.reshape(1, HEAD_WIDTH)

    shard = chip_shard(
        [
            jnp.concatenate([key_matrix, query_weight[:, :HEAD_WIDTH]], axis=1),
            jnp.concatenate([value_matrix, query_weight[:, HEAD_WIDTH:]], axis=1),
        ],
        core,
    )
    entries, other_tokens = gather(shard, tokens)
    own_raw, sent_raw, weights = project(pos, tokens, other_tokens, entries)
    came_raw, weights_later = lax.optimization_barrier((swap_core(sent_raw), weights))
    pair_raw, query_raw, near0, queries = rotate_all(
        pos, own_raw, came_raw, key_gain, query_gain, cosine, sine
    )
    other_weights = swap_core(weights_later)
    near1, near2 = passed_along(near0, 1), passed_along(near0, 2)
    attended, grads0, grads1, grads2, score_grads = attend(
        pos, queries, near0, near1, near2, cotangent
    )
    from2, from1 = passed_along(grads2, -2), passed_along(grads1, -1)
    query_part = query_back(
        score_grads, near0, near1, near2, query_raw, query_gain, cosine, sine
    )
    kept, sent, turned = all_back(
        pos, grads0, from1, from2, pair_raw, key_gain, cosine, sine, query_part
    )
    other_back = swap_core(sent)

    def owners(*offsets):
        return jnp.stack(
            [(tp // 2 + i) % X_SIZE * 2 + (tp % 2 + j) % 2 for i, j in offsets]
        ).astype(jnp.int32)

    far_a, far_b = token_terms(owners((2, 0), (2, 1)), weights, other_weights, turned, True)
    token_up, token_down = up_x(far_a), down_x(far_b)
    mine, far_up, far_down = weight_terms(pos, tokens, other_tokens, kept, other_back)
    up, down = up_z(far_up), down_z(far_down)
    right1, left1, right0, left0, mine1, mine0 = token_terms(
        owners((1, 1), (3, 1), (1, 0), (3, 0), (0, 1), (0, 0)), weights, other_weights, turned, False
    )
    half = ROWS // 2
    token_shape = (PART, ROWS)

    def join(ins, outs):
        second_step(ins[6:], outs[4:])
        came_up, came_down = ins[4:6]
        for number, far_offset in enumerate((1, 0)):
            upward, downward = ins[2 * number : 2 * number + 2]
            out_up, out_down = outs[2 * number : 2 * number + 2]
            out_up[:, :half] = (wide(upward)[:, :half] + came_up[far_offset].astype(F32)).astype(BF)
            out_up[:, half:] = upward[:, half:]
            out_down[:, :half] = downward[:, :half]
            out_down[:, half:] = (
                wide(downward)[:, half:] + came_down[far_offset].astype(F32)
            ).astype(BF)

    def second_step(ins, outs):
        own, up, down = ins
        outs[0][0] = (own[3, 0].astype(F32) + wide(up)).astype(BF)
        outs[0][1] = own[3, 1]
        outs[1][0] = own[5, 0]
        outs[1][1] = (own[5, 1].astype(F32) + wide(down)).astype(BF)

    def later_step(hop):
        def body(ins, outs):
            own, up, down = ins
            outs[0][...] = (own[hop].astype(F32) + wide(up)).astype(BF)
            outs[1][...] = (own[8 - hop].astype(F32) + wide(down)).astype(BF)

        return body

    def last_step(ins, outs):
        own, up, down = ins
        total = own[0].astype(F32) + wide(up) + wide(down)
        outs[0][...] = total[0].astype(BF)
        outs[1][...] = total[1].astype(BF)

    def total3(ins, outs):
        outs[0][...] = (wide(ins[0]) + wide(ins[1]) + wide(ins[2])).astype(BF)

    def total4(ins, outs):
        outs[0][...] = (wide(ins[0]) + wide(ins[1]) + wide(ins[2]) + wide(ins[3])).astype(BF)

    block, both = (BLOCK, WIDE), (2, BLOCK, WIDE)
    x1 = combine(
        join,
        (right1, left1, right0, left0, token_up, token_down, mine, up, down),
        [token_shape] * 4 + [both] * 2,
    )
    got_up1, got_down1 = up_x(x1[0]), down_x(x1[1])
    got_up0, got_down0 = up_x(x1[2]), down_x(x1[3])
    up, down = up_z(x1[4]), down_z(x1[5])
    z3 = combine(later_step(2), (mine, up, down), [both] * 2)
    up, down = up_z(z3[0]), down_z(z3[1])
    (x3,) = combine(total3, (mine1, got_up1, got_down1), [token_shape], (z3[0],))
    far = swap_far(x3)
    z4 = combine(later_step(1), (mine, up, down), [both] * 2, (x3,))
    up, down = up_z(z4[0]), down_z(z4[1])
    (x4,) = combine(total4, (mine0, got_up0, got_down0, far), [token_shape], (z4[0],))
    chip_kept, chip_sent = combine(last_step, (mine, up, down), [block] * 2, (x4,))
    chip_came = swap_y(chip_sent)
    token_gradient = x4.T

    rows = summed(chip_kept, chip_came).reshape(2, BLOCK // 2, WIDE)
    kept_rows = jnp.where(core == 0, rows[0], rows[1])
    came_rows = swap_core(jnp.where(core == 0, rows[1], rows[0]))
    first = jnp.where(core == 0, kept_rows, came_rows)
    second = jnp.where(core == 0, came_rows, kept_rows)
    return (
        attended,
        token_gradient,
        jnp.concatenate([first[:, HEAD_WIDTH:], second[:, HEAD_WIDTH:]], axis=1),
        first[:, :HEAD_WIDTH],
        second[:, :HEAD_WIDTH],
    )


def solution(mesh):
    in_specs = (
        P("ctx", None),
        P("ctx", "tp"),
        P("ctx", "tp"),
        P("ctx", "tp"),
        P(),
        P(),
        P("ctx", "tp"),
    )
    out_specs = (P("ctx", "tp"), P("ctx", "tp"), P("ctx", "tp"), P("ctx", "tp"), P("ctx", "tp"))
    return jax.shard_map(shards, mesh=mesh, in_specs=in_specs, out_specs=out_specs, check_vma=False)
```

```python
import functools

import jax
import jax.numpy as jnp
from jax import lax
from jax.experimental import pallas as pl
from jax.experimental.pallas import tpu as pltpu
from jax.sharding import PartitionSpec as P

HEAD_WIDTH = 128
WINDOW_LENGTH = 1024
QUERY_SCALAR = 168
SCORE_SCALE = QUERY_SCALAR ** (-0.5)

rope_base = 10000.0
norm_eps = 1e-06

Z_SIZE = 8
X_SIZE = 4
ROWS = 512
TILE = 256
SPAN = WINDOW_LENGTH + TILE
BAND = WINDOW_LENGTH + ROWS
DEPTH = 5376
VMEM_MEBIBYTES = 50
BLOCK = 336
PART = 672
BF = jnp.bfloat16
F32 = jnp.float32


def along_z(step):
    return [(i, ((i // 4 + step) % Z_SIZE) * 4 + i % 4) for i in range(4 * Z_SIZE)]


def along_x(step):
    return [(i, ((i // 2 + step) % X_SIZE) * 2 + i % 2) for i in range(2 * X_SIZE)]


SIBLING = [(i, i ^ 1) for i in range(32)]
NEAR_Y = [(i, i ^ 2) for i in range(32)]
FAR_Y = [(i, i ^ 1) for i in range(8)]


def up_z(piece):
    return lax.ppermute(piece, "ctx", along_z(1))


def down_z(piece):
    return lax.ppermute(piece, "ctx", along_z(-1))


def swap_y(piece):
    return lax.ppermute(piece, "ctx", NEAR_Y)


def swap_core(piece):
    return lax.ppermute(piece, "ctx", SIBLING)


def up_x(piece):
    return lax.ppermute(piece, "tp", along_x(1))


def down_x(piece):
    return lax.ppermute(piece, "tp", along_x(-1))


def swap_far(piece):
    return lax.ppermute(piece, "tp", FAR_Y)


def passed_along(shard, by):
    pairs = [(i, i + by) for i in range(32) if 0 <= i + by < 32]
    return lax.ppermute(shard, "ctx", pairs)


def summed(*terms):
    total = terms[0].astype(F32)
    for term in terms[1:]:
        total = total + term.astype(F32)
    return total.astype(BF)


def dot(left, right, left_axis=1, right_axis=0):
    return lax.dot_general(
        left, right, (((left_axis,), (right_axis,)), ((), ())), preferred_element_type=F32
    )


def params(mebibytes=VMEM_MEBIBYTES):
    return pltpu.CompilerParams(vmem_limit_bytes=mebibytes * 1024 * 1024)


def cost(flops, moved):
    return pl.CostEstimate(flops=flops, bytes_accessed=moved, transcendentals=0)


VMEM = pl.BlockSpec(memory_space=pltpu.VMEM)
ANY = pl.BlockSpec(memory_space=pl.ANY)
SMEM = pl.BlockSpec(memory_space=pltpu.SMEM)


def rotate(raw, gain, cosine, sine):
    scale = lax.rsqrt(jnp.mean(raw * raw, axis=-1, keepdims=True) + norm_eps)
    normed = raw * scale * gain
    return normed * cosine + pltpu.roll(normed, HEAD_WIDTH // 2, 1) * sine


def rotate_back(raw, grads, gain, cosine, sine):
    scale = lax.rsqrt(jnp.mean(raw * raw, axis=-1, keepdims=True) + norm_eps)
    turned = (grads * cosine - pltpu.roll(grads, HEAD_WIDTH // 2, 1) * sine) * gain
    inner = jnp.mean(raw * turned, axis=-1, keepdims=True)
    return turned * scale - raw * (scale * scale * scale * inner)


DEPTH_STEPS = 3
DEPTH_STEP = DEPTH // DEPTH_STEPS
WIDE = 2 * HEAD_WIDTH


def by_core(core, first, second):
    return jnp.where(core == 0, first, second), jnp.where(core == 0, second, first)


def project_body(places, pos, tokens, other_tokens, *refs):
    count = len(places)
    pieces = refs[:count]
    own, sent, kept, weights, sems, out_sem = refs[count:]
    step = pl.program_id(0)
    z, y = pos[0], pos[1]

    @pl.when(step == 0)
    def place():
        copies = []
        for number, (z_offset, y_offset, column, width) in enumerate(places):
            block = lax.rem(z + z_offset, 8) * 2 + lax.rem(y + y_offset, 2)
            start = pl.multiple_of(block * BLOCK, 16)
            copies.append(
                pltpu.make_async_copy(
                    pieces[number],
                    weights.at[pl.ds(start, BLOCK), pl.ds(column, width)],
                    sems.at[number],
                )
            )
        for copy in copies:
            copy.start()
        for copy in copies:
            copy.wait()
        pltpu.make_async_copy(weights, kept, out_sem).start()
        own[...] = jnp.zeros_like(own)
        sent[...] = jnp.zeros_like(sent)

    start = pl.multiple_of(step * DEPTH_STEP, DEPTH_STEP)
    block = weights[pl.ds(start, DEPTH_STEP), :]
    own[...] += dot(tokens[...], block)
    sent[...] += dot(other_tokens[...], block)

    @pl.when(step == DEPTH_STEPS - 1)
    def finish():
        pltpu.make_async_copy(weights, kept, out_sem).wait()


def project(pos, tokens, other_tokens, entries):
    places = tuple((e[1], e[2], e[3], e[0].shape[1]) for e in entries)
    whole = lambda shape: pl.BlockSpec(shape, lambda k: (0,) * len(shape))
    return pl.pallas_call(
        functools.partial(project_body, places),
        grid=(DEPTH_STEPS,),
        in_specs=[SMEM] + [pl.BlockSpec((ROWS, DEPTH_STEP), lambda k: (0, k))] * 2 + [ANY] * len(entries),
        out_specs=[whole((ROWS, WIDE)), whole((ROWS, WIDE)), ANY],
        out_shape=[
            jax.ShapeDtypeStruct((ROWS, WIDE), F32),
            jax.ShapeDtypeStruct((ROWS, WIDE), F32),
            jax.ShapeDtypeStruct((DEPTH, WIDE), BF),
        ],
        scratch_shapes=[
            pltpu.VMEM((DEPTH, WIDE), BF),
            pltpu.SemaphoreType.DMA((len(entries),)),
            pltpu.SemaphoreType.DMA,
        ],
        compiler_params=params(),
        cost_estimate=cost(2 * ROWS * DEPTH * 512, 17_000_000),
    )(pos, tokens, other_tokens, *[e[0] for e in entries])


def rotate_all_body(
    pos, own, came, key_gain, query_gain, cosine, sine, pair_raw, query_raw, pair_rows, query_rows
):
    core = pos[2]
    key, value = by_core(core, own[:, :HEAD_WIDTH], came[:, :HEAD_WIDTH])
    first, second = by_core(core, own[:, HEAD_WIDTH:], came[:, HEAD_WIDTH:])
    pair_raw[...] = key
    query_raw[0] = first
    query_raw[1] = second
    pair_rows[0] = rotate(key, key_gain[...], cosine[...], sine[...]).astype(BF)
    pair_rows[1] = value.astype(BF)
    query_rows[0] = rotate(first, query_gain[...], cosine[...], sine[...]).astype(BF)
    query_rows[1] = rotate(second, query_gain[...], cosine[...], sine[...]).astype(BF)


def rotate_all(pos, own, came, key_gain, query_gain, cosine, sine):
    pair = (2, ROWS, HEAD_WIDTH)
    return pl.pallas_call(
        rotate_all_body,
        in_specs=[SMEM] + [VMEM] * 6,
        out_specs=[VMEM] * 4,
        out_shape=[
            jax.ShapeDtypeStruct((ROWS, HEAD_WIDTH), F32),
            jax.ShapeDtypeStruct(pair, F32),
            jax.ShapeDtypeStruct(pair, BF),
            jax.ShapeDtypeStruct(pair, BF),
        ],
        compiler_params=params(),
        cost_estimate=cost(10_000_000, 3_000_000),
    )(pos, own, came, key_gain, query_gain, cosine, sine)


def load_band(nears, number, band, sems):
    copies = []
    for part, near in enumerate(nears):
        copy = pltpu.make_async_copy(
            near.at[number], band.at[pl.ds(part * ROWS, ROWS), :], sems.at[number, part]
        )
        copy.start()
        copies.append(copy)
    return copies


def attend_body(
    pos, queries, near0, near1, near2, cotangent, attended, grads0, grads1, grads2, score_grads,
    keys, values, values_turned, terms, weights, key_sums, value_sums, sems,
):
    nears = (near2, near1, near0)
    copies = load_band(nears, 0, keys, sems) + load_band(nears, 1, values, sems)
    for copy in copies:
        copy.wait()
    for part in range(3):
        rows = slice(part * ROWS, (part + 1) * ROWS)
        values_turned[:, rows] = values[rows].astype(F32).T.astype(BF)
    key_sums[...] = jnp.zeros_like(key_sums)
    value_sums[...] = jnp.zeros_like(value_sums)
    valid2 = (pos[3] >= 2).astype(F32)
    valid1 = (pos[3] >= 1).astype(F32)
    valid = (valid2, valid2, valid1, valid1, None, None)
    key_place = lax.broadcasted_iota(jnp.int32, (TILE, TILE), 0)
    query_place = lax.broadcasted_iota(jnp.int32, (TILE, TILE), 1)
    for head in range(2):
        columns = slice(head * HEAD_WIDTH, (head + 1) * HEAD_WIDTH)
        for tile in range(2):
            here = slice(tile * TILE, (tile + 1) * TILE)
            span = slice(tile * TILE, tile * TILE + SPAN)
            query = queries[head, here]
            out = cotangent[here, columns]
            total = jnp.zeros((1, TILE), F32)
            for block in range(5):
                low = block * TILE
                scores = dot(keys[tile * TILE + low : tile * TILE + low + TILE], query, 1, 1)
                term = jnp.exp(scores * SCORE_SCALE)
                if block == 0:
                    term = jnp.where(key_place > query_place, term, 0.0)
                if block == 4:
                    term = jnp.where(key_place <= query_place, term, 0.0)
                if valid[tile + block] is not None:
                    term = term * valid[tile + block]
                terms[low : low + TILE] = term
                total = total + jnp.sum(term, axis=0, keepdims=True)
            inverse = 1.0 / total
            for block in range(5):
                low = block * TILE
                weights[low : low + TILE] = (terms[low : low + TILE] * inverse).astype(BF)
            mixed = dot(values_turned[:, span], weights[...])
            rounded = mixed.astype(BF).astype(F32)
            attended[here, columns] = mixed.T.astype(BF)
            delta = jnp.sum(out.astype(F32).T * rounded, axis=0, keepdims=True)
            for block in range(5):
                low = block * TILE
                prob_grads = dot(values[tile * TILE + low : tile * TILE + low + TILE], out, 1, 1)
                probs = terms[low : low + TILE] * inverse
                score_grads[head, tile, low : low + TILE] = (probs * (prob_grads - delta)).astype(BF)
            key_sums[span] += dot(score_grads[head, tile], query)
            value_sums[span] += dot(weights[...], out)
    for part, ref in enumerate((grads2, grads1, grads0)):
        rows = slice(part * ROWS, (part + 1) * ROWS)
        ref[0] = (key_sums[rows] * SCORE_SCALE).astype(ref.dtype)
        ref[1] = value_sums[rows].astype(ref.dtype)


def attend(pos, queries, near0, near1, near2, cotangent):
    pair = (2, ROWS, HEAD_WIDTH)
    return pl.pallas_call(
        attend_body,
        in_specs=[SMEM, VMEM] + [ANY] * 3 + [VMEM],
        out_specs=[VMEM] * 5,
        out_shape=[
            jax.ShapeDtypeStruct((ROWS, 2 * HEAD_WIDTH), BF),
            jax.ShapeDtypeStruct(pair, F32),
            jax.ShapeDtypeStruct(pair, BF),
            jax.ShapeDtypeStruct(pair, BF),
            jax.ShapeDtypeStruct((2, 2, SPAN, TILE), BF),
        ],
        scratch_shapes=[
            pltpu.VMEM((BAND, HEAD_WIDTH), BF),
            pltpu.VMEM((BAND, HEAD_WIDTH), BF),
            pltpu.VMEM((HEAD_WIDTH, BAND), BF),
            pltpu.VMEM((SPAN, TILE), F32),
            pltpu.VMEM((SPAN, TILE), BF),
            pltpu.VMEM((BAND, HEAD_WIDTH), F32),
            pltpu.VMEM((BAND, HEAD_WIDTH), F32),
            pltpu.SemaphoreType.DMA((2, 3)),
        ],
        compiler_params=params(),
        cost_estimate=cost(8_000_000_000, 8_000_000),
    )(pos, queries, near0, near1, near2, cotangent)


def query_back_body(
    score_grads, near0, near1, near2, raw, gain, cosine, sine, back, keys, keys_turned, sems
):
    for copy in load_band((near2, near1, near0), 0, keys, sems):
        copy.wait()
    for part in range(3):
        rows = slice(part * ROWS, (part + 1) * ROWS)
        keys_turned[:, rows] = keys[rows].astype(F32).T.astype(BF)
    for head in range(2):
        for tile in range(2):
            here = slice(tile * TILE, (tile + 1) * TILE)
            grads = dot(keys_turned[:, tile * TILE : tile * TILE + SPAN], score_grads[head, tile])
            grads = (grads * SCORE_SCALE).T
            back[head, here] = rotate_back(
                raw[head, here], grads, gain[...], cosine[here], sine[here]
            )


def query_back(score_grads, near0, near1, near2, raw, gain, cosine, sine):
    return pl.pallas_call(
        query_back_body,
        in_specs=[VMEM] + [ANY] * 3 + [VMEM] * 4,
        out_specs=VMEM,
        out_shape=jax.ShapeDtypeStruct((2, ROWS, HEAD_WIDTH), F32),
        scratch_shapes=[
            pltpu.VMEM((BAND, HEAD_WIDTH), BF),
            pltpu.VMEM((HEAD_WIDTH, BAND), BF),
            pltpu.SemaphoreType.DMA((1, 3)),
        ],
        compiler_params=params(),
        cost_estimate=cost(1_000_000_000, 4_000_000),
    )(score_grads, near0, near1, near2, raw, gain, cosine, sine)


def all_back_body(
    pos, own, from1, from2, raw, gain, cosine, sine, query_part, kept, sent, turned
):
    core = pos[2]
    grads = own[...] + from1[...].astype(F32) + from2[...].astype(F32)
    key_part = rotate_back(raw[...], grads[0], gain[...], cosine[...], sine[...])
    mine, other = by_core(core, key_part, grads[1])
    kept[:, :HEAD_WIDTH] = mine.astype(BF)
    sent[:, :HEAD_WIDTH] = other.astype(BF)
    turned[:HEAD_WIDTH] = mine.T.astype(BF)
    turned[WIDE : WIDE + HEAD_WIDTH] = other.T.astype(BF)
    mine, other = by_core(core, query_part[0], query_part[1])
    kept[:, HEAD_WIDTH:] = mine.astype(BF)
    sent[:, HEAD_WIDTH:] = other.astype(BF)
    turned[HEAD_WIDTH:WIDE] = mine.T.astype(BF)
    turned[WIDE + HEAD_WIDTH :] = other.T.astype(BF)


def all_back(pos, own, from1, from2, raw, gain, cosine, sine, query_part):
    return pl.pallas_call(
        all_back_body,
        in_specs=[SMEM] + [VMEM] * 8,
        out_specs=[VMEM] * 3,
        out_shape=[
            jax.ShapeDtypeStruct((ROWS, WIDE), BF),
            jax.ShapeDtypeStruct((ROWS, WIDE), BF),
            jax.ShapeDtypeStruct((2 * WIDE, ROWS), BF),
        ],
        compiler_params=params(),
        cost_estimate=cost(10_000_000, 3_000_000),
    )(pos, own, from1, from2, raw, gain, cosine, sine, query_part)


def weight_terms_body(pos, tokens, other_tokens, back, other_back, mine, far_up, far_down, terms):
    step = pl.program_id(0)
    z, y = pos[0], pos[1]
    rows = pl.ds(pl.multiple_of(step * (DEPTH // 2), DEPTH // 2), DEPTH // 2)
    terms[rows, :] = (
        dot(tokens[...], back[...], 0, 0) + dot(other_tokens[...], other_back[...], 0, 0)
    ).astype(BF)

    @pl.when(step == 1)
    def spread():
        for z_offset in range(8):
            start = lax.rem(z + z_offset, 8) * PART
            same = pl.ds(pl.multiple_of(start + y * BLOCK, 16), BLOCK)
            other = pl.ds(pl.multiple_of(start + (1 - y) * BLOCK, 16), BLOCK)
            if z_offset == 4:
                far_up[...] = terms[same, :]
                far_down[...] = terms[other, :]
            else:
                mine[z_offset, 0] = terms[same, :]
                mine[z_offset, 1] = terms[other, :]


def weight_terms(pos, tokens, other_tokens, back, other_back):
    whole = lambda shape: pl.BlockSpec(shape, lambda k: (0,) * len(shape))
    shapes = [(8, 2, BLOCK, WIDE), (BLOCK, WIDE), (BLOCK, WIDE)]
    return pl.pallas_call(
        weight_terms_body,
        grid=(2,),
        in_specs=[
            SMEM,
            pl.BlockSpec((ROWS, DEPTH // 2), lambda k: (0, k)),
            pl.BlockSpec((ROWS, DEPTH // 2), lambda k: (0, k)),
            whole((ROWS, WIDE)),
            whole((ROWS, WIDE)),
        ],
        out_specs=[whole(shape) for shape in shapes],
        out_shape=[jax.ShapeDtypeStruct(shape, BF) for shape in shapes],
        scratch_shapes=[pltpu.VMEM((DEPTH, WIDE), BF)],
        compiler_params=params(),
        cost_estimate=cost(4 * ROWS * DEPTH * 256, 17_000_000),
    )(pos, tokens, other_tokens, back, other_back)


def token_terms(owners, weights, other_weights, turned, body, extras, shapes, after=()):
    count = owners.shape[0]
    whole = lambda shape: pl.BlockSpec(shape, lambda k, order: (0,) * len(shape))

    def window(number):
        return pl.BlockSpec((PART, WIDE), lambda k, order: (order[number], 0))

    def run(order, *refs):
        turned_ref = refs[2 * count]
        rest = refs[2 * count + 1 :]

        def term(number):
            return dot(refs[number][...], turned_ref[:WIDE]) + dot(
                refs[count + number][...], turned_ref[WIDE:]
            )

        body(term, rest[: len(extras)], rest[len(extras) + len(after) :])

    windows = [window(number) for number in range(count)]
    return pl.pallas_call(
        run,
        grid_spec=pltpu.PrefetchScalarGridSpec(
            num_scalar_prefetch=1,
            grid=(1,),
            in_specs=windows
            + windows
            + [whole((2 * WIDE, ROWS))]
            + [whole(extra.shape) for extra in extras]
            + [ANY] * len(after),
            out_specs=[whole(shape) for shape in shapes],
        ),
        out_shape=[jax.ShapeDtypeStruct(shape, BF) for shape in shapes],
        compiler_params=params(),
        cost_estimate=cost(2 * PART * ROWS * 512 * count, 1_500_000 * count),
    )(owners, *[weights] * count, *[other_weights] * count, turned, *extras, *after)


def combine(body, arrays, shapes, after=()):
    count = len(arrays)

    def run(*refs):
        body(refs[:count], refs[count + len(after) :])

    return pl.pallas_call(
        run,
        in_specs=[VMEM] * count + [ANY] * len(after),
        out_specs=[VMEM] * len(shapes),
        out_shape=[jax.ShapeDtypeStruct(shape, BF) for shape in shapes],
        compiler_params=params(),
        cost_estimate=cost(1_000_000, 2_000_000),
    )(*arrays, *after)


def wide(ref):
    return ref[...].astype(F32)


def chip_shard(halves, core):
    kept = jnp.where(core == 0, halves[0], halves[1])
    came = swap_core(jnp.where(core == 0, halves[1], halves[0]))
    return jnp.concatenate(
        [jnp.where(core == 0, kept, came), jnp.where(core == 0, came, kept)], axis=0
    )


def gather(shard, tokens, late):
    barrier = lax.optimization_barrier
    up1, down1, near = up_z(shard), down_z(shard), swap_y(shard)
    up1, down1, near, tokens = barrier((up1, down1, near, tokens))
    other_tokens = swap_core(tokens)
    up2, down2, near_up1, near_down1 = up_z(up1), down_z(down1), swap_y(up1), swap_y(down1)
    up2, down2, near_up1, near_down1 = barrier((up2, down2, near_up1, near_down1))
    up3, down3, near_up2, near_down2 = up_z(up2), down_z(down2), swap_y(up2), swap_y(down2)
    up3, down3, near_up2, near_down2, other_tokens, late = barrier(
        (up3, down3, near_up2, near_down2, other_tokens, late)
    )
    up4, down4 = up_z(up3[:, :HEAD_WIDTH]), down_z(down3[:, HEAD_WIDTH:])
    near_up3, near_down3 = swap_y(up3), swap_y(down3)
    arrivals = (
        (shard, near, 0, 0),
        (up1, near_up1, 7, 0),
        (down1, near_down1, 1, 0),
        (up2, near_up2, 6, 0),
        (down2, near_down2, 2, 0),
        (up3, near_up3, 5, 0),
        (down3, near_down3, 3, 0),
        (up4, swap_y(up4), 4, 0),
        (down4, swap_y(down4), 4, HEAD_WIDTH),
    )
    entries = []
    for same, other, z_offset, column in arrivals:
        entries += [(same, z_offset, 0, column), (other, z_offset, 1, column)]
    return entries, other_tokens, late


def shards(tokens, query_weight, key_matrix, value_matrix, query_gain, key_norm_gain, cotangent):
    ctx = lax.axis_index("ctx")
    tp = lax.axis_index("tp")
    z, y, core = ctx // 4, (ctx // 2) % 2, ctx % 2
    pos = jnp.stack([z, y, core, ctx]).astype(jnp.int32)
    token_positions = (ctx * ROWS + jnp.arange(ROWS, dtype=jnp.int32)).astype(F32)
    inverse = jnp.power(
        F32(rope_base), -jnp.arange(0, HEAD_WIDTH, 2).astype(F32) / HEAD_WIDTH
    )
    angles = token_positions[:, None] * inverse[None, :]
    cosine, sine = jnp.cos(angles), jnp.sin(angles)
    cosine = jnp.concatenate([cosine, cosine], axis=1)
    sine = jnp.concatenate([-sine, sine], axis=1)
    query_gain = query_gain.reshape(1, HEAD_WIDTH)
    key_gain = key_norm_gain.reshape(1, HEAD_WIDTH)

    shard = chip_shard(
        [
            jnp.concatenate([key_matrix, query_weight[:, :HEAD_WIDTH]], axis=1),
            jnp.concatenate([value_matrix, query_weight[:, HEAD_WIDTH:]], axis=1),
        ],
        core,
    )
    entries, other_tokens, (cosine, sine) = gather(shard, tokens, (cosine, sine))
    own_raw, sent_raw, weights = project(pos, tokens, other_tokens, entries)
    came_raw, weights_later = lax.optimization_barrier((swap_core(sent_raw), weights))
    pair_raw, query_raw, near0, queries = rotate_all(
        pos, own_raw, came_raw, key_gain, query_gain, cosine, sine
    )
    other_weights = swap_core(weights_later)
    near1, near2 = passed_along(near0, 1), passed_along(near0, 2)
    attended, grads0, grads1, grads2, score_grads = attend(
        pos, queries, near0, near1, near2, cotangent
    )
    from2, from1 = passed_along(grads2, -2), passed_along(grads1, -1)
    query_part = query_back(
        score_grads, near0, near1, near2, query_raw, query_gain, cosine, sine
    )
    kept, sent, turned = all_back(
        pos, grads0, from1, from2, pair_raw, key_gain, cosine, sine, query_part
    )
    other_back = swap_core(sent)

    def owners(*offsets):
        return jnp.stack(
            [(tp // 2 + i) % X_SIZE * 2 + (tp % 2 + j) % 2 for i, j in offsets]
        ).astype(jnp.int32)

    half = ROWS // 2
    token_shape = (PART, ROWS)
    terms = functools.partial(token_terms, weights=weights, other_weights=other_weights, turned=turned)

    def farthest(term, ins, outs):
        for number in range(2):
            part = term(number).astype(BF)
            outs[0][number] = part[:, :half]
            outs[1][number] = part[:, half:]

    def joined(far_offset):
        def body(term, ins, outs):
            part = term(0)
            outs[0][:, :half] = (part[:, :half] + ins[0][far_offset].astype(F32)).astype(BF)
            outs[0][:, half:] = part[:, half:].astype(BF)
            part = term(1)
            outs[1][:, :half] = part[:, :half].astype(BF)
            outs[1][:, half:] = (part[:, half:] + ins[1][far_offset].astype(F32)).astype(BF)

        return body

    def to_far(term, ins, outs):
        outs[0][...] = (term(0) + wide(ins[0]) + wide(ins[1])).astype(BF)

    def token_result(term, ins, outs):
        outs[0][...] = (term(0) + wide(ins[0]) + wide(ins[1]) + wide(ins[2])).astype(BF)

    def second_step(ins, outs):
        own, up, down = ins
        outs[0][0] = (own[3, 0].astype(F32) + wide(up)).astype(BF)
        outs[0][1] = own[3, 1]
        outs[1][0] = own[5, 0]
        outs[1][1] = (own[5, 1].astype(F32) + wide(down)).astype(BF)

    def later_step(hop):
        def body(ins, outs):
            own, up, down = ins
            outs[0][...] = (own[hop].astype(F32) + wide(up)).astype(BF)
            outs[1][...] = (own[8 - hop].astype(F32) + wide(down)).astype(BF)

        return body

    def last_step(ins, outs):
        own, up, down = ins
        total = own[0].astype(F32) + wide(up) + wide(down)
        outs[0][...] = total[0].astype(BF)
        outs[1][...] = total[1].astype(BF)

    block, both = (BLOCK, WIDE), (2, BLOCK, WIDE)
    far_a, far_b = terms(
        owners((2, 0), (2, 1)), body=farthest, extras=(), shapes=[(2, PART, half)] * 2
    )
    token_up, token_down = up_x(far_a), down_x(far_b)
    mine, far_up, far_down = weight_terms(pos, tokens, other_tokens, kept, other_back)
    up, down = up_z(far_up), down_z(far_down)
    arrived = (token_up, token_down)
    x1 = terms(
        owners((1, 1), (3, 1)),
        body=joined(1),
        extras=arrived,
        shapes=[token_shape] * 2,
        after=(up, down),
    )
    got_up1, got_down1 = up_x(x1[0]), down_x(x1[1])
    z2 = combine(second_step, (mine, up, down), [both] * 2, (x1[0],))
    up, down = up_z(z2[0]), down_z(z2[1])
    x2 = terms(
        owners((1, 0), (3, 0)),
        body=joined(0),
        extras=arrived,
        shapes=[token_shape] * 2,
        after=(z2[0],),
    )
    got_up0, got_down0 = up_x(x2[0]), down_x(x2[1])
    z3 = combine(later_step(2), (mine, up, down), [both] * 2, (x2[0],))
    up, down = up_z(z3[0]), down_z(z3[1])
    (x3,) = terms(
        owners((0, 1)),
        body=to_far,
        extras=(got_up1, got_down1),
        shapes=[token_shape],
        after=(z3[0],),
    )
    far = swap_far(x3)
    z4 = combine(later_step(1), (mine, up, down), [both] * 2, (x3,))
    up, down = up_z(z4[0]), down_z(z4[1])
    chip_kept, chip_sent = combine(last_step, (mine, up, down), [block] * 2)
    chip_came = swap_y(chip_sent)
    (token_sum,) = terms(
        owners((0, 0)),
        body=token_result,
        extras=(got_up0, got_down0, far),
        shapes=[token_shape],
        after=(chip_sent,),
    )

    def near_sum(ins, outs):
        outs[0][...] = (wide(ins[0]) + wide(ins[1])).astype(BF)

    (rows,) = combine(near_sum, (chip_kept, chip_came), [block], (token_sum,))
    rows = rows.reshape(2, BLOCK // 2, WIDE)
    kept_rows = jnp.where(core == 0, rows[0], rows[1])
    came_rows = swap_core(jnp.where(core == 0, rows[1], rows[0]))
    first = jnp.where(core == 0, kept_rows, came_rows)
    second = jnp.where(core == 0, came_rows, kept_rows)
    return (
        attended,
        token_sum.T,
        jnp.concatenate([first[:, HEAD_WIDTH:], second[:, HEAD_WIDTH:]], axis=1),
        first[:, :HEAD_WIDTH],
        second[:, :HEAD_WIDTH],
    )


def solution(mesh):
    in_specs = (
        P("ctx", None),
        P("ctx", "tp"),
        P("ctx", "tp"),
        P("ctx", "tp"),
        P(),
        P(),
        P("ctx", "tp"),
    )
    out_specs = (P("ctx", "tp"), P("ctx", "tp"), P("ctx", "tp"), P("ctx", "tp"), P("ctx", "tp"))
    return jax.shard_map(shards, mesh=mesh, in_specs=in_specs, out_specs=out_specs, check_vma=False)
```

```python
import functools

import jax
import jax.numpy as jnp
from jax import lax
from jax.experimental import pallas as pl
from jax.experimental.pallas import tpu as pltpu
from jax.sharding import PartitionSpec as P

HEAD_WIDTH = 128
WINDOW_LENGTH = 1024
QUERY_SCALAR = 168
SCORE_SCALE = QUERY_SCALAR ** (-0.5)

rope_base = 10000.0
norm_eps = 1e-06

Z_SIZE = 8
X_SIZE = 4
ROWS = 512
TILE = 256
SPAN = WINDOW_LENGTH + TILE
BAND = WINDOW_LENGTH + ROWS
DEPTH = 5376
VMEM_MEBIBYTES = 50
BLOCK = 336
PART = 672
BF = jnp.bfloat16
F32 = jnp.float32


def along_z(step):
    return [(i, ((i // 4 + step) % Z_SIZE) * 4 + i % 4) for i in range(4 * Z_SIZE)]


def along_x(step):
    return [(i, ((i // 2 + step) % X_SIZE) * 2 + i % 2) for i in range(2 * X_SIZE)]


SIBLING = [(i, i ^ 1) for i in range(32)]
NEAR_Y = [(i, i ^ 2) for i in range(32)]
FAR_Y = [(i, i ^ 1) for i in range(8)]


def up_z(piece):
    return lax.ppermute(piece, "ctx", along_z(1))


def down_z(piece):
    return lax.ppermute(piece, "ctx", along_z(-1))


def swap_y(piece):
    return lax.ppermute(piece, "ctx", NEAR_Y)


def swap_core(piece):
    return lax.ppermute(piece, "ctx", SIBLING)


def up_x(piece):
    return lax.ppermute(piece, "tp", along_x(1))


def down_x(piece):
    return lax.ppermute(piece, "tp", along_x(-1))


def swap_far(piece):
    return lax.ppermute(piece, "tp", FAR_Y)


def passed_along(shard, by):
    pairs = [(i, i + by) for i in range(32) if 0 <= i + by < 32]
    return lax.ppermute(shard, "ctx", pairs)


def summed(*terms):
    total = terms[0].astype(F32)
    for term in terms[1:]:
        total = total + term.astype(F32)
    return total.astype(BF)


def dot(left, right, left_axis=1, right_axis=0):
    return lax.dot_general(
        left, right, (((left_axis,), (right_axis,)), ((), ())), preferred_element_type=F32
    )


def params(mebibytes=VMEM_MEBIBYTES):
    return pltpu.CompilerParams(vmem_limit_bytes=mebibytes * 1024 * 1024)


def cost(flops, moved):
    return pl.CostEstimate(flops=flops, bytes_accessed=moved, transcendentals=0)


VMEM = pl.BlockSpec(memory_space=pltpu.VMEM)
ANY = pl.BlockSpec(memory_space=pl.ANY)
SMEM = pl.BlockSpec(memory_space=pltpu.SMEM)


def rotate(raw, gain, cosine, sine):
    scale = lax.rsqrt(jnp.mean(raw * raw, axis=-1, keepdims=True) + norm_eps)
    normed = raw * scale * gain
    return normed * cosine + pltpu.roll(normed, HEAD_WIDTH // 2, 1) * sine


def rotate_back(raw, grads, gain, cosine, sine):
    scale = lax.rsqrt(jnp.mean(raw * raw, axis=-1, keepdims=True) + norm_eps)
    turned = (grads * cosine - pltpu.roll(grads, HEAD_WIDTH // 2, 1) * sine) * gain
    inner = jnp.mean(raw * turned, axis=-1, keepdims=True)
    return turned * scale - raw * (scale * scale * scale * inner)


DEPTH_STEPS = 3
DEPTH_STEP = DEPTH // DEPTH_STEPS
WIDE = 2 * HEAD_WIDTH


def by_core(core, first, second):
    return jnp.where(core == 0, first, second), jnp.where(core == 0, second, first)


def project_body(places, pos, tokens, other_tokens, *refs):
    count = len(places)
    pieces = refs[:count]
    own, sent, kept, weights, sems, out_sem = refs[count:]
    step = pl.program_id(0)
    z, y = pos[0], pos[1]

    @pl.when(step == 0)
    def place():
        copies = []
        for number, (z_offset, y_offset, column, width) in enumerate(places):
            block = lax.rem(z + z_offset, 8) * 2 + lax.rem(y + y_offset, 2)
            start = pl.multiple_of(block * BLOCK, 16)
            copies.append(
                pltpu.make_async_copy(
                    pieces[number],
                    weights.at[pl.ds(start, BLOCK), pl.ds(column, width)],
                    sems.at[number],
                )
            )
        for copy in copies:
            copy.start()
        for copy in copies:
            copy.wait()
        pltpu.make_async_copy(weights, kept, out_sem).start()
        own[...] = jnp.zeros_like(own)
        sent[...] = jnp.zeros_like(sent)

    start = pl.multiple_of(step * DEPTH_STEP, DEPTH_STEP)
    block = weights[pl.ds(start, DEPTH_STEP), :]
    own[...] += dot(tokens[...], block)
    sent[...] += dot(other_tokens[...], block)

    @pl.when(step == DEPTH_STEPS - 1)
    def finish():
        pltpu.make_async_copy(weights, kept, out_sem).wait()


def project(pos, tokens, other_tokens, entries):
    places = tuple((e[1], e[2], e[3], e[0].shape[1]) for e in entries)
    whole = lambda shape: pl.BlockSpec(shape, lambda k: (0,) * len(shape))
    return pl.pallas_call(
        functools.partial(project_body, places),
        grid=(DEPTH_STEPS,),
        in_specs=[SMEM] + [pl.BlockSpec((ROWS, DEPTH_STEP), lambda k: (0, k))] * 2 + [ANY] * len(entries),
        out_specs=[whole((ROWS, WIDE)), whole((ROWS, WIDE)), ANY],
        out_shape=[
            jax.ShapeDtypeStruct((ROWS, WIDE), F32),
            jax.ShapeDtypeStruct((ROWS, WIDE), F32),
            jax.ShapeDtypeStruct((DEPTH, WIDE), BF),
        ],
        scratch_shapes=[
            pltpu.VMEM((DEPTH, WIDE), BF),
            pltpu.SemaphoreType.DMA((len(entries),)),
            pltpu.SemaphoreType.DMA,
        ],
        compiler_params=params(),
        cost_estimate=cost(2 * ROWS * DEPTH * 512, 17_000_000),
    )(pos, tokens, other_tokens, *[e[0] for e in entries])


def rotate_all_body(
    pos, own, came, key_gain, query_gain, cosine, sine, pair_raw, query_raw, pair_rows, query_rows
):
    core = pos[2]
    key, value = by_core(core, own[:, :HEAD_WIDTH], came[:, :HEAD_WIDTH])
    first, second = by_core(core, own[:, HEAD_WIDTH:], came[:, HEAD_WIDTH:])
    pair_raw[...] = key
    query_raw[0] = first
    query_raw[1] = second
    pair_rows[0] = rotate(key, key_gain[...], cosine[...], sine[...]).astype(BF)
    pair_rows[1] = value.astype(BF)
    query_rows[0] = rotate(first, query_gain[...], cosine[...], sine[...]).astype(BF)
    query_rows[1] = rotate(second, query_gain[...], cosine[...], sine[...]).astype(BF)


def rotate_all(pos, own, came, key_gain, query_gain, cosine, sine):
    pair = (2, ROWS, HEAD_WIDTH)
    return pl.pallas_call(
        rotate_all_body,
        in_specs=[SMEM] + [VMEM] * 6,
        out_specs=[VMEM] * 4,
        out_shape=[
            jax.ShapeDtypeStruct((ROWS, HEAD_WIDTH), F32),
            jax.ShapeDtypeStruct(pair, F32),
            jax.ShapeDtypeStruct(pair, BF),
            jax.ShapeDtypeStruct(pair, BF),
        ],
        compiler_params=params(),
        cost_estimate=cost(10_000_000, 3_000_000),
    )(pos, own, came, key_gain, query_gain, cosine, sine)


def load_band(nears, number, band, sems):
    copies = []
    for part, near in enumerate(nears):
        copy = pltpu.make_async_copy(
            near.at[number], band.at[pl.ds(part * ROWS, ROWS), :], sems.at[number, part]
        )
        copy.start()
        copies.append(copy)
    return copies


def attend_body(
    pos, queries, near0, near1, near2, cotangent, attended, grads0, grads1, grads2, score_grads,
    keys, values, values_turned, terms, weights, key_sums, value_sums, sems,
):
    nears = (near2, near1, near0)
    copies = load_band(nears, 0, keys, sems) + load_band(nears, 1, values, sems)
    for copy in copies:
        copy.wait()
    for part in range(3):
        rows = slice(part * ROWS, (part + 1) * ROWS)
        values_turned[:, rows] = values[rows].astype(F32).T.astype(BF)
    key_sums[...] = jnp.zeros_like(key_sums)
    value_sums[...] = jnp.zeros_like(value_sums)
    valid2 = (pos[3] >= 2).astype(F32)
    valid1 = (pos[3] >= 1).astype(F32)
    valid = (valid2, valid2, valid1, valid1, None, None)
    key_place = lax.broadcasted_iota(jnp.int32, (TILE, TILE), 0)
    query_place = lax.broadcasted_iota(jnp.int32, (TILE, TILE), 1)
    for head in range(2):
        columns = slice(head * HEAD_WIDTH, (head + 1) * HEAD_WIDTH)
        for tile in range(2):
            here = slice(tile * TILE, (tile + 1) * TILE)
            span = slice(tile * TILE, tile * TILE + SPAN)
            query = queries[head, here]
            out = cotangent[here, columns]
            total = jnp.zeros((1, TILE), F32)
            for block in range(5):
                low = block * TILE
                scores = dot(keys[tile * TILE + low : tile * TILE + low + TILE], query, 1, 1)
                term = jnp.exp(scores * SCORE_SCALE)
                if block == 0:
                    term = jnp.where(key_place > query_place, term, 0.0)
                if block == 4:
                    term = jnp.where(key_place <= query_place, term, 0.0)
                if valid[tile + block] is not None:
                    term = term * valid[tile + block]
                terms[low : low + TILE] = term
                total = total + jnp.sum(term, axis=0, keepdims=True)
            inverse = 1.0 / total
            for block in range(5):
                low = block * TILE
                weights[low : low + TILE] = (terms[low : low + TILE] * inverse).astype(BF)
            mixed = dot(values_turned[:, span], weights[...])
            rounded = mixed.astype(BF).astype(F32)
            attended[here, columns] = mixed.T.astype(BF)
            delta = jnp.sum(out.astype(F32).T * rounded, axis=0, keepdims=True)
            for block in range(5):
                low = block * TILE
                prob_grads = dot(values[tile * TILE + low : tile * TILE + low + TILE], out, 1, 1)
                probs = terms[low : low + TILE] * inverse
                score_grads[head, tile, low : low + TILE] = (probs * (prob_grads - delta)).astype(BF)
            key_sums[span] += dot(score_grads[head, tile], query)
            value_sums[span] += dot(weights[...], out)
    for part, ref in enumerate((grads2, grads1, grads0)):
        rows = slice(part * ROWS, (part + 1) * ROWS)
        ref[0] = (key_sums[rows] * SCORE_SCALE).astype(ref.dtype)
        ref[1] = value_sums[rows].astype(ref.dtype)


def attend(pos, queries, near0, near1, near2, cotangent):
    pair = (2, ROWS, HEAD_WIDTH)
    return pl.pallas_call(
        attend_body,
        in_specs=[SMEM, VMEM] + [ANY] * 3 + [VMEM],
        out_specs=[VMEM] * 5,
        out_shape=[
            jax.ShapeDtypeStruct((ROWS, 2 * HEAD_WIDTH), BF),
            jax.ShapeDtypeStruct(pair, F32),
            jax.ShapeDtypeStruct(pair, BF),
            jax.ShapeDtypeStruct(pair, BF),
            jax.ShapeDtypeStruct((2, 2, SPAN, TILE), BF),
        ],
        scratch_shapes=[
            pltpu.VMEM((BAND, HEAD_WIDTH), BF),
            pltpu.VMEM((BAND, HEAD_WIDTH), BF),
            pltpu.VMEM((HEAD_WIDTH, BAND), BF),
            pltpu.VMEM((SPAN, TILE), F32),
            pltpu.VMEM((SPAN, TILE), BF),
            pltpu.VMEM((BAND, HEAD_WIDTH), F32),
            pltpu.VMEM((BAND, HEAD_WIDTH), F32),
            pltpu.SemaphoreType.DMA((2, 3)),
        ],
        compiler_params=params(),
        cost_estimate=cost(8_000_000_000, 8_000_000),
    )(pos, queries, near0, near1, near2, cotangent)


def query_back_body(
    score_grads, near0, near1, near2, raw, gain, cosine, sine, back, keys, keys_turned, sems
):
    for copy in load_band((near2, near1, near0), 0, keys, sems):
        copy.wait()
    for part in range(3):
        rows = slice(part * ROWS, (part + 1) * ROWS)
        keys_turned[:, rows] = keys[rows].astype(F32).T.astype(BF)
    for head in range(2):
        for tile in range(2):
            here = slice(tile * TILE, (tile + 1) * TILE)
            grads = dot(keys_turned[:, tile * TILE : tile * TILE + SPAN], score_grads[head, tile])
            grads = (grads * SCORE_SCALE).T
            back[head, here] = rotate_back(
                raw[head, here], grads, gain[...], cosine[here], sine[here]
            )


def query_back(score_grads, near0, near1, near2, raw, gain, cosine, sine):
    return pl.pallas_call(
        query_back_body,
        in_specs=[VMEM] + [ANY] * 3 + [VMEM] * 4,
        out_specs=VMEM,
        out_shape=jax.ShapeDtypeStruct((2, ROWS, HEAD_WIDTH), F32),
        scratch_shapes=[
            pltpu.VMEM((BAND, HEAD_WIDTH), BF),
            pltpu.VMEM((HEAD_WIDTH, BAND), BF),
            pltpu.SemaphoreType.DMA((1, 3)),
        ],
        compiler_params=params(),
        cost_estimate=cost(1_000_000_000, 4_000_000),
    )(score_grads, near0, near1, near2, raw, gain, cosine, sine)


def all_back_body(
    pos, own, from1, from2, raw, gain, cosine, sine, query_part, kept, sent, turned
):
    core = pos[2]
    grads = own[...] + from1[...].astype(F32) + from2[...].astype(F32)
    key_part = rotate_back(raw[...], grads[0], gain[...], cosine[...], sine[...])
    mine, other = by_core(core, key_part, grads[1])
    kept[:, :HEAD_WIDTH] = mine.astype(BF)
    sent[:, :HEAD_WIDTH] = other.astype(BF)
    turned[:HEAD_WIDTH] = mine.T.astype(BF)
    turned[WIDE : WIDE + HEAD_WIDTH] = other.T.astype(BF)
    mine, other = by_core(core, query_part[0], query_part[1])
    kept[:, HEAD_WIDTH:] = mine.astype(BF)
    sent[:, HEAD_WIDTH:] = other.astype(BF)
    turned[HEAD_WIDTH:WIDE] = mine.T.astype(BF)
    turned[WIDE + HEAD_WIDTH :] = other.T.astype(BF)


def all_back(pos, own, from1, from2, raw, gain, cosine, sine, query_part):
    return pl.pallas_call(
        all_back_body,
        in_specs=[SMEM] + [VMEM] * 8,
        out_specs=[VMEM] * 3,
        out_shape=[
            jax.ShapeDtypeStruct((ROWS, WIDE), BF),
            jax.ShapeDtypeStruct((ROWS, WIDE), BF),
            jax.ShapeDtypeStruct((2 * WIDE, ROWS), BF),
        ],
        compiler_params=params(),
        cost_estimate=cost(10_000_000, 3_000_000),
    )(pos, own, from1, from2, raw, gain, cosine, sine, query_part)


def weight_terms_body(pos, tokens, other_tokens, back, other_back, mine, far_up, far_down, terms):
    step = pl.program_id(0)
    z, y = pos[0], pos[1]
    rows = pl.ds(pl.multiple_of(step * (DEPTH // 2), DEPTH // 2), DEPTH // 2)
    terms[rows, :] = (
        dot(tokens[...], back[...], 0, 0) + dot(other_tokens[...], other_back[...], 0, 0)
    ).astype(BF)

    @pl.when(step == 1)
    def spread():
        for z_offset in range(8):
            start = lax.rem(z + z_offset, 8) * PART
            same = pl.ds(pl.multiple_of(start + y * BLOCK, 16), BLOCK)
            other = pl.ds(pl.multiple_of(start + (1 - y) * BLOCK, 16), BLOCK)
            if z_offset == 4:
                far_up[...] = terms[same, :]
                far_down[...] = terms[other, :]
            else:
                mine[z_offset, 0] = terms[same, :]
                mine[z_offset, 1] = terms[other, :]


def weight_terms(pos, tokens, other_tokens, back, other_back):
    whole = lambda shape: pl.BlockSpec(shape, lambda k: (0,) * len(shape))
    shapes = [(8, 2, BLOCK, WIDE), (BLOCK, WIDE), (BLOCK, WIDE)]
    return pl.pallas_call(
        weight_terms_body,
        grid=(2,),
        in_specs=[
            SMEM,
            pl.BlockSpec((ROWS, DEPTH // 2), lambda k: (0, k)),
            pl.BlockSpec((ROWS, DEPTH // 2), lambda k: (0, k)),
            whole((ROWS, WIDE)),
            whole((ROWS, WIDE)),
        ],
        out_specs=[whole(shape) for shape in shapes],
        out_shape=[jax.ShapeDtypeStruct(shape, BF) for shape in shapes],
        scratch_shapes=[pltpu.VMEM((DEPTH, WIDE), BF)],
        compiler_params=params(),
        cost_estimate=cost(4 * ROWS * DEPTH * 256, 17_000_000),
    )(pos, tokens, other_tokens, back, other_back)


def token_terms(owners, weights, other_weights, turned, body, extras, shapes, after=()):
    count = owners.shape[0]
    whole = lambda shape: pl.BlockSpec(shape, lambda k, order: (0,) * len(shape))

    def window(number):
        return pl.BlockSpec((PART, WIDE), lambda k, order: (order[number], 0))

    def run(order, *refs):
        turned_ref = refs[2 * count]
        rest = refs[2 * count + 1 :]

        def term(number):
            return dot(refs[number][...], turned_ref[:WIDE]) + dot(
                refs[count + number][...], turned_ref[WIDE:]
            )

        body(term, rest[: len(extras)], rest[len(extras) + len(after) :])

    windows = [window(number) for number in range(count)]
    return pl.pallas_call(
        run,
        grid_spec=pltpu.PrefetchScalarGridSpec(
            num_scalar_prefetch=1,
            grid=(1,),
            in_specs=windows
            + windows
            + [whole((2 * WIDE, ROWS))]
            + [whole(extra.shape) for extra in extras]
            + [ANY] * len(after),
            out_specs=[whole(shape) for shape in shapes],
        ),
        out_shape=[jax.ShapeDtypeStruct(shape, BF) for shape in shapes],
        compiler_params=params(),
        cost_estimate=cost(2 * PART * ROWS * 512 * count, 1_500_000 * count),
    )(owners, *[weights] * count, *[other_weights] * count, turned, *extras, *after)


def combine(body, arrays, shapes, after=()):
    count = len(arrays)
    specs, operands = [], []
    for entry in arrays:
        if isinstance(entry, tuple):
            array, number = entry
            shape = (1,) + array.shape[1:]
            specs.append(pl.BlockSpec(shape, lambda k, number=number: (number, 0, 0, 0)))
        else:
            array = entry
            specs.append(SMEM if array.dtype == jnp.int32 else VMEM)
        operands.append(array)

    def run(*refs):
        body(refs[:count], refs[count + len(after) :])

    return pl.pallas_call(
        run,
        grid=(1,),
        in_specs=specs + [ANY] * len(after),
        out_specs=[VMEM] * len(shapes),
        out_shape=[jax.ShapeDtypeStruct(shape, BF) for shape in shapes],
        compiler_params=params(),
        cost_estimate=cost(1_000_000, 2_000_000),
    )(*operands, *after)


def wide(ref):
    return ref[...].astype(F32)


def chip_shard(halves, core):
    kept = jnp.where(core == 0, halves[0], halves[1])
    came = swap_core(jnp.where(core == 0, halves[1], halves[0]))
    return jnp.concatenate(
        [jnp.where(core == 0, kept, came), jnp.where(core == 0, came, kept)], axis=0
    )


def gather(shard, tokens, late):
    barrier = lax.optimization_barrier
    up1, down1, near = up_z(shard), down_z(shard), swap_y(shard)
    up1, down1, near, tokens = barrier((up1, down1, near, tokens))
    other_tokens = swap_core(tokens)
    up2, down2, near_up1, near_down1 = up_z(up1), down_z(down1), swap_y(up1), swap_y(down1)
    up2, down2, near_up1, near_down1 = barrier((up2, down2, near_up1, near_down1))
    up3, down3, near_up2, near_down2 = up_z(up2), down_z(down2), swap_y(up2), swap_y(down2)
    up3, down3, near_up2, near_down2, other_tokens, late = barrier(
        (up3, down3, near_up2, near_down2, other_tokens, late)
    )
    up4, down4 = up_z(up3[:, :HEAD_WIDTH]), down_z(down3[:, HEAD_WIDTH:])
    near_up3, near_down3 = up_z(near_up2), down_z(near_down2)
    arrivals = (
        (shard, near, 0, 0),
        (up1, near_up1, 7, 0),
        (down1, near_down1, 1, 0),
        (up2, near_up2, 6, 0),
        (down2, near_down2, 2, 0),
        (up3, near_up3, 5, 0),
        (down3, near_down3, 3, 0),
        (up4, swap_y(up4), 4, 0),
        (down4, swap_y(down4), 4, HEAD_WIDTH),
    )
    entries = []
    for same, other, z_offset, column in arrivals:
        entries += [(same, z_offset, 0, column), (other, z_offset, 1, column)]
    return entries, other_tokens, late


def shards(tokens, query_weight, key_matrix, value_matrix, query_gain, key_norm_gain, cotangent):
    ctx = lax.axis_index("ctx")
    tp = lax.axis_index("tp")
    z, y, core = ctx // 4, (ctx // 2) % 2, ctx % 2
    pos = jnp.stack([z, y, core, ctx]).astype(jnp.int32)
    token_positions = (ctx * ROWS + jnp.arange(ROWS, dtype=jnp.int32)).astype(F32)
    inverse = jnp.power(
        F32(rope_base), -jnp.arange(0, HEAD_WIDTH, 2).astype(F32) / HEAD_WIDTH
    )
    angles = token_positions[:, None] * inverse[None, :]
    cosine, sine = jnp.cos(angles), jnp.sin(angles)
    cosine = jnp.concatenate([cosine, cosine], axis=1)
    sine = jnp.concatenate([-sine, sine], axis=1)
    query_gain = query_gain.reshape(1, HEAD_WIDTH)
    key_gain = key_norm_gain.reshape(1, HEAD_WIDTH)

    shard = chip_shard(
        [
            jnp.concatenate([key_matrix, query_weight[:, :HEAD_WIDTH]], axis=1),
            jnp.concatenate([value_matrix, query_weight[:, HEAD_WIDTH:]], axis=1),
        ],
        core,
    )
    entries, other_tokens, (cosine, sine) = gather(shard, tokens, (cosine, sine))
    own_raw, sent_raw, weights = project(pos, tokens, other_tokens, entries)
    came_raw, weights_later = lax.optimization_barrier((swap_core(sent_raw), weights))
    pair_raw, query_raw, near0, queries = rotate_all(
        pos, own_raw, came_raw, key_gain, query_gain, cosine, sine
    )
    other_weights = swap_core(weights_later)
    near1, near2 = passed_along(near0, 1), passed_along(near0, 2)
    attended, grads0, grads1, grads2, score_grads = attend(
        pos, queries, near0, near1, near2, cotangent
    )
    from2, from1 = passed_along(grads2, -2), passed_along(grads1, -1)
    query_part = query_back(
        score_grads, near0, near1, near2, query_raw, query_gain, cosine, sine
    )
    kept, sent, turned = all_back(
        pos, grads0, from1, from2, pair_raw, key_gain, cosine, sine, query_part
    )
    other_back = swap_core(sent)

    def owners(*offsets):
        return jnp.stack(
            [(tp // 2 + i) % X_SIZE * 2 + (tp % 2 + j) % 2 for i, j in offsets]
        ).astype(jnp.int32)

    half = ROWS // 2
    token_shape = (PART, ROWS)
    terms = functools.partial(token_terms, weights=weights, other_weights=other_weights, turned=turned)

    def farthest(term, ins, outs):
        for number in range(2):
            part = term(number).astype(BF)
            outs[0][number] = part[:, :half]
            outs[1][number] = part[:, half:]

    def joined(far_offset):
        def body(term, ins, outs):
            part = term(0)
            outs[0][:, :half] = (part[:, :half] + ins[0][far_offset].astype(F32)).astype(BF)
            outs[0][:, half:] = part[:, half:].astype(BF)
            part = term(1)
            outs[1][:, :half] = part[:, :half].astype(BF)
            outs[1][:, half:] = (part[:, half:] + ins[1][far_offset].astype(F32)).astype(BF)

        return body

    def to_far(term, ins, outs):
        outs[0][...] = (term(0) + wide(ins[0]) + wide(ins[1])).astype(BF)

    def token_result(term, ins, outs):
        outs[0][...] = (term(0) + wide(ins[0]) + wide(ins[1]) + wide(ins[2])).astype(BF)

    def second_step(ins, outs):
        upper, lower, up, down = ins
        outs[0][0] = (upper[0, 0].astype(F32) + wide(up)).astype(BF)
        outs[0][1] = upper[0, 1]
        outs[1][0] = lower[0, 0]
        outs[1][1] = (lower[0, 1].astype(F32) + wide(down)).astype(BF)

    def later_step(ins, outs):
        upper, lower, up, down = ins
        outs[0][...] = (upper[0].astype(F32) + wide(up)).astype(BF)
        outs[1][...] = (lower[0].astype(F32) + wide(down)).astype(BF)

    def last_step(ins, outs):
        own, up, down = ins
        total = own[0].astype(F32) + wide(up) + wide(down)
        outs[0][...] = total[0].astype(BF)
        outs[1][...] = total[1].astype(BF)

    def near_sum(ins, outs):
        total = wide(ins[1]) + wide(ins[2])
        first, second = by_core(ins[0][2], total[: BLOCK // 2], total[BLOCK // 2 :])
        outs[0][...] = first.astype(BF)
        outs[1][...] = second.astype(BF)

    def to_outputs(ins, outs):
        first, second = by_core(ins[0][2], wide(ins[1]), wide(ins[2]))
        outs[0][:, :HEAD_WIDTH] = first[:, HEAD_WIDTH:].astype(BF)
        outs[0][:, HEAD_WIDTH:] = second[:, HEAD_WIDTH:].astype(BF)
        outs[1][...] = first[:, :HEAD_WIDTH].astype(BF)
        outs[2][...] = second[:, :HEAD_WIDTH].astype(BF)

    block, both = (BLOCK, WIDE), (2, BLOCK, WIDE)
    far_a, far_b = terms(
        owners((2, 0), (2, 1)), body=farthest, extras=(), shapes=[(2, PART, half)] * 2
    )
    token_up, token_down = up_x(far_a), down_x(far_b)
    mine, far_up, far_down = weight_terms(pos, tokens, other_tokens, kept, other_back)
    up, down = up_z(far_up), down_z(far_down)
    arrived = (token_up, token_down)
    z2 = combine(second_step, ((mine, 3), (mine, 5), up, down), [both] * 2)
    up, down = up_z(z2[0]), down_z(z2[1])
    x1 = terms(
        owners((1, 1), (3, 1)),
        body=joined(1),
        extras=arrived,
        shapes=[token_shape] * 2,
        after=(z2[0],),
    )
    got_up1, got_down1 = up_x(x1[0]), down_x(x1[1])
    z3 = combine(later_step, ((mine, 2), (mine, 6), up, down), [both] * 2, (x1[0],))
    up, down = up_z(z3[0]), down_z(z3[1])
    x2 = terms(
        owners((1, 0), (3, 0)),
        body=joined(0),
        extras=arrived,
        shapes=[token_shape] * 2,
        after=(z3[0],),
    )
    got_up0, got_down0 = up_x(x2[0]), down_x(x2[1])
    (x3,) = terms(
        owners((0, 1)),
        body=to_far,
        extras=(got_up1, got_down1),
        shapes=[token_shape],
        after=(x2[0],),
    )
    far = swap_far(x3)
    z4 = combine(later_step, ((mine, 1), (mine, 7), up, down), [both] * 2, (x3,))
    up, down = up_z(z4[0]), down_z(z4[1])
    chip_kept, chip_sent = combine(last_step, ((mine, 0), up, down), [block] * 2)
    chip_came = swap_y(chip_sent)
    (token_sum,) = terms(
        owners((0, 0)),
        body=token_result,
        extras=(got_up0, got_down0, far),
        shapes=[token_shape],
        after=(chip_sent,),
    )
    rows = (BLOCK // 2, WIDE)
    row_kept, row_sent = combine(near_sum, (pos, chip_kept, chip_came), [rows] * 2, (token_sum,))
    narrow = (BLOCK // 2, HEAD_WIDTH)
    query_gradient, key_gradient, value_gradient = combine(
        to_outputs, (pos, row_kept, swap_core(row_sent)), [rows, narrow, narrow]
    )
    return (attended, token_sum.T, query_gradient, key_gradient, value_gradient)


def solution(mesh):
    in_specs = (
        P("ctx", None),
        P("ctx", "tp"),
        P("ctx", "tp"),
        P("ctx", "tp"),
        P(),
        P(),
        P("ctx", "tp"),
    )
    out_specs = (P("ctx", "tp"), P("ctx", "tp"), P("ctx", "tp"), P("ctx", "tp"), P("ctx", "tp"))
    return jax.shard_map(shards, mesh=mesh, in_specs=in_specs, out_specs=out_specs, check_vma=False)
```

```python
import functools

import jax
import jax.numpy as jnp
from jax import lax
from jax.experimental import pallas as pl
from jax.experimental.pallas import tpu as pltpu
from jax.sharding import PartitionSpec as P

HEAD_WIDTH = 128
WINDOW_LENGTH = 1024
QUERY_SCALAR = 168
SCORE_SCALE = QUERY_SCALAR ** (-0.5)

rope_base = 10000.0
norm_eps = 1e-06

Z_SIZE = 8
X_SIZE = 4
ROWS = 512
TILE = 256
SPAN = WINDOW_LENGTH + TILE
BAND = WINDOW_LENGTH + ROWS
DEPTH = 5376
VMEM_MEBIBYTES = 50
BLOCK = 336
PART = 672
BF = jnp.bfloat16
F32 = jnp.float32


def along_z(step):
    return [(i, ((i // 4 + step) % Z_SIZE) * 4 + i % 4) for i in range(4 * Z_SIZE)]


def along_x(step):
    return [(i, ((i // 2 + step) % X_SIZE) * 2 + i % 2) for i in range(2 * X_SIZE)]


SIBLING = [(i, i ^ 1) for i in range(32)]
NEAR_Y = [(i, i ^ 2) for i in range(32)]
FAR_Y = [(i, i ^ 1) for i in range(8)]


def up_z(piece):
    return lax.ppermute(piece, "ctx", along_z(1))


def down_z(piece):
    return lax.ppermute(piece, "ctx", along_z(-1))


def swap_y(piece):
    return lax.ppermute(piece, "ctx", NEAR_Y)


def swap_core(piece):
    return lax.ppermute(piece, "ctx", SIBLING)


def up_x(piece):
    return lax.ppermute(piece, "tp", along_x(1))


def down_x(piece):
    return lax.ppermute(piece, "tp", along_x(-1))


def swap_far(piece):
    return lax.ppermute(piece, "tp", FAR_Y)


def passed_along(shard, by):
    pairs = [(i, i + by) for i in range(32) if 0 <= i + by < 32]
    return lax.ppermute(shard, "ctx", pairs)


def summed(*terms):
    total = terms[0].astype(F32)
    for term in terms[1:]:
        total = total + term.astype(F32)
    return total.astype(BF)


def dot(left, right, left_axis=1, right_axis=0):
    return lax.dot_general(
        left, right, (((left_axis,), (right_axis,)), ((), ())), preferred_element_type=F32
    )


def params(mebibytes=VMEM_MEBIBYTES):
    return pltpu.CompilerParams(vmem_limit_bytes=mebibytes * 1024 * 1024)


def cost(flops, moved):
    return pl.CostEstimate(flops=flops, bytes_accessed=moved, transcendentals=0)


VMEM = pl.BlockSpec(memory_space=pltpu.VMEM)
ANY = pl.BlockSpec(memory_space=pl.ANY)
SMEM = pl.BlockSpec(memory_space=pltpu.SMEM)


def rotate(raw, gain, cosine, sine):
    scale = lax.rsqrt(jnp.mean(raw * raw, axis=-1, keepdims=True) + norm_eps)
    normed = raw * scale * gain
    return normed * cosine + pltpu.roll(normed, HEAD_WIDTH // 2, 1) * sine


def rotate_back(raw, grads, gain, cosine, sine):
    scale = lax.rsqrt(jnp.mean(raw * raw, axis=-1, keepdims=True) + norm_eps)
    turned = (grads * cosine - pltpu.roll(grads, HEAD_WIDTH // 2, 1) * sine) * gain
    inner = jnp.mean(raw * turned, axis=-1, keepdims=True)
    return turned * scale - raw * (scale * scale * scale * inner)


DEPTH_STEPS = 3
DEPTH_STEP = DEPTH // DEPTH_STEPS
WIDE = 2 * HEAD_WIDTH


def by_core(core, first, second):
    return jnp.where(core == 0, first, second), jnp.where(core == 0, second, first)


def project_body(places, pos, tokens, other_tokens, *refs):
    count = len(places)
    pieces = refs[:count]
    own, sent, kept, weights, sems, out_sem = refs[count:]
    step = pl.program_id(0)
    z, y = pos[0], pos[1]

    @pl.when(step == 0)
    def place():
        copies = []
        for number, (z_offset, y_offset, column, width) in enumerate(places):
            block = lax.rem(z + z_offset, 8) * 2 + lax.rem(y + y_offset, 2)
            start = pl.multiple_of(block * BLOCK, 16)
            copies.append(
                pltpu.make_async_copy(
                    pieces[number],
                    weights.at[pl.ds(start, BLOCK), pl.ds(column, width)],
                    sems.at[number],
                )
            )
        for copy in copies:
            copy.start()
        for copy in copies:
            copy.wait()
        pltpu.make_async_copy(weights, kept, out_sem).start()
        own[...] = jnp.zeros_like(own)
        sent[...] = jnp.zeros_like(sent)

    start = pl.multiple_of(step * DEPTH_STEP, DEPTH_STEP)
    block = weights[pl.ds(start, DEPTH_STEP), :]
    own[...] += dot(tokens[...], block)
    sent[...] += dot(other_tokens[...], block)

    @pl.when(step == DEPTH_STEPS - 1)
    def finish():
        pltpu.make_async_copy(weights, kept, out_sem).wait()


def project(pos, tokens, other_tokens, entries):
    places = tuple((e[1], e[2], e[3], e[0].shape[1]) for e in entries)
    whole = lambda shape: pl.BlockSpec(shape, lambda k: (0,) * len(shape))
    return pl.pallas_call(
        functools.partial(project_body, places),
        grid=(DEPTH_STEPS,),
        in_specs=[SMEM] + [pl.BlockSpec((ROWS, DEPTH_STEP), lambda k: (0, k))] * 2 + [ANY] * len(entries),
        out_specs=[whole((ROWS, WIDE)), whole((ROWS, WIDE)), ANY],
        out_shape=[
            jax.ShapeDtypeStruct((ROWS, WIDE), F32),
            jax.ShapeDtypeStruct((ROWS, WIDE), F32),
            jax.ShapeDtypeStruct((DEPTH, WIDE), BF),
        ],
        scratch_shapes=[
            pltpu.VMEM((DEPTH, WIDE), BF),
            pltpu.SemaphoreType.DMA((len(entries),)),
            pltpu.SemaphoreType.DMA,
        ],
        compiler_params=params(),
        cost_estimate=cost(2 * ROWS * DEPTH * 512, 17_000_000),
    )(pos, tokens, other_tokens, *[e[0] for e in entries])


def rotate_all_body(
    pos, own, came, key_gain, query_gain, cosine, sine, pair_raw, query_raw, pair_rows, query_rows
):
    core = pos[2]
    key, value = by_core(core, own[:, :HEAD_WIDTH], came[:, :HEAD_WIDTH])
    first, second = by_core(core, own[:, HEAD_WIDTH:], came[:, HEAD_WIDTH:])
    pair_raw[...] = key
    query_raw[0] = first
    query_raw[1] = second
    pair_rows[0] = rotate(key, key_gain[...], cosine[...], sine[...]).astype(BF)
    pair_rows[1] = value.astype(BF)
    query_rows[0] = rotate(first, query_gain[...], cosine[...], sine[...]).astype(BF)
    query_rows[1] = rotate(second, query_gain[...], cosine[...], sine[...]).astype(BF)


def rotate_all(pos, own, came, key_gain, query_gain, cosine, sine):
    pair = (2, ROWS, HEAD_WIDTH)
    return pl.pallas_call(
        rotate_all_body,
        in_specs=[SMEM] + [VMEM] * 6,
        out_specs=[VMEM] * 4,
        out_shape=[
            jax.ShapeDtypeStruct((ROWS, HEAD_WIDTH), F32),
            jax.ShapeDtypeStruct(pair, F32),
            jax.ShapeDtypeStruct(pair, BF),
            jax.ShapeDtypeStruct(pair, BF),
        ],
        compiler_params=params(),
        cost_estimate=cost(10_000_000, 3_000_000),
    )(pos, own, came, key_gain, query_gain, cosine, sine)


def load_band(nears, number, band, sems):
    copies = []
    for part, near in enumerate(nears):
        copy = pltpu.make_async_copy(
            near.at[number], band.at[pl.ds(part * ROWS, ROWS), :], sems.at[number, part]
        )
        copy.start()
        copies.append(copy)
    return copies


def attend_body(
    pos, queries, near0, near1, near2, cotangent, attended, grads0, grads1, grads2, score_grads,
    keys, values, values_turned, terms, weights, key_sums, value_sums, sems,
):
    nears = (near2, near1, near0)
    copies = load_band(nears, 0, keys, sems) + load_band(nears, 1, values, sems)
    for copy in copies:
        copy.wait()
    for part in range(3):
        rows = slice(part * ROWS, (part + 1) * ROWS)
        values_turned[:, rows] = values[rows].astype(F32).T.astype(BF)
    key_sums[...] = jnp.zeros_like(key_sums)
    value_sums[...] = jnp.zeros_like(value_sums)
    valid2 = (pos[3] >= 2).astype(F32)
    valid1 = (pos[3] >= 1).astype(F32)
    valid = (valid2, valid2, valid1, valid1, None, None)
    key_place = lax.broadcasted_iota(jnp.int32, (TILE, TILE), 0)
    query_place = lax.broadcasted_iota(jnp.int32, (TILE, TILE), 1)
    for head in range(2):
        columns = slice(head * HEAD_WIDTH, (head + 1) * HEAD_WIDTH)
        for tile in range(2):
            here = slice(tile * TILE, (tile + 1) * TILE)
            span = slice(tile * TILE, tile * TILE + SPAN)
            query = queries[head, here]
            out = cotangent[here, columns]
            total = jnp.zeros((1, TILE), F32)
            for block in range(5):
                low = block * TILE
                scores = dot(keys[tile * TILE + low : tile * TILE + low + TILE], query, 1, 1)
                term = jnp.exp(scores * SCORE_SCALE)
                if block == 0:
                    term = jnp.where(key_place > query_place, term, 0.0)
                if block == 4:
                    term = jnp.where(key_place <= query_place, term, 0.0)
                if valid[tile + block] is not None:
                    term = term * valid[tile + block]
                terms[low : low + TILE] = term
                total = total + jnp.sum(term, axis=0, keepdims=True)
            inverse = 1.0 / total
            for block in range(5):
                low = block * TILE
                weights[low : low + TILE] = (terms[low : low + TILE] * inverse).astype(BF)
            mixed = dot(values_turned[:, span], weights[...])
            rounded = mixed.astype(BF).astype(F32)
            attended[here, columns] = mixed.T.astype(BF)
            delta = jnp.sum(out.astype(F32).T * rounded, axis=0, keepdims=True)
            for block in range(5):
                low = block * TILE
                prob_grads = dot(values[tile * TILE + low : tile * TILE + low + TILE], out, 1, 1)
                probs = terms[low : low + TILE] * inverse
                score_grads[head, tile, low : low + TILE] = (probs * (prob_grads - delta)).astype(BF)
            key_sums[span] += dot(score_grads[head, tile], query)
            value_sums[span] += dot(weights[...], out)
    for part, ref in enumerate((grads2, grads1, grads0)):
        rows = slice(part * ROWS, (part + 1) * ROWS)
        ref[0] = (key_sums[rows] * SCORE_SCALE).astype(ref.dtype)
        ref[1] = value_sums[rows].astype(ref.dtype)


def attend(pos, queries, near0, near1, near2, cotangent):
    pair = (2, ROWS, HEAD_WIDTH)
    return pl.pallas_call(
        attend_body,
        in_specs=[SMEM, VMEM] + [ANY] * 3 + [VMEM],
        out_specs=[VMEM] * 5,
        out_shape=[
            jax.ShapeDtypeStruct((ROWS, 2 * HEAD_WIDTH), BF),
            jax.ShapeDtypeStruct(pair, F32),
            jax.ShapeDtypeStruct(pair, BF),
            jax.ShapeDtypeStruct(pair, BF),
            jax.ShapeDtypeStruct((2, 2, SPAN, TILE), BF),
        ],
        scratch_shapes=[
            pltpu.VMEM((BAND, HEAD_WIDTH), BF),
            pltpu.VMEM((BAND, HEAD_WIDTH), BF),
            pltpu.VMEM((HEAD_WIDTH, BAND), BF),
            pltpu.VMEM((SPAN, TILE), F32),
            pltpu.VMEM((SPAN, TILE), BF),
            pltpu.VMEM((BAND, HEAD_WIDTH), F32),
            pltpu.VMEM((BAND, HEAD_WIDTH), F32),
            pltpu.SemaphoreType.DMA((2, 3)),
        ],
        compiler_params=params(),
        cost_estimate=cost(8_000_000_000, 8_000_000),
    )(pos, queries, near0, near1, near2, cotangent)


def query_back_body(
    score_grads, near0, near1, near2, raw, gain, cosine, sine, back, keys, keys_turned, sems
):
    for copy in load_band((near2, near1, near0), 0, keys, sems):
        copy.wait()
    for part in range(3):
        rows = slice(part * ROWS, (part + 1) * ROWS)
        keys_turned[:, rows] = keys[rows].astype(F32).T.astype(BF)
    for head in range(2):
        for tile in range(2):
            here = slice(tile * TILE, (tile + 1) * TILE)
            grads = dot(keys_turned[:, tile * TILE : tile * TILE + SPAN], score_grads[head, tile])
            grads = (grads * SCORE_SCALE).T
            back[head, here] = rotate_back(
                raw[head, here], grads, gain[...], cosine[here], sine[here]
            )


def query_back(score_grads, near0, near1, near2, raw, gain, cosine, sine):
    return pl.pallas_call(
        query_back_body,
        in_specs=[VMEM] + [ANY] * 3 + [VMEM] * 4,
        out_specs=VMEM,
        out_shape=jax.ShapeDtypeStruct((2, ROWS, HEAD_WIDTH), F32),
        scratch_shapes=[
            pltpu.VMEM((BAND, HEAD_WIDTH), BF),
            pltpu.VMEM((HEAD_WIDTH, BAND), BF),
            pltpu.SemaphoreType.DMA((1, 3)),
        ],
        compiler_params=params(),
        cost_estimate=cost(1_000_000_000, 4_000_000),
    )(score_grads, near0, near1, near2, raw, gain, cosine, sine)


def all_back_body(
    pos, own, from1, from2, raw, gain, cosine, sine, query_part, kept, sent, turned
):
    core = pos[2]
    grads = own[...] + from1[...].astype(F32) + from2[...].astype(F32)
    key_part = rotate_back(raw[...], grads[0], gain[...], cosine[...], sine[...])
    mine, other = by_core(core, key_part, grads[1])
    kept[:, :HEAD_WIDTH] = mine.astype(BF)
    sent[:, :HEAD_WIDTH] = other.astype(BF)
    turned[:HEAD_WIDTH] = mine.T.astype(BF)
    turned[WIDE : WIDE + HEAD_WIDTH] = other.T.astype(BF)
    mine, other = by_core(core, query_part[0], query_part[1])
    kept[:, HEAD_WIDTH:] = mine.astype(BF)
    sent[:, HEAD_WIDTH:] = other.astype(BF)
    turned[HEAD_WIDTH:WIDE] = mine.T.astype(BF)
    turned[WIDE + HEAD_WIDTH :] = other.T.astype(BF)


def all_back(pos, own, from1, from2, raw, gain, cosine, sine, query_part):
    return pl.pallas_call(
        all_back_body,
        in_specs=[SMEM] + [VMEM] * 8,
        out_specs=[VMEM] * 3,
        out_shape=[
            jax.ShapeDtypeStruct((ROWS, WIDE), BF),
            jax.ShapeDtypeStruct((ROWS, WIDE), BF),
            jax.ShapeDtypeStruct((2 * WIDE, ROWS), BF),
        ],
        compiler_params=params(),
        cost_estimate=cost(10_000_000, 3_000_000),
    )(pos, own, from1, from2, raw, gain, cosine, sine, query_part)


def weight_terms_body(pos, tokens, other_tokens, back, other_back, mine, far_up, far_down, terms):
    step = pl.program_id(0)
    z, y = pos[0], pos[1]
    rows = pl.ds(pl.multiple_of(step * (DEPTH // 2), DEPTH // 2), DEPTH // 2)
    terms[rows, :] = (
        dot(tokens[...], back[...], 0, 0) + dot(other_tokens[...], other_back[...], 0, 0)
    ).astype(BF)

    @pl.when(step == 1)
    def spread():
        for z_offset in range(8):
            start = lax.rem(z + z_offset, 8) * PART
            same = pl.ds(pl.multiple_of(start + y * BLOCK, 16), BLOCK)
            other = pl.ds(pl.multiple_of(start + (1 - y) * BLOCK, 16), BLOCK)
            if z_offset == 4:
                far_up[...] = terms[same, :]
                far_down[...] = terms[other, :]
            else:
                mine[z_offset, 0] = terms[same, :]
                mine[z_offset, 1] = terms[other, :]


def weight_terms(pos, tokens, other_tokens, back, other_back):
    whole = lambda shape: pl.BlockSpec(shape, lambda k: (0,) * len(shape))
    shapes = [(8, 2, BLOCK, WIDE), (BLOCK, WIDE), (BLOCK, WIDE)]
    return pl.pallas_call(
        weight_terms_body,
        grid=(2,),
        in_specs=[
            SMEM,
            pl.BlockSpec((ROWS, DEPTH // 2), lambda k: (0, k)),
            pl.BlockSpec((ROWS, DEPTH // 2), lambda k: (0, k)),
            whole((ROWS, WIDE)),
            whole((ROWS, WIDE)),
        ],
        out_specs=[whole(shape) for shape in shapes],
        out_shape=[jax.ShapeDtypeStruct(shape, BF) for shape in shapes],
        scratch_shapes=[pltpu.VMEM((DEPTH, WIDE), BF)],
        compiler_params=params(),
        cost_estimate=cost(4 * ROWS * DEPTH * 256, 17_000_000),
    )(pos, tokens, other_tokens, back, other_back)


def token_terms(owners, weights, other_weights, turned, body, extras, shapes, after=()):
    count = owners.shape[0]
    whole = lambda shape: pl.BlockSpec(shape, lambda k, order: (0,) * len(shape))

    def window(number):
        return pl.BlockSpec((PART, WIDE), lambda k, order: (order[number], 0))

    def run(order, *refs):
        turned_ref = refs[2 * count]
        rest = refs[2 * count + 1 :]

        def term(number):
            return dot(refs[number][...], turned_ref[:WIDE]) + dot(
                refs[count + number][...], turned_ref[WIDE:]
            )

        body(term, rest[: len(extras)], rest[len(extras) + len(after) :])

    windows = [window(number) for number in range(count)]
    return pl.pallas_call(
        run,
        grid_spec=pltpu.PrefetchScalarGridSpec(
            num_scalar_prefetch=1,
            grid=(1,),
            in_specs=windows
            + windows
            + [whole((2 * WIDE, ROWS))]
            + [whole(extra.shape) for extra in extras]
            + [ANY] * len(after),
            out_specs=[whole(shape) for shape in shapes],
        ),
        out_shape=[jax.ShapeDtypeStruct(shape, BF) for shape in shapes],
        compiler_params=params(),
        cost_estimate=cost(2 * PART * ROWS * 512 * count, 1_500_000 * count),
    )(owners, *[weights] * count, *[other_weights] * count, turned, *extras, *after)


def combine(body, arrays, shapes, after=()):
    count = len(arrays)
    specs, operands = [], []
    for entry in arrays:
        if isinstance(entry, tuple):
            array, number = entry
            shape = (1,) + array.shape[1:]
            specs.append(pl.BlockSpec(shape, lambda k, number=number: (number, 0, 0, 0)))
        else:
            array = entry
            specs.append(SMEM if array.dtype == jnp.int32 else VMEM)
        operands.append(array)

    def run(*refs):
        body(refs[:count], refs[count + len(after) :])

    return pl.pallas_call(
        run,
        grid=(1,),
        in_specs=specs + [ANY] * len(after),
        out_specs=[VMEM] * len(shapes),
        out_shape=[jax.ShapeDtypeStruct(shape, BF) for shape in shapes],
        compiler_params=params(),
        cost_estimate=cost(1_000_000, 2_000_000),
    )(*operands, *after)


def wide(ref):
    return ref[...].astype(F32)


def chip_shard(halves, core):
    kept = jnp.where(core == 0, halves[0], halves[1])
    came = swap_core(jnp.where(core == 0, halves[1], halves[0]))
    return jnp.concatenate(
        [jnp.where(core == 0, kept, came), jnp.where(core == 0, came, kept)], axis=0
    )


def gather(shard, tokens, late):
    barrier = lax.optimization_barrier
    up1, down1, near = up_z(shard), down_z(shard), swap_y(shard)
    up1, down1, near, tokens = barrier((up1, down1, near, tokens))
    other_tokens = swap_core(tokens)
    up2, down2, near_up1, near_down1 = up_z(up1), down_z(down1), swap_y(up1), swap_y(down1)
    up2, down2, near_up1, near_down1 = barrier((up2, down2, near_up1, near_down1))
    up3, down3, near_up2, near_down2 = up_z(up2), down_z(down2), swap_y(up2), swap_y(down2)
    up3, down3, near_up2, near_down2, other_tokens, late = barrier(
        (up3, down3, near_up2, near_down2, other_tokens, late)
    )
    up4, down4 = up_z(up3[:, :HEAD_WIDTH]), down_z(down3[:, HEAD_WIDTH:])
    near_up3, near_down3 = up_z(near_up2), down_z(near_down2)
    arrivals = (
        (shard, near, 0, 0),
        (up1, near_up1, 7, 0),
        (down1, near_down1, 1, 0),
        (up2, near_up2, 6, 0),
        (down2, near_down2, 2, 0),
        (up3, near_up3, 5, 0),
        (down3, near_down3, 3, 0),
        (up4, swap_y(up4), 4, 0),
        (down4, swap_y(down4), 4, HEAD_WIDTH),
    )
    entries = []
    for same, other, z_offset, column in arrivals:
        entries += [(same, z_offset, 0, column), (other, z_offset, 1, column)]
    return entries, other_tokens, late


def shards(tokens, query_weight, key_matrix, value_matrix, query_gain, key_norm_gain, cotangent):
    ctx = lax.axis_index("ctx")
    tp = lax.axis_index("tp")
    z, y, core = ctx // 4, (ctx // 2) % 2, ctx % 2
    pos = jnp.stack([z, y, core, ctx]).astype(jnp.int32)
    token_positions = (ctx * ROWS + jnp.arange(ROWS, dtype=jnp.int32)).astype(F32)
    inverse = jnp.power(
        F32(rope_base), -jnp.arange(0, HEAD_WIDTH, 2).astype(F32) / HEAD_WIDTH
    )
    angles = token_positions[:, None] * inverse[None, :]
    cosine, sine = jnp.cos(angles), jnp.sin(angles)
    cosine = jnp.concatenate([cosine, cosine], axis=1)
    sine = jnp.concatenate([-sine, sine], axis=1)
    query_gain = query_gain.reshape(1, HEAD_WIDTH)
    key_gain = key_norm_gain.reshape(1, HEAD_WIDTH)

    shard = chip_shard(
        [
            jnp.concatenate([key_matrix, query_weight[:, :HEAD_WIDTH]], axis=1),
            jnp.concatenate([value_matrix, query_weight[:, HEAD_WIDTH:]], axis=1),
        ],
        core,
    )
    entries, other_tokens, (cosine, sine) = gather(shard, tokens, (cosine, sine))
    own_raw, sent_raw, weights = project(pos, tokens, other_tokens, entries)
    came_raw, weights_later = lax.optimization_barrier((swap_core(sent_raw), weights))
    pair_raw, query_raw, near0, queries = rotate_all(
        pos, own_raw, came_raw, key_gain, query_gain, cosine, sine
    )
    other_weights = swap_core(weights_later)
    near1, near2 = passed_along(near0, 1), passed_along(near0, 2)
    attended, grads0, grads1, grads2, score_grads = attend(
        pos, queries, near0, near1, near2, cotangent
    )
    from2, from1 = passed_along(grads2, -2), passed_along(grads1, -1)
    query_part = query_back(
        score_grads, near0, near1, near2, query_raw, query_gain, cosine, sine
    )
    kept, sent, turned = all_back(
        pos, grads0, from1, from2, pair_raw, key_gain, cosine, sine, query_part
    )
    other_back = swap_core(sent)

    def owners(*offsets):
        return jnp.stack(
            [(tp // 2 + i) % X_SIZE * 2 + (tp % 2 + j) % 2 for i, j in offsets]
        ).astype(jnp.int32)

    half = ROWS // 2
    token_shape = (PART, ROWS)
    terms = functools.partial(token_terms, weights=weights, other_weights=other_weights, turned=turned)

    def farthest(term, ins, outs):
        for number in range(2):
            part = term(number).astype(BF)
            outs[0][number] = part[:, :half]
            outs[1][number] = part[:, half:]

    def joined(far_offset):
        def body(term, ins, outs):
            part = term(0)
            outs[0][:, :half] = (part[:, :half] + ins[0][far_offset].astype(F32)).astype(BF)
            outs[0][:, half:] = part[:, half:].astype(BF)
            part = term(1)
            outs[1][:, :half] = part[:, :half].astype(BF)
            outs[1][:, half:] = (part[:, half:] + ins[1][far_offset].astype(F32)).astype(BF)

        return body

    def to_far(term, ins, outs):
        outs[0][...] = (term(0) + wide(ins[0]) + wide(ins[1])).astype(BF)

    def token_result(term, ins, outs):
        outs[0][...] = (term(0) + wide(ins[0]) + wide(ins[1]) + wide(ins[2])).astype(BF)

    def second_step(ins, outs):
        upper, lower, up, down = ins
        outs[0][0] = (upper[0, 0].astype(F32) + wide(up)).astype(BF)
        outs[0][1] = upper[0, 1]
        outs[1][0] = lower[0, 0]
        outs[1][1] = (lower[0, 1].astype(F32) + wide(down)).astype(BF)

    def later_step(ins, outs):
        upper, lower, up, down = ins
        outs[0][...] = (upper[0].astype(F32) + wide(up)).astype(BF)
        outs[1][...] = (lower[0].astype(F32) + wide(down)).astype(BF)

    def last_step(ins, outs):
        own, up, down = ins
        total = own[0].astype(F32) + wide(up) + wide(down)
        outs[0][...] = total[0].astype(BF)
        outs[1][...] = total[1].astype(BF)

    def near_sum(ins, outs):
        total = wide(ins[1]) + wide(ins[2])
        first, second = by_core(ins[0][2], total[: BLOCK // 2], total[BLOCK // 2 :])
        outs[0][...] = first.astype(BF)
        outs[1][...] = second.astype(BF)

    def to_outputs(ins, outs):
        first, second = by_core(ins[0][2], wide(ins[1]), wide(ins[2]))
        outs[0][:, :HEAD_WIDTH] = first[:, HEAD_WIDTH:].astype(BF)
        outs[0][:, HEAD_WIDTH:] = second[:, HEAD_WIDTH:].astype(BF)
        outs[1][...] = first[:, :HEAD_WIDTH].astype(BF)
        outs[2][...] = second[:, :HEAD_WIDTH].astype(BF)

    block, both = (BLOCK, WIDE), (2, BLOCK, WIDE)
    far_a, far_b = terms(
        owners((2, 0), (2, 1)), body=farthest, extras=(), shapes=[(2, PART, half)] * 2
    )
    token_up, token_down = up_x(far_a), down_x(far_b)
    mine, far_up, far_down = weight_terms(pos, tokens, other_tokens, kept, other_back)
    up, down = up_z(far_up), down_z(far_down)
    arrived = (token_up, token_down)
    z2 = combine(second_step, ((mine, 3), (mine, 5), up, down), [both] * 2)
    up, down = up_z(z2[0]), down_z(z2[1])
    x1 = terms(
        owners((1, 1), (3, 1)),
        body=joined(1),
        extras=arrived,
        shapes=[token_shape] * 2,
        after=(z2[0],),
    )
    got_up1, got_down1 = up_x(x1[0]), down_x(x1[1])
    x2 = terms(
        owners((1, 0), (3, 0)),
        body=joined(0),
        extras=arrived,
        shapes=[token_shape] * 2,
        after=(x1[0],),
    )
    got_up0, got_down0 = up_x(x2[0]), down_x(x2[1])
    z3 = combine(later_step, ((mine, 2), (mine, 6), up, down), [both] * 2, (x2[0],))
    up, down = up_z(z3[0]), down_z(z3[1])
    (x3,) = terms(
        owners((0, 1)),
        body=to_far,
        extras=(got_up1, got_down1),
        shapes=[token_shape],
        after=(z3[0],),
    )
    far = swap_far(x3)
    z4 = combine(later_step, ((mine, 1), (mine, 7), up, down), [both] * 2, (x3,))
    up, down = up_z(z4[0]), down_z(z4[1])
    chip_kept, chip_sent = combine(last_step, ((mine, 0), up, down), [block] * 2)
    chip_came = swap_y(chip_sent)
    (token_sum,) = terms(
        owners((0, 0)),
        body=token_result,
        extras=(got_up0, got_down0, far),
        shapes=[token_shape],
        after=(chip_sent,),
    )
    rows = (BLOCK // 2, WIDE)
    row_kept, row_sent = combine(near_sum, (pos, chip_kept, chip_came), [rows] * 2)
    narrow = (BLOCK // 2, HEAD_WIDTH)
    query_gradient, key_gradient, value_gradient = combine(
        to_outputs, (pos, row_kept, swap_core(row_sent)), [rows, narrow, narrow], (token_sum,)
    )
    return (attended, token_sum.T, query_gradient, key_gradient, value_gradient)


def solution(mesh):
    in_specs = (
        P("ctx", None),
        P("ctx", "tp"),
        P("ctx", "tp"),
        P("ctx", "tp"),
        P(),
        P(),
        P("ctx", "tp"),
    )
    out_specs = (P("ctx", "tp"), P("ctx", "tp"), P("ctx", "tp"), P("ctx", "tp"), P("ctx", "tp"))
    return jax.shard_map(shards, mesh=mesh, in_specs=in_specs, out_specs=out_specs, check_vma=False)
```

```python
import functools

import jax
import jax.numpy as jnp
from jax import lax
from jax.experimental import pallas as pl
from jax.experimental.pallas import tpu as pltpu
from jax.sharding import PartitionSpec as P

HEAD_WIDTH = 128
WINDOW_LENGTH = 1024
QUERY_SCALAR = 168
SCORE_SCALE = QUERY_SCALAR ** (-0.5)

rope_base = 10000.0
norm_eps = 1e-06

Z_SIZE = 8
X_SIZE = 4
ROWS = 512
TILE = 256
SPAN = WINDOW_LENGTH + TILE
BAND = WINDOW_LENGTH + ROWS
DEPTH = 5376
VMEM_MEBIBYTES = 50
BLOCK = 336
PART = 672
BF = jnp.bfloat16
F32 = jnp.float32


def along_z(step):
    return [(i, ((i // 4 + step) % Z_SIZE) * 4 + i % 4) for i in range(4 * Z_SIZE)]


def along_x(step):
    return [(i, ((i // 2 + step) % X_SIZE) * 2 + i % 2) for i in range(2 * X_SIZE)]


SIBLING = [(i, i ^ 1) for i in range(32)]
NEAR_Y = [(i, i ^ 2) for i in range(32)]
FAR_Y = [(i, i ^ 1) for i in range(8)]


def up_z(piece):
    return lax.ppermute(piece, "ctx", along_z(1))


def down_z(piece):
    return lax.ppermute(piece, "ctx", along_z(-1))


def swap_y(piece):
    return lax.ppermute(piece, "ctx", NEAR_Y)


def swap_core(piece):
    return lax.ppermute(piece, "ctx", SIBLING)


def up_x(piece):
    return lax.ppermute(piece, "tp", along_x(1))


def down_x(piece):
    return lax.ppermute(piece, "tp", along_x(-1))


def swap_far(piece):
    return lax.ppermute(piece, "tp", FAR_Y)


def passed_along(shard, by):
    pairs = [(i, i + by) for i in range(32) if 0 <= i + by < 32]
    return lax.ppermute(shard, "ctx", pairs)


def summed(*terms):
    total = terms[0].astype(F32)
    for term in terms[1:]:
        total = total + term.astype(F32)
    return total.astype(BF)


def dot(left, right, left_axis=1, right_axis=0):
    return lax.dot_general(
        left, right, (((left_axis,), (right_axis,)), ((), ())), preferred_element_type=F32
    )


def params(mebibytes=VMEM_MEBIBYTES):
    return pltpu.CompilerParams(vmem_limit_bytes=mebibytes * 1024 * 1024)


def cost(flops, moved):
    return pl.CostEstimate(flops=flops, bytes_accessed=moved, transcendentals=0)


VMEM = pl.BlockSpec(memory_space=pltpu.VMEM)
ANY = pl.BlockSpec(memory_space=pl.ANY)
SMEM = pl.BlockSpec(memory_space=pltpu.SMEM)


def rotate(raw, gain, cosine, sine):
    scale = lax.rsqrt(jnp.mean(raw * raw, axis=-1, keepdims=True) + norm_eps)
    normed = raw * scale * gain
    return normed * cosine + pltpu.roll(normed, HEAD_WIDTH // 2, 1) * sine


def rotate_back(raw, grads, gain, cosine, sine):
    scale = lax.rsqrt(jnp.mean(raw * raw, axis=-1, keepdims=True) + norm_eps)
    turned = (grads * cosine - pltpu.roll(grads, HEAD_WIDTH // 2, 1) * sine) * gain
    inner = jnp.mean(raw * turned, axis=-1, keepdims=True)
    return turned * scale - raw * (scale * scale * scale * inner)


DEPTH_STEPS = 3
DEPTH_STEP = DEPTH // DEPTH_STEPS
WIDE = 2 * HEAD_WIDTH


def by_core(core, first, second):
    return jnp.where(core == 0, first, second), jnp.where(core == 0, second, first)


def project_body(places, pos, tokens, other_tokens, *refs):
    count = len(places)
    pieces = refs[:count]
    own, sent, kept, weights, total, sems, out_sem = refs[count:]
    step = pl.program_id(0)
    z, y = pos[0], pos[1]

    @pl.when(step == 0)
    def place():
        copies = []
        for number, (z_offset, y_offset, column, width) in enumerate(places):
            block = lax.rem(z + z_offset, 8) * 2 + lax.rem(y + y_offset, 2)
            start = pl.multiple_of(block * BLOCK, 16)
            copies.append(
                pltpu.make_async_copy(
                    pieces[number],
                    weights.at[pl.ds(start, BLOCK), pl.ds(column, width)],
                    sems.at[number],
                )
            )
        for copy in copies:
            copy.start()
        for copy in copies:
            copy.wait()
        pltpu.make_async_copy(weights, kept, out_sem).start()
        total[...] = jnp.zeros_like(total)

    start = pl.multiple_of(step * DEPTH_STEP, DEPTH_STEP)
    both = jnp.concatenate([tokens[...], other_tokens[...]], axis=0)
    total[...] += dot(both, weights[pl.ds(start, DEPTH_STEP), :])

    @pl.when(step == DEPTH_STEPS - 1)
    def finish():
        own[...] = total[:ROWS]
        sent[...] = total[ROWS:]
        pltpu.make_async_copy(weights, kept, out_sem).wait()


def project(pos, tokens, other_tokens, entries):
    places = tuple((e[1], e[2], e[3], e[0].shape[1]) for e in entries)
    whole = lambda shape: pl.BlockSpec(shape, lambda k: (0,) * len(shape))
    return pl.pallas_call(
        functools.partial(project_body, places),
        grid=(DEPTH_STEPS,),
        in_specs=[SMEM] + [pl.BlockSpec((ROWS, DEPTH_STEP), lambda k: (0, k))] * 2 + [ANY] * len(entries),
        out_specs=[whole((ROWS, WIDE)), whole((ROWS, WIDE)), ANY],
        out_shape=[
            jax.ShapeDtypeStruct((ROWS, WIDE), F32),
            jax.ShapeDtypeStruct((ROWS, WIDE), F32),
            jax.ShapeDtypeStruct((DEPTH, WIDE), BF),
        ],
        scratch_shapes=[
            pltpu.VMEM((DEPTH, WIDE), BF),
            pltpu.VMEM((2 * ROWS, WIDE), F32),
            pltpu.SemaphoreType.DMA((len(entries),)),
            pltpu.SemaphoreType.DMA,
        ],
        compiler_params=params(),
        cost_estimate=cost(2 * ROWS * DEPTH * 512, 17_000_000),
    )(pos, tokens, other_tokens, *[e[0] for e in entries])


def rotate_all_body(
    pos, own, came, key_gain, query_gain, cosine, sine, pair_raw, query_raw, pair_rows, query_rows
):
    core = pos[2]
    key, value = by_core(core, own[:, :HEAD_WIDTH], came[:, :HEAD_WIDTH])
    first, second = by_core(core, own[:, HEAD_WIDTH:], came[:, HEAD_WIDTH:])
    pair_raw[...] = key
    query_raw[0] = first
    query_raw[1] = second
    pair_rows[0] = rotate(key, key_gain[...], cosine[...], sine[...]).astype(BF)
    pair_rows[1] = value.astype(BF)
    query_rows[0] = rotate(first, query_gain[...], cosine[...], sine[...]).astype(BF)
    query_rows[1] = rotate(second, query_gain[...], cosine[...], sine[...]).astype(BF)


def rotate_all(pos, own, came, key_gain, query_gain, cosine, sine):
    pair = (2, ROWS, HEAD_WIDTH)
    return pl.pallas_call(
        rotate_all_body,
        in_specs=[SMEM] + [VMEM] * 6,
        out_specs=[VMEM] * 4,
        out_shape=[
            jax.ShapeDtypeStruct((ROWS, HEAD_WIDTH), F32),
            jax.ShapeDtypeStruct(pair, F32),
            jax.ShapeDtypeStruct(pair, BF),
            jax.ShapeDtypeStruct(pair, BF),
        ],
        compiler_params=params(),
        cost_estimate=cost(10_000_000, 3_000_000),
    )(pos, own, came, key_gain, query_gain, cosine, sine)


def load_band(nears, number, band, sems):
    copies = []
    for part, near in enumerate(nears):
        copy = pltpu.make_async_copy(
            near.at[number], band.at[pl.ds(part * ROWS, ROWS), :], sems.at[number, part]
        )
        copy.start()
        copies.append(copy)
    return copies


def attend_body(
    pos, queries, near0, near1, near2, cotangent, attended, grads0, grads1, grads2, score_grads,
    keys, values, values_turned, terms, weights, key_sums, value_sums, sems,
):
    nears = (near2, near1, near0)
    key_copies, value_copies = load_band(nears, 0, keys, sems), load_band(nears, 1, values, sems)
    for copy in key_copies:
        copy.wait()
    key_sums[...] = jnp.zeros_like(key_sums)
    value_sums[...] = jnp.zeros_like(value_sums)
    valid2 = (pos[3] >= 2).astype(F32)
    valid1 = (pos[3] >= 1).astype(F32)
    valid = (valid2, valid2, valid1, valid1, None, None)
    key_place = lax.broadcasted_iota(jnp.int32, (TILE, TILE), 0)
    query_place = lax.broadcasted_iota(jnp.int32, (TILE, TILE), 1)
    for head in range(2):
        columns = slice(head * HEAD_WIDTH, (head + 1) * HEAD_WIDTH)
        for tile in range(2):
            here = slice(tile * TILE, (tile + 1) * TILE)
            span = slice(tile * TILE, tile * TILE + SPAN)
            query = queries[head, here]
            out = cotangent[here, columns]
            total = jnp.zeros((1, TILE), F32)
            for block in range(5):
                low = block * TILE
                scores = dot(keys[tile * TILE + low : tile * TILE + low + TILE], query, 1, 1)
                term = jnp.exp(scores * SCORE_SCALE)
                if block == 0:
                    term = jnp.where(key_place > query_place, term, 0.0)
                if block == 4:
                    term = jnp.where(key_place <= query_place, term, 0.0)
                if valid[tile + block] is not None:
                    term = term * valid[tile + block]
                terms[low : low + TILE] = term
                total = total + jnp.sum(term, axis=0, keepdims=True)
            inverse = 1.0 / total
            for block in range(5):
                low = block * TILE
                weights[low : low + TILE] = (terms[low : low + TILE] * inverse).astype(BF)
            if head == 0 and tile == 0:
                for copy in value_copies:
                    copy.wait()
                for part in range(3):
                    rows = slice(part * ROWS, (part + 1) * ROWS)
                    values_turned[:, rows] = values[rows].astype(F32).T.astype(BF)
            mixed = dot(values_turned[:, span], weights[...])
            rounded = mixed.astype(BF).astype(F32)
            attended[here, columns] = mixed.T.astype(BF)
            delta = jnp.sum(out.astype(F32).T * rounded, axis=0, keepdims=True)
            for block in range(5):
                low = block * TILE
                prob_grads = dot(values[tile * TILE + low : tile * TILE + low + TILE], out, 1, 1)
                probs = terms[low : low + TILE] * inverse
                score_grads[head, tile, low : low + TILE] = (probs * (prob_grads - delta)).astype(BF)
            key_sums[span] += dot(score_grads[head, tile], query)
            value_sums[span] += dot(weights[...], out)
    for part, ref in enumerate((grads2, grads1, grads0)):
        rows = slice(part * ROWS, (part + 1) * ROWS)
        ref[0] = (key_sums[rows] * SCORE_SCALE).astype(ref.dtype)
        ref[1] = value_sums[rows].astype(ref.dtype)


def attend(pos, queries, near0, near1, near2, cotangent):
    pair = (2, ROWS, HEAD_WIDTH)
    return pl.pallas_call(
        attend_body,
        in_specs=[SMEM, VMEM] + [ANY] * 3 + [VMEM],
        out_specs=[VMEM] * 5,
        out_shape=[
            jax.ShapeDtypeStruct((ROWS, 2 * HEAD_WIDTH), BF),
            jax.ShapeDtypeStruct(pair, F32),
            jax.ShapeDtypeStruct(pair, BF),
            jax.ShapeDtypeStruct(pair, BF),
            jax.ShapeDtypeStruct((2, 2, SPAN, TILE), BF),
        ],
        scratch_shapes=[
            pltpu.VMEM((BAND, HEAD_WIDTH), BF),
            pltpu.VMEM((BAND, HEAD_WIDTH), BF),
            pltpu.VMEM((HEAD_WIDTH, BAND), BF),
            pltpu.VMEM((SPAN, TILE), F32),
            pltpu.VMEM((SPAN, TILE), BF),
            pltpu.VMEM((BAND, HEAD_WIDTH), F32),
            pltpu.VMEM((BAND, HEAD_WIDTH), F32),
            pltpu.SemaphoreType.DMA((2, 3)),
        ],
        compiler_params=params(),
        cost_estimate=cost(8_000_000_000, 8_000_000),
    )(pos, queries, near0, near1, near2, cotangent)


def query_back_body(
    score_grads, near0, near1, near2, raw, gain, cosine, sine, back, keys, keys_turned, sems
):
    for copy in load_band((near2, near1, near0), 0, keys, sems):
        copy.wait()
    for part in range(3):
        rows = slice(part * ROWS, (part + 1) * ROWS)
        keys_turned[:, rows] = keys[rows].astype(F32).T.astype(BF)
    for head in range(2):
        for tile in range(2):
            here = slice(tile * TILE, (tile + 1) * TILE)
            grads = dot(keys_turned[:, tile * TILE : tile * TILE + SPAN], score_grads[head, tile])
            grads = (grads * SCORE_SCALE).T
            back[head, here] = rotate_back(
                raw[head, here], grads, gain[...], cosine[here], sine[here]
            )


def query_back(score_grads, near0, near1, near2, raw, gain, cosine, sine):
    return pl.pallas_call(
        query_back_body,
        in_specs=[VMEM] + [ANY] * 3 + [VMEM] * 4,
        out_specs=VMEM,
        out_shape=jax.ShapeDtypeStruct((2, ROWS, HEAD_WIDTH), F32),
        scratch_shapes=[
            pltpu.VMEM((BAND, HEAD_WIDTH), BF),
            pltpu.VMEM((HEAD_WIDTH, BAND), BF),
            pltpu.SemaphoreType.DMA((1, 3)),
        ],
        compiler_params=params(),
        cost_estimate=cost(1_000_000_000, 4_000_000),
    )(score_grads, near0, near1, near2, raw, gain, cosine, sine)


def all_back_body(
    pos, own, from1, from2, raw, gain, cosine, sine, query_part, kept, sent, turned
):
    core = pos[2]
    grads = own[...] + from1[...].astype(F32) + from2[...].astype(F32)
    key_part = rotate_back(raw[...], grads[0], gain[...], cosine[...], sine[...])
    mine, other = by_core(core, key_part, grads[1])
    kept[:, :HEAD_WIDTH] = mine.astype(BF)
    sent[:, :HEAD_WIDTH] = other.astype(BF)
    turned[:HEAD_WIDTH] = mine.T.astype(BF)
    turned[WIDE : WIDE + HEAD_WIDTH] = other.T.astype(BF)
    mine, other = by_core(core, query_part[0], query_part[1])
    kept[:, HEAD_WIDTH:] = mine.astype(BF)
    sent[:, HEAD_WIDTH:] = other.astype(BF)
    turned[HEAD_WIDTH:WIDE] = mine.T.astype(BF)
    turned[WIDE + HEAD_WIDTH :] = other.T.astype(BF)


def all_back(pos, own, from1, from2, raw, gain, cosine, sine, query_part):
    return pl.pallas_call(
        all_back_body,
        in_specs=[SMEM] + [VMEM] * 8,
        out_specs=[VMEM] * 3,
        out_shape=[
            jax.ShapeDtypeStruct((ROWS, WIDE), BF),
            jax.ShapeDtypeStruct((ROWS, WIDE), BF),
            jax.ShapeDtypeStruct((2 * WIDE, ROWS), BF),
        ],
        compiler_params=params(),
        cost_estimate=cost(10_000_000, 3_000_000),
    )(pos, own, from1, from2, raw, gain, cosine, sine, query_part)


def weight_terms_body(pos, tokens, other_tokens, back, other_back, mine, far_up, far_down, terms):
    step = pl.program_id(0)
    z, y = pos[0], pos[1]
    rows = pl.ds(pl.multiple_of(step * (DEPTH // 2), DEPTH // 2), DEPTH // 2)
    terms[rows, :] = (
        dot(tokens[...], back[...], 0, 0) + dot(other_tokens[...], other_back[...], 0, 0)
    ).astype(BF)

    @pl.when(step == 1)
    def spread():
        for z_offset in range(8):
            start = lax.rem(z + z_offset, 8) * PART
            same = pl.ds(pl.multiple_of(start + y * BLOCK, 16), BLOCK)
            other = pl.ds(pl.multiple_of(start + (1 - y) * BLOCK, 16), BLOCK)
            if z_offset == 4:
                far_up[...] = terms[same, :]
                far_down[...] = terms[other, :]
            else:
                mine[z_offset, 0] = terms[same, :]
                mine[z_offset, 1] = terms[other, :]


def weight_terms(pos, tokens, other_tokens, back, other_back):
    whole = lambda shape: pl.BlockSpec(shape, lambda k: (0,) * len(shape))
    shapes = [(8, 2, BLOCK, WIDE), (BLOCK, WIDE), (BLOCK, WIDE)]
    return pl.pallas_call(
        weight_terms_body,
        grid=(2,),
        in_specs=[
            SMEM,
            pl.BlockSpec((ROWS, DEPTH // 2), lambda k: (0, k)),
            pl.BlockSpec((ROWS, DEPTH // 2), lambda k: (0, k)),
            whole((ROWS, WIDE)),
            whole((ROWS, WIDE)),
        ],
        out_specs=[whole(shape) for shape in shapes],
        out_shape=[jax.ShapeDtypeStruct(shape, BF) for shape in shapes],
        scratch_shapes=[pltpu.VMEM((DEPTH, WIDE), BF)],
        compiler_params=params(),
        cost_estimate=cost(4 * ROWS * DEPTH * 256, 17_000_000),
    )(pos, tokens, other_tokens, back, other_back)


def token_terms(owners, weights, other_weights, turned, body, extras, shapes, after=()):
    count = owners.shape[0]
    whole = lambda shape: pl.BlockSpec(shape, lambda k, order: (0,) * len(shape))

    def extra_spec(extra):
        if isinstance(extra, tuple):
            array, number = extra
            return pl.BlockSpec((1,) + array.shape[1:], lambda k, order: (number, 0, 0))
        return whole(extra.shape)

    arrays = [extra[0] if isinstance(extra, tuple) else extra for extra in extras]

    def window(number):
        return pl.BlockSpec((PART, WIDE), lambda k, order: (order[number], 0))

    def run(order, *refs):
        turned_ref = refs[2 * count]
        rest = refs[2 * count + 1 :]

        def term(number):
            return dot(refs[number][...], turned_ref[:WIDE]) + dot(
                refs[count + number][...], turned_ref[WIDE:]
            )

        body(term, rest[: len(extras)], rest[len(extras) + len(after) :])

    windows = [window(number) for number in range(count)]
    return pl.pallas_call(
        run,
        grid_spec=pltpu.PrefetchScalarGridSpec(
            num_scalar_prefetch=1,
            grid=(1,),
            in_specs=windows
            + windows
            + [whole((2 * WIDE, ROWS))]
            + [extra_spec(extra) for extra in extras]
            + [ANY] * len(after),
            out_specs=[whole(shape) for shape in shapes],
        ),
        out_shape=[jax.ShapeDtypeStruct(shape, BF) for shape in shapes],
        compiler_params=params(),
        cost_estimate=cost(2 * PART * ROWS * 512 * count, 1_500_000 * count),
    )(owners, *[weights] * count, *[other_weights] * count, turned, *arrays, *after)


def combine(body, arrays, shapes, after=()):
    count = len(arrays)
    specs, operands = [], []
    for entry in arrays:
        if isinstance(entry, tuple):
            array, number = entry
            shape = (1,) + array.shape[1:]
            specs.append(pl.BlockSpec(shape, lambda k, number=number: (number, 0, 0, 0)))
        else:
            array = entry
            specs.append(SMEM if array.dtype == jnp.int32 else VMEM)
        operands.append(array)

    def run(*refs):
        body(refs[:count], refs[count + len(after) :])

    return pl.pallas_call(
        run,
        grid=(1,),
        in_specs=specs + [ANY] * len(after),
        out_specs=[VMEM] * len(shapes),
        out_shape=[jax.ShapeDtypeStruct(shape, BF) for shape in shapes],
        compiler_params=params(),
        cost_estimate=cost(1_000_000, 2_000_000),
    )(*operands, *after)


def wide(ref):
    return ref[...].astype(F32)


def chip_shard(pos, key_matrix, value_matrix, query_weight):
    def choose(ins, outs):
        position, key, value, query = ins
        keys, values = by_core(position[2], wide(key), wide(value))
        first, second = by_core(
            position[2], wide(query)[:, :HEAD_WIDTH], wide(query)[:, HEAD_WIDTH:]
        )
        outs[0][...] = jnp.concatenate([keys, first], axis=1).astype(BF)
        outs[1][...] = jnp.concatenate([values, second], axis=1).astype(BF)

    def stack(ins, outs):
        first, second = by_core(ins[0][2], wide(ins[1]), wide(ins[2]))
        outs[0][...] = jnp.concatenate([first, second], axis=0).astype(BF)

    rows = key_matrix.shape[0]
    kept, sent = combine(
        choose, (pos, key_matrix, value_matrix, query_weight), [(rows, WIDE)] * 2
    )
    (shard,) = combine(stack, (pos, kept, swap_core(sent)), [(2 * rows, WIDE)])
    return shard


def gather(shard, tokens, late):
    barrier = lax.optimization_barrier
    up1, down1, near = up_z(shard), down_z(shard), swap_y(shard)
    up1, down1, near, tokens = barrier((up1, down1, near, tokens))
    other_tokens = swap_core(tokens)
    up2, down2, near_up1, near_down1 = up_z(up1), down_z(down1), swap_y(up1), swap_y(down1)
    up2, down2, near_up1, near_down1 = barrier((up2, down2, near_up1, near_down1))
    up3, down3, near_up2, near_down2 = up_z(up2), down_z(down2), swap_y(up2), swap_y(down2)
    up3, down3, near_up2, near_down2, other_tokens, late = barrier(
        (up3, down3, near_up2, near_down2, other_tokens, late)
    )
    up4, down4 = up_z(up3[:, :HEAD_WIDTH]), down_z(down3[:, HEAD_WIDTH:])
    near_up3, near_down3 = up_z(near_up2), down_z(near_down2)
    arrivals = (
        (shard, near, 0, 0),
        (up1, near_up1, 7, 0),
        (down1, near_down1, 1, 0),
        (up2, near_up2, 6, 0),
        (down2, near_down2, 2, 0),
        (up3, near_up3, 5, 0),
        (down3, near_down3, 3, 0),
        (up4, swap_y(up4), 4, 0),
        (down4, swap_y(down4), 4, HEAD_WIDTH),
    )
    entries = []
    for same, other, z_offset, column in arrivals:
        entries += [(same, z_offset, 0, column), (other, z_offset, 1, column)]
    return entries, other_tokens, late


def shards(tokens, query_weight, key_matrix, value_matrix, query_gain, key_norm_gain, cotangent):
    ctx = lax.axis_index("ctx")
    tp = lax.axis_index("tp")
    z, y, core = ctx // 4, (ctx // 2) % 2, ctx % 2
    pos = jnp.stack([z, y, core, ctx]).astype(jnp.int32)
    token_positions = (ctx * ROWS + jnp.arange(ROWS, dtype=jnp.int32)).astype(F32)
    inverse = jnp.power(
        F32(rope_base), -jnp.arange(0, HEAD_WIDTH, 2).astype(F32) / HEAD_WIDTH
    )
    angles = token_positions[:, None] * inverse[None, :]
    cosine, sine = jnp.cos(angles), jnp.sin(angles)
    cosine = jnp.concatenate([cosine, cosine], axis=1)
    sine = jnp.concatenate([-sine, sine], axis=1)
    query_gain = query_gain.reshape(1, HEAD_WIDTH)
    key_gain = key_norm_gain.reshape(1, HEAD_WIDTH)

    shard = chip_shard(pos, key_matrix, value_matrix, query_weight)
    entries, other_tokens, (cosine, sine) = gather(shard, tokens, (cosine, sine))
    own_raw, sent_raw, weights = project(pos, tokens, other_tokens, entries)
    came_raw, weights_later = lax.optimization_barrier((swap_core(sent_raw), weights))
    pair_raw, query_raw, near0, queries = rotate_all(
        pos, own_raw, came_raw, key_gain, query_gain, cosine, sine
    )
    other_weights = swap_core(weights_later)
    near1, near2 = passed_along(near0, 1), passed_along(near0, 2)
    attended, grads0, grads1, grads2, score_grads = attend(
        pos, queries, near0, near1, near2, cotangent
    )
    from2, from1 = passed_along(grads2, -2), passed_along(grads1, -1)
    query_part = query_back(
        score_grads, near0, near1, near2, query_raw, query_gain, cosine, sine
    )
    kept, sent, turned = all_back(
        pos, grads0, from1, from2, pair_raw, key_gain, cosine, sine, query_part
    )
    other_back = swap_core(sent)

    def owners(*offsets):
        return jnp.stack(
            [(tp // 2 + i) % X_SIZE * 2 + (tp % 2 + j) % 2 for i, j in offsets]
        ).astype(jnp.int32)

    half = ROWS // 2
    token_shape = (PART, ROWS)
    terms = functools.partial(token_terms, weights=weights, other_weights=other_weights, turned=turned)

    def farthest(term, ins, outs):
        for number in range(2):
            part = term(number).astype(BF)
            outs[0][number] = part[:, :half]
            outs[1][number] = part[:, half:]

    def joined(term, ins, outs):
        part = term(0)
        outs[0][:, :half] = (part[:, :half] + ins[0][0].astype(F32)).astype(BF)
        outs[0][:, half:] = part[:, half:].astype(BF)
        part = term(1)
        outs[1][:, :half] = part[:, :half].astype(BF)
        outs[1][:, half:] = (part[:, half:] + ins[1][0].astype(F32)).astype(BF)

    def to_far(term, ins, outs):
        outs[0][...] = (term(0) + wide(ins[0]) + wide(ins[1])).astype(BF)

    def token_result(term, ins, outs):
        outs[0][...] = (term(0) + wide(ins[0]) + wide(ins[1]) + wide(ins[2])).astype(BF)

    def second_step(ins, outs):
        upper, lower, up, down = ins
        outs[0][0] = (upper[0, 0].astype(F32) + wide(up)).astype(BF)
        outs[0][1] = upper[0, 1]
        outs[1][0] = lower[0, 0]
        outs[1][1] = (lower[0, 1].astype(F32) + wide(down)).astype(BF)

    def later_step(ins, outs):
        upper, lower, up, down = ins
        outs[0][...] = (upper[0].astype(F32) + wide(up)).astype(BF)
        outs[1][...] = (lower[0].astype(F32) + wide(down)).astype(BF)

    def last_step(ins, outs):
        own, up, down = ins
        total = own[0].astype(F32) + wide(up) + wide(down)
        outs[0][...] = total[0].astype(BF)
        outs[1][...] = total[1].astype(BF)

    def near_sum(ins, outs):
        total = wide(ins[1]) + wide(ins[2])
        first, second = by_core(ins[0][2], total[: BLOCK // 2], total[BLOCK // 2 :])
        outs[0][...] = first.astype(BF)
        outs[1][...] = second.astype(BF)

    def to_outputs(ins, outs):
        first, second = by_core(ins[0][2], wide(ins[1]), wide(ins[2]))
        outs[0][:, :HEAD_WIDTH] = first[:, HEAD_WIDTH:].astype(BF)
        outs[0][:, HEAD_WIDTH:] = second[:, HEAD_WIDTH:].astype(BF)
        outs[1][...] = first[:, :HEAD_WIDTH].astype(BF)
        outs[2][...] = second[:, :HEAD_WIDTH].astype(BF)

    block, both = (BLOCK, WIDE), (2, BLOCK, WIDE)
    far_a, far_b = terms(
        owners((2, 0), (2, 1)), body=farthest, extras=(), shapes=[(2, PART, half)] * 2
    )
    token_up, token_down = up_x(far_a), down_x(far_b)
    mine, far_up, far_down = weight_terms(pos, tokens, other_tokens, kept, other_back)
    up, down = up_z(far_up), down_z(far_down)
    z2 = combine(second_step, ((mine, 3), (mine, 5), up, down), [both] * 2)
    up, down = up_z(z2[0]), down_z(z2[1])
    x1 = terms(
        owners((1, 1), (3, 1)),
        body=joined,
        extras=((token_up, 1), (token_down, 1)),
        shapes=[token_shape] * 2,
        after=(z2[0],),
    )
    got_up1, got_down1 = up_x(x1[0]), down_x(x1[1])
    x2 = terms(
        owners((1, 0), (3, 0)),
        body=joined,
        extras=((token_up, 0), (token_down, 0)),
        shapes=[token_shape] * 2,
        after=(x1[0],),
    )
    got_up0, got_down0 = up_x(x2[0]), down_x(x2[1])
    z3 = combine(later_step, ((mine, 2), (mine, 6), up, down), [both] * 2, (x2[0],))
    up, down = up_z(z3[0]), down_z(z3[1])
    (x3,) = terms(
        owners((0, 1)),
        body=to_far,
        extras=(got_up1, got_down1),
        shapes=[token_shape],
        after=(z3[0],),
    )
    far = swap_far(x3)
    z4 = combine(later_step, ((mine, 1), (mine, 7), up, down), [both] * 2, (x3,))
    up, down = up_z(z4[0]), down_z(z4[1])
    chip_kept, chip_sent = combine(last_step, ((mine, 0), up, down), [block] * 2)
    chip_came = swap_y(chip_sent)
    (token_sum,) = terms(
        owners((0, 0)),
        body=token_result,
        extras=(got_up0, got_down0, far),
        shapes=[token_shape],
        after=(chip_sent,),
    )
    rows = (BLOCK // 2, WIDE)
    row_kept, row_sent = combine(near_sum, (pos, chip_kept, chip_came), [rows] * 2, (token_sum,))
    narrow = (BLOCK // 2, HEAD_WIDTH)
    query_gradient, key_gradient, value_gradient = combine(
        to_outputs, (pos, row_kept, swap_core(row_sent)), [rows, narrow, narrow]
    )
    return (attended, token_sum.T, query_gradient, key_gradient, value_gradient)


def solution(mesh):
    in_specs = (
        P("ctx", None),
        P("ctx", "tp"),
        P("ctx", "tp"),
        P("ctx", "tp"),
        P(),
        P(),
        P("ctx", "tp"),
    )
    out_specs = (P("ctx", "tp"), P("ctx", "tp"), P("ctx", "tp"), P("ctx", "tp"), P("ctx", "tp"))
    return jax.shard_map(shards, mesh=mesh, in_specs=in_specs, out_specs=out_specs, check_vma=False)
```

```python
import functools

import jax
import jax.numpy as jnp
from jax import lax
from jax.experimental import pallas as pl
from jax.experimental.pallas import tpu as pltpu
from jax.sharding import PartitionSpec as P

HEAD_WIDTH = 128
WINDOW_LENGTH = 1024
QUERY_SCALAR = 168
SCORE_SCALE = QUERY_SCALAR ** (-0.5)

rope_base = 10000.0
norm_eps = 1e-06

Z_SIZE = 8
X_SIZE = 4
ROWS = 512
TILE = 256
SPAN = WINDOW_LENGTH + TILE
BAND = WINDOW_LENGTH + ROWS
DEPTH = 5376
VMEM_MEBIBYTES = 50
BLOCK = 336
PART = 672
BF = jnp.bfloat16
F32 = jnp.float32


def along_z(step):
    return [(i, ((i // 4 + step) % Z_SIZE) * 4 + i % 4) for i in range(4 * Z_SIZE)]


def along_x(step):
    return [(i, ((i // 2 + step) % X_SIZE) * 2 + i % 2) for i in range(2 * X_SIZE)]


SIBLING = [(i, i ^ 1) for i in range(32)]
NEAR_Y = [(i, i ^ 2) for i in range(32)]
FAR_Y = [(i, i ^ 1) for i in range(8)]


def up_z(piece):
    return lax.ppermute(piece, "ctx", along_z(1))


def down_z(piece):
    return lax.ppermute(piece, "ctx", along_z(-1))


def swap_y(piece):
    return lax.ppermute(piece, "ctx", NEAR_Y)


def swap_core(piece):
    return lax.ppermute(piece, "ctx", SIBLING)


def up_x(piece):
    return lax.ppermute(piece, "tp", along_x(1))


def down_x(piece):
    return lax.ppermute(piece, "tp", along_x(-1))


def swap_far(piece):
    return lax.ppermute(piece, "tp", FAR_Y)


def passed_along(shard, by):
    pairs = [(i, i + by) for i in range(32) if 0 <= i + by < 32]
    return lax.ppermute(shard, "ctx", pairs)


def summed(*terms):
    total = terms[0].astype(F32)
    for term in terms[1:]:
        total = total + term.astype(F32)
    return total.astype(BF)


def dot(left, right, left_axis=1, right_axis=0):
    return lax.dot_general(
        left, right, (((left_axis,), (right_axis,)), ((), ())), preferred_element_type=F32
    )


def params(mebibytes=VMEM_MEBIBYTES):
    return pltpu.CompilerParams(vmem_limit_bytes=mebibytes * 1024 * 1024)


def cost(flops, moved):
    return pl.CostEstimate(flops=flops, bytes_accessed=moved, transcendentals=0)


VMEM = pl.BlockSpec(memory_space=pltpu.VMEM)
ANY = pl.BlockSpec(memory_space=pl.ANY)
SMEM = pl.BlockSpec(memory_space=pltpu.SMEM)


def rotate(raw, gain, cosine, sine):
    scale = lax.rsqrt(jnp.mean(raw * raw, axis=-1, keepdims=True) + norm_eps)
    normed = raw * scale * gain
    return normed * cosine + pltpu.roll(normed, HEAD_WIDTH // 2, 1) * sine


def rotate_back(raw, grads, gain, cosine, sine):
    scale = lax.rsqrt(jnp.mean(raw * raw, axis=-1, keepdims=True) + norm_eps)
    turned = (grads * cosine - pltpu.roll(grads, HEAD_WIDTH // 2, 1) * sine) * gain
    inner = jnp.mean(raw * turned, axis=-1, keepdims=True)
    return turned * scale - raw * (scale * scale * scale * inner)


DEPTH_STEPS = 3
DEPTH_STEP = DEPTH // DEPTH_STEPS
WIDE = 2 * HEAD_WIDTH


def by_core(core, first, second):
    return jnp.where(core == 0, first, second), jnp.where(core == 0, second, first)


def project_body(places, pos, tokens, other_tokens, *refs):
    count = len(places)
    pieces = refs[:count]
    own, sent, kept, weights, sems, out_sem = refs[count:]
    step = pl.program_id(0)
    z, y = pos[0], pos[1]

    @pl.when(step == 0)
    def place():
        copies = []
        for number, (z_offset, y_offset, column, width) in enumerate(places):
            block = lax.rem(z + z_offset, 8) * 2 + lax.rem(y + y_offset, 2)
            start = pl.multiple_of(block * BLOCK, 16)
            copies.append(
                pltpu.make_async_copy(
                    pieces[number],
                    weights.at[pl.ds(start, BLOCK), pl.ds(column, width)],
                    sems.at[number],
                )
            )
        for copy in copies:
            copy.start()
        for copy in copies:
            copy.wait()
        pltpu.make_async_copy(weights, kept, out_sem).start()
        own[...] = jnp.zeros_like(own)
        sent[...] = jnp.zeros_like(sent)

    start = pl.multiple_of(step * DEPTH_STEP, DEPTH_STEP)
    block = weights[pl.ds(start, DEPTH_STEP), :]
    own[...] += dot(tokens[...], block)
    sent[...] += dot(other_tokens[...], block)

    @pl.when(step == DEPTH_STEPS - 1)
    def finish():
        pltpu.make_async_copy(weights, kept, out_sem).wait()


def project(pos, tokens, other_tokens, entries):
    places = tuple((e[1], e[2], e[3], e[0].shape[1]) for e in entries)
    whole = lambda shape: pl.BlockSpec(shape, lambda k: (0,) * len(shape))
    return pl.pallas_call(
        functools.partial(project_body, places),
        grid=(DEPTH_STEPS,),
        in_specs=[SMEM] + [pl.BlockSpec((ROWS, DEPTH_STEP), lambda k: (0, k))] * 2 + [ANY] * len(entries),
        out_specs=[whole((ROWS, WIDE)), whole((ROWS, WIDE)), ANY],
        out_shape=[
            jax.ShapeDtypeStruct((ROWS, WIDE), F32),
            jax.ShapeDtypeStruct((ROWS, WIDE), F32),
            jax.ShapeDtypeStruct((DEPTH, WIDE), BF),
        ],
        scratch_shapes=[
            pltpu.VMEM((DEPTH, WIDE), BF),
            pltpu.SemaphoreType.DMA((len(entries),)),
            pltpu.SemaphoreType.DMA,
        ],
        compiler_params=params(),
        cost_estimate=cost(2 * ROWS * DEPTH * 512, 17_000_000),
    )(pos, tokens, other_tokens, *[e[0] for e in entries])


def rotate_all_body(
    pos, own, came, key_gain, query_gain, cosine, sine, pair_raw, query_raw, pair_rows, query_rows
):
    core = pos[2]
    key, value = by_core(core, own[:, :HEAD_WIDTH], came[:, :HEAD_WIDTH])
    first, second = by_core(core, own[:, HEAD_WIDTH:], came[:, HEAD_WIDTH:])
    pair_raw[...] = key
    query_raw[0] = first
    query_raw[1] = second
    pair_rows[0] = rotate(key, key_gain[...], cosine[...], sine[...]).astype(BF)
    pair_rows[1] = value.astype(BF)
    query_rows[0] = rotate(first, query_gain[...], cosine[...], sine[...]).astype(BF)
    query_rows[1] = rotate(second, query_gain[...], cosine[...], sine[...]).astype(BF)


def rotate_all(pos, own, came, key_gain, query_gain, cosine, sine):
    pair = (2, ROWS, HEAD_WIDTH)
    return pl.pallas_call(
        rotate_all_body,
        in_specs=[SMEM] + [VMEM] * 6,
        out_specs=[VMEM] * 4,
        out_shape=[
            jax.ShapeDtypeStruct((ROWS, HEAD_WIDTH), F32),
            jax.ShapeDtypeStruct(pair, F32),
            jax.ShapeDtypeStruct(pair, BF),
            jax.ShapeDtypeStruct(pair, BF),
        ],
        compiler_params=params(),
        cost_estimate=cost(10_000_000, 3_000_000),
    )(pos, own, came, key_gain, query_gain, cosine, sine)


def load_band(nears, number, band, sems):
    copies = []
    for part, near in enumerate(nears):
        copy = pltpu.make_async_copy(
            near.at[number], band.at[pl.ds(part * ROWS, ROWS), :], sems.at[number, part]
        )
        copy.start()
        copies.append(copy)
    return copies


def attend_body(
    pos, queries, near0, near1, near2, cotangent, attended, grads0, grads1, grads2, score_grads,
    keys, values, values_turned, terms, weights, key_sums, value_sums, sems,
):
    nears = (near2, near1, near0)
    copies = load_band(nears, 0, keys, sems) + load_band(nears, 1, values, sems)
    for copy in copies:
        copy.wait()
    for part in range(3):
        rows = slice(part * ROWS, (part + 1) * ROWS)
        values_turned[:, rows] = values[rows].astype(F32).T.astype(BF)
    key_sums[...] = jnp.zeros_like(key_sums)
    value_sums[...] = jnp.zeros_like(value_sums)
    valid2 = (pos[3] >= 2).astype(F32)
    valid1 = (pos[3] >= 1).astype(F32)
    valid = (valid2, valid2, valid1, valid1, None, None)
    key_place = lax.broadcasted_iota(jnp.int32, (TILE, TILE), 0)
    query_place = lax.broadcasted_iota(jnp.int32, (TILE, TILE), 1)
    for head in range(2):
        columns = slice(head * HEAD_WIDTH, (head + 1) * HEAD_WIDTH)
        for tile in range(2):
            here = slice(tile * TILE, (tile + 1) * TILE)
            span = slice(tile * TILE, tile * TILE + SPAN)
            query = queries[head, here]
            out = cotangent[here, columns]
            total = jnp.zeros((1, TILE), F32)
            for block in range(5):
                low = block * TILE
                scores = dot(keys[tile * TILE + low : tile * TILE + low + TILE], query, 1, 1)
                term = jnp.exp(scores * SCORE_SCALE)
                if block == 0:
                    term = jnp.where(key_place > query_place, term, 0.0)
                if block == 4:
                    term = jnp.where(key_place <= query_place, term, 0.0)
                if valid[tile + block] is not None:
                    term = term * valid[tile + block]
                terms[low : low + TILE] = term
                total = total + jnp.sum(term, axis=0, keepdims=True)
            inverse = 1.0 / total
            for block in range(5):
                low = block * TILE
                weights[low : low + TILE] = (terms[low : low + TILE] * inverse).astype(BF)
            mixed = dot(values_turned[:, span], weights[...])
            rounded = mixed.astype(BF).astype(F32)
            attended[here, columns] = mixed.T.astype(BF)
            delta = jnp.sum(out.astype(F32).T * rounded, axis=0, keepdims=True)
            for block in range(5):
                low = block * TILE
                prob_grads = dot(values[tile * TILE + low : tile * TILE + low + TILE], out, 1, 1)
                probs = terms[low : low + TILE] * inverse
                score_grads[head, tile, low : low + TILE] = (probs * (prob_grads - delta)).astype(BF)
            key_sums[span] += dot(score_grads[head, tile], query)
            value_sums[span] += dot(weights[...], out)
    for part, ref in enumerate((grads2, grads1, grads0)):
        rows = slice(part * ROWS, (part + 1) * ROWS)
        ref[0] = (key_sums[rows] * SCORE_SCALE).astype(ref.dtype)
        ref[1] = value_sums[rows].astype(ref.dtype)


def attend(pos, queries, near0, near1, near2, cotangent):
    pair = (2, ROWS, HEAD_WIDTH)
    return pl.pallas_call(
        attend_body,
        in_specs=[SMEM, VMEM] + [ANY] * 3 + [VMEM],
        out_specs=[VMEM] * 5,
        out_shape=[
            jax.ShapeDtypeStruct((ROWS, 2 * HEAD_WIDTH), BF),
            jax.ShapeDtypeStruct(pair, F32),
            jax.ShapeDtypeStruct(pair, BF),
            jax.ShapeDtypeStruct(pair, BF),
            jax.ShapeDtypeStruct((2, 2, SPAN, TILE), BF),
        ],
        scratch_shapes=[
            pltpu.VMEM((BAND, HEAD_WIDTH), BF),
            pltpu.VMEM((BAND, HEAD_WIDTH), BF),
            pltpu.VMEM((HEAD_WIDTH, BAND), BF),
            pltpu.VMEM((SPAN, TILE), F32),
            pltpu.VMEM((SPAN, TILE), BF),
            pltpu.VMEM((BAND, HEAD_WIDTH), F32),
            pltpu.VMEM((BAND, HEAD_WIDTH), F32),
            pltpu.SemaphoreType.DMA((2, 3)),
        ],
        compiler_params=params(),
        cost_estimate=cost(8_000_000_000, 8_000_000),
    )(pos, queries, near0, near1, near2, cotangent)


def query_back_body(
    score_grads, near0, near1, near2, raw, gain, cosine, sine, back, keys, keys_turned, sems
):
    for copy in load_band((near2, near1, near0), 0, keys, sems):
        copy.wait()
    for part in range(3):
        rows = slice(part * ROWS, (part + 1) * ROWS)
        keys_turned[:, rows] = keys[rows].astype(F32).T.astype(BF)
    for head in range(2):
        for tile in range(2):
            here = slice(tile * TILE, (tile + 1) * TILE)
            grads = dot(keys_turned[:, tile * TILE : tile * TILE + SPAN], score_grads[head, tile])
            grads = (grads * SCORE_SCALE).T
            back[head, here] = rotate_back(
                raw[head, here], grads, gain[...], cosine[here], sine[here]
            )


def query_back(score_grads, near0, near1, near2, raw, gain, cosine, sine):
    return pl.pallas_call(
        query_back_body,
        in_specs=[VMEM] + [ANY] * 3 + [VMEM] * 4,
        out_specs=VMEM,
        out_shape=jax.ShapeDtypeStruct((2, ROWS, HEAD_WIDTH), F32),
        scratch_shapes=[
            pltpu.VMEM((BAND, HEAD_WIDTH), BF),
            pltpu.VMEM((HEAD_WIDTH, BAND), BF),
            pltpu.SemaphoreType.DMA((1, 3)),
        ],
        compiler_params=params(),
        cost_estimate=cost(1_000_000_000, 4_000_000),
    )(score_grads, near0, near1, near2, raw, gain, cosine, sine)


def all_back_body(
    pos, own, from1, from2, raw, gain, cosine, sine, query_part, kept, sent, turned
):
    core = pos[2]
    grads = own[...] + from1[...].astype(F32) + from2[...].astype(F32)
    key_part = rotate_back(raw[...], grads[0], gain[...], cosine[...], sine[...])
    mine, other = by_core(core, key_part, grads[1])
    kept[:, :HEAD_WIDTH] = mine.astype(BF)
    sent[:, :HEAD_WIDTH] = other.astype(BF)
    turned[:HEAD_WIDTH] = mine.T.astype(BF)
    turned[WIDE : WIDE + HEAD_WIDTH] = other.T.astype(BF)
    mine, other = by_core(core, query_part[0], query_part[1])
    kept[:, HEAD_WIDTH:] = mine.astype(BF)
    sent[:, HEAD_WIDTH:] = other.astype(BF)
    turned[HEAD_WIDTH:WIDE] = mine.T.astype(BF)
    turned[WIDE + HEAD_WIDTH :] = other.T.astype(BF)


def all_back(pos, own, from1, from2, raw, gain, cosine, sine, query_part):
    return pl.pallas_call(
        all_back_body,
        in_specs=[SMEM] + [VMEM] * 8,
        out_specs=[VMEM] * 3,
        out_shape=[
            jax.ShapeDtypeStruct((ROWS, WIDE), BF),
            jax.ShapeDtypeStruct((ROWS, WIDE), BF),
            jax.ShapeDtypeStruct((2 * WIDE, ROWS), BF),
        ],
        compiler_params=params(),
        cost_estimate=cost(10_000_000, 3_000_000),
    )(pos, own, from1, from2, raw, gain, cosine, sine, query_part)


def weight_terms_body(pos, tokens, other_tokens, back, other_back, mine, far_up, far_down, terms):
    step = pl.program_id(0)
    z, y = pos[0], pos[1]
    rows = pl.ds(pl.multiple_of(step * (DEPTH // 2), DEPTH // 2), DEPTH // 2)
    terms[rows, :] = (
        dot(tokens[...], back[...], 0, 0) + dot(other_tokens[...], other_back[...], 0, 0)
    ).astype(BF)

    @pl.when(step == 1)
    def spread():
        for z_offset in range(8):
            start = lax.rem(z + z_offset, 8) * PART
            same = pl.ds(pl.multiple_of(start + y * BLOCK, 16), BLOCK)
            other = pl.ds(pl.multiple_of(start + (1 - y) * BLOCK, 16), BLOCK)
            if z_offset == 4:
                far_up[...] = terms[same, :]
                far_down[...] = terms[other, :]
            else:
                mine[z_offset, 0] = terms[same, :]
                mine[z_offset, 1] = terms[other, :]


def weight_terms(pos, tokens, other_tokens, back, other_back):
    whole = lambda shape: pl.BlockSpec(shape, lambda k: (0,) * len(shape))
    shapes = [(8, 2, BLOCK, WIDE), (BLOCK, WIDE), (BLOCK, WIDE)]
    return pl.pallas_call(
        weight_terms_body,
        grid=(2,),
        in_specs=[
            SMEM,
            pl.BlockSpec((ROWS, DEPTH // 2), lambda k: (0, k)),
            pl.BlockSpec((ROWS, DEPTH // 2), lambda k: (0, k)),
            whole((ROWS, WIDE)),
            whole((ROWS, WIDE)),
        ],
        out_specs=[whole(shape) for shape in shapes],
        out_shape=[jax.ShapeDtypeStruct(shape, BF) for shape in shapes],
        scratch_shapes=[pltpu.VMEM((DEPTH, WIDE), BF)],
        compiler_params=params(),
        cost_estimate=cost(4 * ROWS * DEPTH * 256, 17_000_000),
    )(pos, tokens, other_tokens, back, other_back)


def token_terms(owners, weights, other_weights, turned, body, extras, shapes, after=()):
    count = owners.shape[0]
    whole = lambda shape: pl.BlockSpec(shape, lambda k, order: (0,) * len(shape))

    def extra_spec(extra):
        if isinstance(extra, tuple):
            array, number = extra
            return pl.BlockSpec((1,) + array.shape[1:], lambda k, order: (number, 0, 0))
        return whole(extra.shape)

    arrays = [extra[0] if isinstance(extra, tuple) else extra for extra in extras]

    def window(number):
        return pl.BlockSpec((PART, WIDE), lambda k, order: (order[number], 0))

    def run(order, *refs):
        turned_ref = refs[2 * count]
        rest = refs[2 * count + 1 :]

        def term(number):
            return dot(refs[number][...], turned_ref[:WIDE]) + dot(
                refs[count + number][...], turned_ref[WIDE:]
            )

        body(term, rest[: len(extras)], rest[len(extras) + len(after) :])

    windows = [window(number) for number in range(count)]
    return pl.pallas_call(
        run,
        grid_spec=pltpu.PrefetchScalarGridSpec(
            num_scalar_prefetch=1,
            grid=(1,),
            in_specs=windows
            + windows
            + [whole((2 * WIDE, ROWS))]
            + [extra_spec(extra) for extra in extras]
            + [ANY] * len(after),
            out_specs=[whole(shape) for shape in shapes],
        ),
        out_shape=[jax.ShapeDtypeStruct(shape, BF) for shape in shapes],
        compiler_params=params(),
        cost_estimate=cost(2 * PART * ROWS * 512 * count, 1_500_000 * count),
    )(owners, *[weights] * count, *[other_weights] * count, turned, *arrays, *after)


def combine(body, arrays, shapes, after=()):
    count = len(arrays)
    specs, operands = [], []
    for entry in arrays:
        if isinstance(entry, tuple):
            array, number = entry
            shape = (1,) + array.shape[1:]
            specs.append(pl.BlockSpec(shape, lambda k, number=number: (number, 0, 0, 0)))
        else:
            array = entry
            specs.append(SMEM if array.dtype == jnp.int32 else VMEM)
        operands.append(array)

    def run(*refs):
        body(refs[:count], refs[count + len(after) :])

    return pl.pallas_call(
        run,
        grid=(1,),
        in_specs=specs + [ANY] * len(after),
        out_specs=[VMEM] * len(shapes),
        out_shape=[jax.ShapeDtypeStruct(shape, BF) for shape in shapes],
        compiler_params=params(),
        cost_estimate=cost(1_000_000, 2_000_000),
    )(*operands, *after)


def wide(ref):
    return ref[...].astype(F32)


def chip_shard(halves, core):
    kept = jnp.where(core == 0, halves[0], halves[1])
    came = swap_core(jnp.where(core == 0, halves[1], halves[0]))
    return jnp.concatenate(
        [jnp.where(core == 0, kept, came), jnp.where(core == 0, came, kept)], axis=0
    )


def gather(shard, tokens, late):
    barrier = lax.optimization_barrier
    up1, down1, near = up_z(shard), down_z(shard), swap_y(shard)
    up1, down1, near, tokens = barrier((up1, down1, near, tokens))
    other_tokens = swap_core(tokens)
    up2, down2, near_up1, near_down1 = up_z(up1), down_z(down1), swap_y(up1), swap_y(down1)
    up2, down2, near_up1, near_down1 = barrier((up2, down2, near_up1, near_down1))
    up3, down3, near_up2, near_down2 = up_z(up2), down_z(down2), swap_y(up2), swap_y(down2)
    up3, down3, near_up2, near_down2, other_tokens, late = barrier(
        (up3, down3, near_up2, near_down2, other_tokens, late)
    )
    up4, down4 = up_z(up3[:, :HEAD_WIDTH]), down_z(down3[:, HEAD_WIDTH:])
    near_up3, near_down3 = up_z(near_up2), down_z(near_down2)
    arrivals = (
        (shard, near, 0, 0),
        (up1, near_up1, 7, 0),
        (down1, near_down1, 1, 0),
        (up2, near_up2, 6, 0),
        (down2, near_down2, 2, 0),
        (up3, near_up3, 5, 0),
        (down3, near_down3, 3, 0),
        (up4, swap_y(up4), 4, 0),
        (down4, swap_y(down4), 4, HEAD_WIDTH),
    )
    entries = []
    for same, other, z_offset, column in arrivals:
        entries += [(same, z_offset, 0, column), (other, z_offset, 1, column)]
    return entries, other_tokens, late


def shards(tokens, query_weight, key_matrix, value_matrix, query_gain, key_norm_gain, cotangent):
    ctx = lax.axis_index("ctx")
    tp = lax.axis_index("tp")
    z, y, core = ctx // 4, (ctx // 2) % 2, ctx % 2
    pos = jnp.stack([z, y, core, ctx]).astype(jnp.int32)
    token_positions = (ctx * ROWS + jnp.arange(ROWS, dtype=jnp.int32)).astype(F32)
    inverse = jnp.power(
        F32(rope_base), -jnp.arange(0, HEAD_WIDTH, 2).astype(F32) / HEAD_WIDTH
    )
    angles = token_positions[:, None] * inverse[None, :]
    cosine, sine = jnp.cos(angles), jnp.sin(angles)
    cosine = jnp.concatenate([cosine, cosine], axis=1)
    sine = jnp.concatenate([-sine, sine], axis=1)
    query_gain = query_gain.reshape(1, HEAD_WIDTH)
    key_gain = key_norm_gain.reshape(1, HEAD_WIDTH)

    shard = chip_shard(
        [
            jnp.concatenate([key_matrix, query_weight[:, :HEAD_WIDTH]], axis=1),
            jnp.concatenate([value_matrix, query_weight[:, HEAD_WIDTH:]], axis=1),
        ],
        core,
    )
    entries, other_tokens, (cosine, sine) = gather(shard, tokens, (cosine, sine))
    own_raw, sent_raw, weights = project(pos, tokens, other_tokens, entries)
    came_raw, weights_later = lax.optimization_barrier((swap_core(sent_raw), weights))
    pair_raw, query_raw, near0, queries = rotate_all(
        pos, own_raw, came_raw, key_gain, query_gain, cosine, sine
    )
    other_weights = swap_core(weights_later)
    near1, near2 = passed_along(near0, 1), passed_along(near0, 2)
    attended, grads0, grads1, grads2, score_grads = attend(
        pos, queries, near0, near1, near2, cotangent
    )
    from2, from1 = passed_along(grads2, -2), passed_along(grads1, -1)
    query_part = query_back(
        score_grads, near0, near1, near2, query_raw, query_gain, cosine, sine
    )
    kept, sent, turned = all_back(
        pos, grads0, from1, from2, pair_raw, key_gain, cosine, sine, query_part
    )
    other_back = swap_core(sent)

    def owners(*offsets):
        return jnp.stack(
            [(tp // 2 + i) % X_SIZE * 2 + (tp % 2 + j) % 2 for i, j in offsets]
        ).astype(jnp.int32)

    half = ROWS // 2
    token_shape = (PART, ROWS)
    terms = functools.partial(token_terms, weights=weights, other_weights=other_weights, turned=turned)

    def farthest(term, ins, outs):
        for number in range(2):
            part = term(number).astype(BF)
            outs[0][number] = part[:, :half]
            outs[1][number] = part[:, half:]

    def joined(term, ins, outs):
        part = term(0)
        outs[0][:, :half] = (part[:, :half] + ins[0][0].astype(F32)).astype(BF)
        outs[0][:, half:] = part[:, half:].astype(BF)
        part = term(1)
        outs[1][:, :half] = part[:, :half].astype(BF)
        outs[1][:, half:] = (part[:, half:] + ins[1][0].astype(F32)).astype(BF)

    def to_far(term, ins, outs):
        outs[0][...] = (term(0) + wide(ins[0]) + wide(ins[1])).astype(BF)

    def token_result(term, ins, outs):
        outs[0][...] = (term(0) + wide(ins[0]) + wide(ins[1]) + wide(ins[2])).astype(BF)

    def second_step(ins, outs):
        upper, lower, up, down = ins
        outs[0][0] = (upper[0, 0].astype(F32) + wide(up)).astype(BF)
        outs[0][1] = upper[0, 1]
        outs[1][0] = lower[0, 0]
        outs[1][1] = (lower[0, 1].astype(F32) + wide(down)).astype(BF)

    def later_step(ins, outs):
        upper, lower, up, down = ins
        outs[0][...] = (upper[0].astype(F32) + wide(up)).astype(BF)
        outs[1][...] = (lower[0].astype(F32) + wide(down)).astype(BF)

    def last_step(ins, outs):
        own, up, down = ins
        total = own[0].astype(F32) + wide(up) + wide(down)
        outs[0][...] = total[0].astype(BF)
        outs[1][...] = total[1].astype(BF)

    def near_sum(ins, outs):
        total = wide(ins[1]) + wide(ins[2])
        first, second = by_core(ins[0][2], total[: BLOCK // 2], total[BLOCK // 2 :])
        outs[0][...] = first.astype(BF)
        outs[1][...] = second.astype(BF)

    def to_outputs(ins, outs):
        first, second = by_core(ins[0][2], wide(ins[1]), wide(ins[2]))
        outs[0][:, :HEAD_WIDTH] = first[:, HEAD_WIDTH:].astype(BF)
        outs[0][:, HEAD_WIDTH:] = second[:, HEAD_WIDTH:].astype(BF)
        outs[1][...] = first[:, :HEAD_WIDTH].astype(BF)
        outs[2][...] = second[:, :HEAD_WIDTH].astype(BF)

    block, both = (BLOCK, WIDE), (2, BLOCK, WIDE)
    far_a, far_b = terms(
        owners((2, 0), (2, 1)), body=farthest, extras=(), shapes=[(2, PART, half)] * 2
    )
    token_up, token_down = up_x(far_a), down_x(far_b)
    mine, far_up, far_down = weight_terms(pos, tokens, other_tokens, kept, other_back)
    up, down = up_z(far_up), down_z(far_down)
    z2 = combine(second_step, ((mine, 3), (mine, 5), up, down), [both] * 2)
    up, down = up_z(z2[0]), down_z(z2[1])
    x1 = terms(
        owners((1, 1), (3, 1)),
        body=joined,
        extras=((token_up, 1), (token_down, 1)),
        shapes=[token_shape] * 2,
        after=(z2[0],),
    )
    got_up1, got_down1 = up_x(x1[0]), down_x(x1[1])
    x2 = terms(
        owners((1, 0), (3, 0)),
        body=joined,
        extras=((token_up, 0), (token_down, 0)),
        shapes=[token_shape] * 2,
        after=(x1[0],),
    )
    got_up0, got_down0 = up_x(x2[0]), down_x(x2[1])
    z3 = combine(later_step, ((mine, 2), (mine, 6), up, down), [both] * 2, (x2[0],))
    up, down = up_z(z3[0]), down_z(z3[1])
    (x3,) = terms(
        owners((0, 1)),
        body=to_far,
        extras=(got_up1, got_down1),
        shapes=[token_shape],
        after=(z3[0],),
    )
    far = swap_far(x3)
    z4 = combine(later_step, ((mine, 1), (mine, 7), up, down), [both] * 2, (x3,))
    up, down = up_z(z4[0]), down_z(z4[1])
    chip_kept, chip_sent = combine(last_step, ((mine, 0), up, down), [block] * 2)
    chip_came = swap_y(chip_sent)
    (token_sum,) = terms(
        owners((0, 0)),
        body=token_result,
        extras=(got_up0, got_down0, far),
        shapes=[token_shape],
        after=(chip_sent,),
    )
    rows = (BLOCK // 2, WIDE)
    row_kept, row_sent = combine(near_sum, (pos, chip_kept, chip_came), [rows] * 2, (token_sum,))
    narrow = (BLOCK // 2, HEAD_WIDTH)
    query_gradient, key_gradient, value_gradient = combine(
        to_outputs, (pos, row_kept, swap_core(row_sent)), [rows, narrow, narrow]
    )
    return (attended, token_sum.T, query_gradient, key_gradient, value_gradient)


def solution(mesh):
    in_specs = (
        P("ctx", None),
        P("ctx", "tp"),
        P("ctx", "tp"),
        P("ctx", "tp"),
        P(),
        P(),
        P("ctx", "tp"),
    )
    out_specs = (P("ctx", "tp"), P("ctx", "tp"), P("ctx", "tp"), P("ctx", "tp"), P("ctx", "tp"))
    return jax.shard_map(shards, mesh=mesh, in_specs=in_specs, out_specs=out_specs, check_vma=False)
```
